32 devices in a mesh: groups: 2 (over y), dp: 4 (over z), section: 2 (over x), tensor: 2 (over core).
Axes of the slice: x: 2, y: 2, z: 4, core: 2. Of those that a mesh axis runs over, the one named last changes fastest.
Arguments:
- cotangent: bfloat16 [2, 1024, 2048], P('section', ('groups', 'dp')), parts along dimension 1, may hold values from -6 to 6
- routes: int32 [2, 8, 2], P('section', ('groups', 'dp')), parts along dimension 1, may hold values from 0 to 3, all different within a row
- gate_values: float32 [2, 1024, 2], P('section', ('groups', 'dp')), parts along dimension 1, may hold values from 0.1 to 0.9
- up_weight: bfloat16 [2, 4, 2048, 7168], P('section', 'dp', None, 'tensor'), may hold values from -0.125 to 0.125
- down_weight: bfloat16 [2, 4, 7168, 2048], P('section', 'dp', 'tensor'), may hold values from -0.0625 to 0.0625
- pre_activation: bfloat16 [2, 8, 4, 128, 7168], P('section', ('groups', 'dp'), None, None, 'tensor'), parts along dimension 1, may hold values from -6 to 6
- input_sketch: float32 [2, 1024, 64], P('section', ('groups', 'dp')), parts along dimension 1, may hold values from -6 to 6
- model_sketch: bfloat16 [2, 2048, 64], P('section'), may hold values from -0.125 to 0.125
- hidden_sketch: bfloat16 [2, 4, 7168, 64], P('section', 'dp', 'tensor'), may hold values from -0.0625 to 0.0625
- lengths: int32 [2, 8, 4], P('section', ('groups', 'dp')), parts along dimension 1, may hold values from 1 to 64, 128 in all within a row
Outputs:
- handed: bfloat16 [2, 1024, 2048], P('section', ('groups', 'dp')), parts along dimension 1
- features: float32 [2, 32, 64, 128], P('section', ('groups', 'dp')), parts along dimension 1
The draws below stay inside these ranges and needn't reach their ends.
There are 2 independent parts, one for each index of `groups`. The reference program is written for one: setup_inputs(seed, part) draws one part's arguments, and reference() takes and returns one part's arrays. A program takes and returns all parts, laid end to end along the dimension named above; an argument that names none is the same for every part. Nothing has to cross between parts.
Inputs may be any that keep to these rules, and one draw needn't show every extreme that they name: `routes`: the two experts of a block differ. `lengths`: each row of counts sums to 128, and its largest is 64.
All inputs are finite; a program needn't handle non-finite values.
Results may differ from the reference program's by a relative error of at most 0.0037.
Values may be sent and summed in bfloat16 or wider, within the bound.
No kernel may reach another device: no remote copies, remote signals or barrier semaphores. Data moves between devices by JAX's collectives and lax.ppermute only.
A program may use at most 128 MiB of HBM per device.

```python
import math
import jax
import jax.numpy as jnp
import numpy as np
from jax import lax

D = 2048
FF = 7168
EXPERTS = 4
RANK = 64
BLOCK = 128
TOK_DEV = 128
EX_DEV = 4
MOST_EX = 64
PIECES = 4
FF_PIECE = 7168
TOKENS = 512
BLOCKS = 4
EXAMPLES = 16
SECTIONS = 2


def level_of(own_key, dims, pieces, low, high):
    def one(axis_at, shards_of):
        draws = jax.random.uniform(jax.random.fold_in(jax.random.fold_in(own_key, 6), axis_at), (shards_of,), jnp.float32, low / len(pieces), high / len(pieces))
        return jnp.repeat(jnp.exp(draws), dims[axis_at] // shards_of).reshape((-1,) + (1,) * (len(dims) - axis_at - 1))

    level = one(*pieces[0])
    for cut in pieces[1:]:
        level = level * one(*cut)
    return level


def different_ones(own_key, rows, number_of, top, lift):
    order = jax.random.permutation(jax.random.fold_in(own_key, 1), number_of)
    pull = order
    for power in range(3):
        pull = pull * pull // number_of
    pull = pull * lift // number_of
    lots = jax.random.randint(jax.random.fold_in(own_key, 2), (rows, number_of), 0, 4096) + pull
    fixed_rows = jax.random.permutation(jax.random.fold_in(own_key, 3), rows)[jnp.arange(number_of) % rows]
    lots = jnp.where(jnp.arange(rows)[:, None] == fixed_rows[None, :], 1 << 14, lots)
    score = lots * number_of + jnp.arange(number_of)
    return lax.top_k(score.astype(jnp.int32), top)[1].astype(jnp.int32)


def profile(number_of, total, most, lean):
    loads = [(1 << 20) // math.isqrt(grade ** lean) + 1 for grade in range(2, number_of + 1)]
    spare, given = total - most - (number_of - 1), [1] * (number_of - 1)
    while spare > 0:
        candidates = [i for i in range(number_of - 1) if given[i] < most]
        whole, remaining = sum([loads[i] for i in candidates]), spare
        for i in candidates:
            more = min(most - given[i], max(1, remaining * loads[i] // whole), spare)
            given[i] = given[i] + more
            spare = spare - more
    return np.array([most] + given)


def ragged_sizes(key, count, total, most, lean):
    if count == 2:
        one = jax.random.randint(key, (), max(1, total - most), min(most, total - 1) + 1)
        return jnp.stack([one, total - one])
    sizes = jnp.asarray(profile(count, total, most, lean), jnp.int32)
    pairs = (count - 1) // 2
    source_of, receiver = sizes[1:1 + 2 * pairs:2], sizes[2:2 + 2 * pairs:2]
    margin = jnp.minimum(source_of - 1, most - receiver)
    moved = jax.random.randint(jax.random.fold_in(key, 1), (pairs,), 0, 1 << 20) % (margin + 1)
    sizes = sizes.at[1:1 + 2 * pairs:2].set(source_of - moved).at[2:2 + 2 * pairs:2].set(receiver + moved)
    return sizes[jax.random.permutation(jax.random.fold_in(key, 2), count)]


def noise(stream_key, extent, width, limit, pieces=(), kind=jnp.bfloat16):
    result = jax.random.normal(stream_key, extent, jnp.float32) * width
    if len(pieces) > 0:
        result = level_of(stream_key, extent, pieces, -0.22, 0.18) * result
    return jnp.clip(result, min=-limit, max=limit).astype(kind)


def setup_inputs(seed: int = 0, part: int = 0) -> dict:
    key_of = jax.random.split(jax.random.key(seed), 11)
    own_keys = jax.random.split(jax.random.fold_in(key_of[10], part), 11)
    cotangent = noise(own_keys[0], (SECTIONS, TOKENS, D), 1.0, 6.0, ((0, 2), (1, 4)))
    routes = different_ones(own_keys[1], SECTIONS * BLOCKS, EXPERTS, 2, 8192).reshape((SECTIONS, BLOCKS, 2))
    gate_values = jnp.clip(0.1 + 0.79999997 * jax.random.uniform(own_keys[2], (SECTIONS, TOKENS, 2), jnp.float32) ** level_of(own_keys[2], (SECTIONS, TOKENS, 2), ((0, 2), (1, 4)), -0.2, 0.2), 0.1, 0.9)
    up_weight = noise(key_of[3], (SECTIONS, PIECES, D, FF_PIECE), D ** -0.5, 0.125, ((0, 2), (1, 4), (3, 2)))
    down_weight = noise(key_of[4], (SECTIONS, PIECES, FF_PIECE, D), FF ** -0.5, 0.0625, ((0, 2), (1, 4), (2, 2)))
    pre_activation = noise(own_keys[5], (SECTIONS, PIECES, PIECES, TOK_DEV, FF_PIECE), 1.0, 6.0, ((0, 2), (1, 4), (4, 2)))
    input_sketch = noise(own_keys[6], (SECTIONS, TOKENS, RANK), 1.0, 6.0, ((0, 2), (1, 4)), jnp.float32)
    model_sketch = noise(key_of[7], (SECTIONS, D, RANK), D ** -0.5, 0.125, ((0, 2),))
    hidden_sketch = noise(key_of[8], (SECTIONS, PIECES, FF_PIECE, RANK), FF ** -0.5, 0.0625, ((0, 2), (1, 4), (2, 2)))
    lengths = jax.vmap(lambda own: ragged_sizes(own, EX_DEV, TOK_DEV, MOST_EX, 2))(jax.random.split(own_keys[9], SECTIONS * PIECES)).reshape((SECTIONS, PIECES, EX_DEV)).astype(jnp.int32)
    return {"cotangent": cotangent, "routes": routes, "gate_values": gate_values, "up_weight": up_weight, "down_weight": down_weight, "pre_activation": pre_activation, "input_sketch": input_sketch, "model_sketch": model_sketch, "hidden_sketch": hidden_sketch, "lengths": lengths}


def expert_rows(rows_in, pre_rows, up_local, down_local, sketch_local):
    pre = pre_rows.astype(jnp.float32)
    sig = jax.nn.sigmoid(pre)
    hidden = (pre * sig).astype(jnp.bfloat16)
    slope = sig * (1.0 + pre * (1.0 - sig))
    grad_hidden = lax.dot_general(rows_in, down_local, (((1,), (1,)), ((), ())), preferred_element_type=jnp.float32)
    grad_pre = (grad_hidden * slope).astype(jnp.bfloat16)
    partial_in = lax.dot_general(grad_pre, up_local, (((1,), (1,)), ((), ())), preferred_element_type=jnp.float32)
    down_part = jnp.dot(hidden, sketch_local, preferred_element_type=jnp.float32)
    up_part = jnp.dot(grad_pre, sketch_local, preferred_element_type=jnp.float32)
    return partial_in, down_part, up_part


def reference(cotangent, routes, gate_values, up_weight, down_weight, pre_activation, input_sketch, model_sketch, hidden_sketch, lengths):
    per_expert = PIECES // EXPERTS
    grads = []
    feats = []
    for section in range(SECTIONS):
        cot = cotangent[section]
        cot_f = cot.astype(jnp.float32)
        token_routes = jnp.repeat(routes[section], BLOCK, axis=0)
        section_gates = gate_values[section]

        def piece_step(carry, piece):
            grad_term, down_vec, up_vec = carry
            expert = piece // per_expert
            weight = jnp.sum(jnp.where(token_routes == expert, section_gates, 0.0), axis=1)
            rows_in = (weight[:, None] * cot_f).astype(jnp.bfloat16)
            pre_rows = lax.dynamic_index_in_dim(pre_activation[section], piece, 0, keepdims=False).reshape(TOKENS, FF_PIECE)
            up_local = lax.dynamic_index_in_dim(up_weight[section], piece, 0, keepdims=False)
            down_local = lax.dynamic_index_in_dim(down_weight[section], piece, 0, keepdims=False)
            sketch_local = lax.dynamic_index_in_dim(hidden_sketch[section], piece, 0, keepdims=False)
            partial_in, down_part, up_part = expert_rows(rows_in, pre_rows, up_local, down_local, sketch_local)
            return (grad_term + partial_in, down_vec + weight[:, None] * down_part, up_vec + up_part), None

        start = (jnp.zeros((TOKENS, D), jnp.float32), jnp.zeros((TOKENS, RANK), jnp.float32), jnp.zeros((TOKENS, RANK), jnp.float32))
        (grad_term, down_vec, up_vec), unused = lax.scan(piece_step, start, jnp.arange(PIECES, dtype=jnp.int32))
        grads.append((cot_f + grad_term).astype(jnp.bfloat16))
        out_vec = jnp.dot(cot, model_sketch[section], preferred_element_type=jnp.float32)
        counts = lengths[section]
        ends = jnp.cumsum(counts, axis=1)
        starts = ends - counts
        position = jnp.arange(TOK_DEV, dtype=jnp.int32)
        member = ((position[None, None, :] >= starts[:, :, None]) & (position[None, None, :] < ends[:, :, None])).astype(jnp.float32)
        down_feat = jnp.einsum("qet,qta,qtb->qeab", member, out_vec.reshape(PIECES, TOK_DEV, RANK), down_vec.reshape(PIECES, TOK_DEV, RANK), precision=lax.Precision.HIGHEST)
        up_feat = jnp.einsum("qet,qta,qtb->qeab", member, up_vec.reshape(PIECES, TOK_DEV, RANK), input_sketch[section].reshape(PIECES, TOK_DEV, RANK), precision=lax.Precision.HIGHEST)
        feats.append(jnp.concatenate([down_feat, up_feat], axis=3).reshape(EXAMPLES, RANK, 2 * RANK))
    handed = jnp.roll(jnp.stack(grads), -1, axis=0)
    return handed, jnp.stack(feats)
```

```python
import jax
import jax.numpy as jnp
from jax import lax
from jax.sharding import PartitionSpec as P

EXPERTS = 4


def shifted(block, axis, distance):
    n = lax.axis_size(axis)
    return lax.ppermute(block, axis, [(i, (i + distance) % n) for i in range(n)])


def both_halves(mine, theirs, core):
    first = jnp.where(core == 0, mine, theirs)
    second = jnp.where(core == 0, theirs, mine)
    return jnp.concatenate([first, second], axis=0)


def per_device(
    cotangent,
    routes,
    gate_values,
    up_weight,
    down_weight,
    pre_activation,
    input_sketch,
    model_sketch,
    hidden_sketch,
    lengths,
):
    pieces = lax.axis_size("dp")
    per_expert = pieces // EXPERTS
    place = lax.axis_index("dp")
    core = lax.axis_index("tensor")
    cot = cotangent[0]
    tok_dev, width = cot.shape
    half = tok_dev // 2
    rank = model_sketch.shape[2]
    blocks = routes.shape[1]
    block_len = tok_dev // blocks
    up_local = up_weight[0, 0]
    down_local = down_weight[0, 0]
    sketch_local = hidden_sketch[0, 0]
    pre_all = pre_activation[0, 0]
    hidden_cols = up_local.shape[1]

    cot_half = lax.dynamic_slice_in_dim(cot, core * half, half, 0)
    got = [shifted(cot_half, "dp", k) for k in range(1, pieces)]
    traded = [shifted(g, "tensor", 1) for g in got]
    rows_in = jnp.zeros((pieces, tok_dev, width), cot.dtype)
    rows_in = lax.dynamic_update_slice(rows_in, cot[None], (place, 0, 0))
    for k in range(1, pieces):
        source = (place - k) % pieces
        block = both_halves(got[k - 1], traded[k - 1], core)
        rows_in = lax.dynamic_update_slice(rows_in, block[None], (source, 0, 0))
    rows_in = rows_in.reshape(pieces * tok_dev, width)

    pre = pre_all.reshape(pieces * tok_dev, hidden_cols).astype(jnp.float32)
    sig = jax.nn.sigmoid(pre)
    hidden = (pre * sig).astype(jnp.bfloat16)
    slope = sig * (1.0 + pre * (1.0 - sig))
    down_part = jnp.dot(hidden, sketch_local, preferred_element_type=jnp.float32)

    grad_hidden = lax.dot_general(
        rows_in, down_local, (((1,), (1,)), ((), ())), preferred_element_type=jnp.float32
    )
    grad_pre = (grad_hidden * slope).astype(jnp.bfloat16)
    partial_in = lax.dot_general(
        grad_pre, up_local, (((1,), (1,)), ((), ())), preferred_element_type=jnp.float32
    )
    up_part = jnp.dot(grad_pre, sketch_local, preferred_element_type=jnp.float32)
    terms = jnp.concatenate([partial_in, down_part, up_part], axis=1)
    terms = terms.reshape(pieces, 2, half, width + 2 * rank)

    keep = lax.dynamic_index_in_dim(terms, core, 1, keepdims=False)
    give = lax.dynamic_index_in_dim(terms, 1 - core, 1, keepdims=False).astype(jnp.bfloat16)
    summed = keep + shifted(give, "tensor", 1).astype(jnp.float32)
    sent = summed.astype(jnp.bfloat16)
    own = lax.dynamic_index_in_dim(summed, place, 0, keepdims=False)
    backs = []
    for k in range(1, pieces):
        source = (place - k) % pieces
        backs.append(shifted(lax.dynamic_index_in_dim(sent, source, 0, keepdims=False), "dp", -k))

    token_routes = jnp.broadcast_to(routes[0][:, None, :], (blocks, block_len, 2)).reshape(
        tok_dev, 2
    )
    half_routes = lax.dynamic_slice_in_dim(token_routes, core * half, half, 0)
    half_gates = lax.dynamic_slice_in_dim(gate_values[0], core * half, half, 0)

    def weight_of(piece):
        return jnp.sum(
            jnp.where(half_routes == piece // per_expert, half_gates, 0.0), axis=1, keepdims=True
        )

    def weighted(piece, block):
        scale = weight_of(piece)
        return block * scale

    total = weighted(place, own)
    for k in range(1, pieces):
        total = total + weighted((place + k) % pieces, backs[k - 1].astype(jnp.float32))
    grad_half = (
        lax.dynamic_slice_in_dim(cot, core * half, half, 0).astype(jnp.float32) + total[:, :width]
    ).astype(jnp.bfloat16)
    handed_half = shifted(grad_half, "section", -1)
    handed = both_halves(handed_half, shifted(handed_half, "tensor", 1), core)

    sketch_half = total[:, width:]
    sketch_sum = both_halves(sketch_half, shifted(sketch_half, "tensor", 1), core)
    out_vec = jnp.dot(cot, model_sketch[0], preferred_element_type=jnp.float32)
    counts = lengths[0, 0]
    ends = jnp.cumsum(counts)
    starts = ends - counts
    position = jnp.arange(tok_dev, dtype=jnp.int32)
    member = ((position[None, :] >= starts[:, None]) & (position[None, :] < ends[:, None])).astype(
        jnp.float32
    )
    down_feat = jnp.einsum(
        "et,ta,tb->eab", member, out_vec, sketch_sum[:, :rank], precision=lax.Precision.HIGHEST
    )
    up_feat = jnp.einsum(
        "et,ta,tb->eab",
        member,
        sketch_sum[:, rank:],
        input_sketch[0],
        precision=lax.Precision.HIGHEST,
    )
    features = jnp.concatenate([down_feat, up_feat], axis=2)
    return (handed[None], features[None])


def solution(mesh):
    in_specs = (
        P("section", ("groups", "dp"), None),
        P("section", ("groups", "dp"), None),
        P("section", ("groups", "dp"), None),
        P("section", "dp", None, "tensor"),
        P("section", "dp", "tensor", None),
        P("section", ("groups", "dp"), None, None, "tensor"),
        P("section", ("groups", "dp"), None),
        P("section", None, None),
        P("section", "dp", "tensor", None),
        P("section", ("groups", "dp"), None),
    )
    out_specs = (P("section", ("groups", "dp"), None), P("section", ("groups", "dp"), None, None))
    return jax.shard_map(
        per_device, mesh=mesh, in_specs=in_specs, out_specs=out_specs, check_vma=False
    )
```

```python
import functools

import jax
import jax.numpy as jnp
from jax import lax
from jax.experimental import pallas as pl
from jax.experimental.pallas import tpu as pltpu
from jax.sharding import PartitionSpec as P

EXPERTS = 4
CHUNKS = 2
NT = (((1,), (1,)), ((), ()))


def xored(block, axis, bits):
    n = lax.axis_size(axis)
    return lax.ppermute(block, axis, [(i, i ^ bits) for i in range(n)])


def returned(block, bits):
    sections, pieces = lax.axis_size("section"), lax.axis_size("dp")
    route = []
    for s in range(sections):
        for z in range(pieces):
            route.append((z * sections + s, (z ^ bits) * sections + (s - 1) % sections))
    return lax.ppermute(block, ("dp", "section"), route)


def flipped(array, axis, by):
    n = array.shape[axis]
    bit = 1
    while bit < n:
        shape = array.shape
        cut = shape[:axis] + (n // (2 * bit), 2, bit) + shape[axis + 1 :]
        other = jnp.flip(array.reshape(cut), axis + 1).reshape(shape)
        array = jnp.where((by // bit) % 2 == 1, other, array)
        bit *= 2
    return array


def tile_of(size, most):
    best = 128
    for tile in range(128, most + 1, 128):
        if size % tile == 0:
            best = tile
    return best


def slope_kernel(groups, index_ref, *refs):
    del index_ref
    pre_refs = refs[:groups]
    sketch_ref, slope_ref, down_ref = refs[groups:]
    pre = jnp.concatenate([r[0, 0, 0] for r in pre_refs], axis=0).astype(jnp.float32)
    sig = jax.nn.sigmoid(pre)
    hidden = (pre * sig).astype(jnp.bfloat16)
    slope_ref[0] = (sig * (1.0 + pre * (1.0 - sig))).astype(slope_ref.dtype)
    term = jnp.dot(hidden, sketch_ref[...], preferred_element_type=jnp.float32)

    @pl.when(pl.program_id(1) == 0)
    def _():
        down_ref[0] = jnp.zeros_like(down_ref[0])

    down_ref[0] += term


def slopes(pre, sketch, place, core):
    n, _, chunks, rows, cols = pre.shape
    rank = sketch.shape[1]
    groups = 2 * n
    tile = tile_of(cols, 512)
    index = jnp.stack([place, core]).astype(jnp.int32)

    def spec_of(h, slot):
        return pl.BlockSpec(
            (1, 1, 1, rows, tile), lambda a, j, ix: (ix[0] ^ slot, ix[1] ^ h, a, 0, j)
        )

    return pl.pallas_call(
        functools.partial(slope_kernel, groups),
        grid_spec=pltpu.PrefetchScalarGridSpec(
            num_scalar_prefetch=1,
            grid=(chunks, cols // tile),
            in_specs=[spec_of(h, slot) for h in range(2) for slot in range(n)]
            + [pl.BlockSpec((tile, rank), lambda a, j, ix: (j, 0))],
            out_specs=[
                pl.BlockSpec((1, groups * rows, tile), lambda a, j, ix: (a, 0, j)),
                pl.BlockSpec((1, groups * rows, rank), lambda a, j, ix: (a, 0, 0)),
            ],
        ),
        out_shape=[
            jax.ShapeDtypeStruct((chunks, groups * rows, cols), jnp.bfloat16),
            jax.ShapeDtypeStruct((chunks, groups * rows, rank), jnp.float32),
        ],
        cost_estimate=pl.CostEstimate(
            flops=2 * chunks * groups * rows * cols * rank,
            bytes_accessed=4 * chunks * groups * rows * cols,
            transcendentals=chunks * groups * rows * cols,
        ),
        name="slopes",
    )(index, *([pre] * groups), sketch)


def expert_kernel(
    tile_f,
    tile_d,
    rows_ref,
    weight_ref,
    slope_ref,
    sketch_ref,
    down_hbm,
    up_hbm,
    keep_ref,
    give_ref,
    vec_ref,
    down_buf,
    up_buf,
    grad_buf,
    down_sem,
    up_sem,
):
    hidden_cols, width = down_buf.shape
    steps_f, steps_d = hidden_cols // tile_f, width // tile_d

    def down_copy(j):
        part = pl.ds(pl.multiple_of(j * tile_f, tile_f), tile_f)
        return pltpu.make_async_copy(down_hbm.at[part], down_buf.at[part], down_sem.at[j])

    def up_copy(j):
        part = pl.ds(pl.multiple_of(j * tile_d, tile_d), tile_d)
        return pltpu.make_async_copy(up_hbm.at[part], up_buf.at[part], up_sem.at[j])

    for j in range(steps_f):
        down_copy(j).start()
    for j in range(steps_d):
        up_copy(j).start()
    vec_ref[...] = jnp.zeros_like(vec_ref)

    def first(j, carry):
        down_copy(j).wait()
        part = pl.ds(pl.multiple_of(j * tile_f, tile_f), tile_f)
        grad_hidden = lax.dot_general(
            rows_ref[...], down_buf[part, :], NT, preferred_element_type=jnp.float32
        )
        slope = slope_ref[0, :, part].astype(jnp.float32)
        grad_pre = (grad_hidden * slope).astype(jnp.bfloat16)
        grad_buf[:, part] = grad_pre
        vec_ref[...] += jnp.dot(
            grad_pre, sketch_ref[part, :], preferred_element_type=jnp.float32
        )
        return carry

    lax.fori_loop(0, steps_f, first, 0)
    half = keep_ref.shape[0]

    def second(j, carry):
        up_copy(j).wait()
        part = pl.ds(pl.multiple_of(j * tile_d, tile_d), tile_d)
        term = lax.dot_general(
            grad_buf[...], up_buf[part, :], NT, preferred_element_type=jnp.float32
        )
        keep_ref[:, part] = term[:half]
        give_ref[:, part] = term[half:].astype(jnp.bfloat16)
        return carry

    lax.fori_loop(0, steps_d, second, 0)


def expert(chunk, rows, weight, slope, sketch, down_local, up_local):
    count, width = rows.shape
    hidden_cols = down_local.shape[0]
    rank = sketch.shape[1]
    tile_f, tile_d = tile_of(hidden_cols, 512), tile_of(width, 256)
    return pl.pallas_call(
        functools.partial(expert_kernel, tile_f, tile_d),
        grid=(1,),
        in_specs=[
            pl.BlockSpec((count, width), lambda i: (0, 0)),
            pl.BlockSpec((count, 1), lambda i: (0, 0)),
            pl.BlockSpec((1, count, hidden_cols), lambda i: (chunk, 0, 0)),
            pl.BlockSpec((hidden_cols, rank), lambda i: (0, 0)),
            pl.BlockSpec(memory_space=pl.ANY),
            pl.BlockSpec(memory_space=pl.ANY),
        ],
        out_specs=[
            pl.BlockSpec((count // 2, width), lambda i: (0, 0)),
            pl.BlockSpec((count // 2, width), lambda i: (0, 0)),
            pl.BlockSpec((count, rank), lambda i: (0, 0)),
        ],
        out_shape=[
            jax.ShapeDtypeStruct((count // 2, width), jnp.float32),
            jax.ShapeDtypeStruct((count // 2, width), jnp.bfloat16),
            jax.ShapeDtypeStruct((count, rank), jnp.float32),
        ],
        scratch_shapes=[
            pltpu.VMEM((hidden_cols, width), jnp.bfloat16),
            pltpu.VMEM((width, hidden_cols), jnp.bfloat16),
            pltpu.VMEM((count, hidden_cols), jnp.bfloat16),
            pltpu.SemaphoreType.DMA((hidden_cols // tile_f,)),
            pltpu.SemaphoreType.DMA((width // tile_d,)),
        ],
        compiler_params=pltpu.CompilerParams(vmem_limit_bytes=50 << 20),
        cost_estimate=pl.CostEstimate(
            flops=4 * count * hidden_cols * width,
            bytes_accessed=4 * hidden_cols * width,
            transcendentals=0,
        ),
        name="expert",
    )(rows, weight, slope, sketch, down_local, up_local)


def per_device(
    cotangent,
    routes,
    gate_values,
    up_weight,
    down_weight,
    pre_activation,
    input_sketch,
    model_sketch,
    hidden_sketch,
    lengths,
):
    pieces = lax.axis_size("dp")
    per_expert = pieces // EXPERTS
    place = lax.axis_index("dp")
    core = lax.axis_index("tensor")
    cot = cotangent[0]
    tok_dev, width = cot.shape
    half = tok_dev // 2
    rows = half // CHUNKS
    rank = model_sketch.shape[2]
    blocks = routes.shape[1]
    block_len = tok_dev // blocks
    sketch_local = hidden_sketch[0, 0]
    pre_all = pre_activation[0, 0]
    hidden_cols = pre_all.shape[2]

    token_routes = jnp.broadcast_to(routes[0][:, None, :], (blocks, block_len, 2)).reshape(
        tok_dev, 2
    )
    dest_expert = jnp.arange(pieces, dtype=jnp.int32) // per_expert
    hits = token_routes[None, :, :] == dest_expert[:, None, None]
    weight = jnp.sum(jnp.where(hits, gate_values[0][None, :, :], 0.0), axis=2)
    weight_all = lax.all_gather(weight, "dp", axis=0)
    weight_here = lax.dynamic_index_in_dim(weight_all, place, 1, keepdims=False)
    weight_here = flipped(weight_here.reshape(pieces, 2, CHUNKS, rows), 0, place)
    weight_here = flipped(weight_here, 1, core).transpose(2, 1, 0, 3)
    weight_here = weight_here.reshape(CHUNKS, 2 * pieces * rows, 1)

    cot_mine = lax.dynamic_slice_in_dim(cot, core * half, half, 0)
    cot_theirs = lax.dynamic_slice_in_dim(cot, (1 - core) * half, half, 0)
    chunk_rows = []
    for a in range(CHUNKS):
        part = slice(a * rows, (a + 1) * rows)
        mine, theirs = {0: cot_mine[part]}, {0: cot_theirs[part]}
        order = sorted(range(1, pieces), key=lambda k: (bin(k).count("1"), -k))
        for slot in order:
            low = slot & -slot
            mine[slot] = xored(mine[slot ^ low], "dp", low)
        for slot in order:
            theirs[slot] = xored(mine[slot], "tensor", 1)
        chunk_rows.append(
            jnp.concatenate(
                [mine[k] for k in range(pieces)] + [theirs[k] for k in range(pieces)], axis=0
            )
        )

    sections = lax.axis_size("section")
    cot_below = lax.ppermute(
        cot_mine, "section", [(s, (s - 1) % sections) for s in range(sections)]
    )

    slope, down_part = slopes(
        pre_all.reshape(pieces, 2, CHUNKS, rows, hidden_cols), sketch_local, place, core
    )

    finished, vectors = [], []
    for a in range(CHUNKS):
        dispatched = (weight_here[a] * chunk_rows[a].astype(jnp.float32)).astype(jnp.bfloat16)
        keep, give, up_part = expert(
            a, dispatched, weight_here[a], slope, sketch_local, down_weight[0, 0], up_weight[0, 0]
        )
        summed = (keep + xored(give, "tensor", 1).astype(jnp.float32)).astype(jnp.bfloat16)
        summed = summed.reshape(pieces, rows, width)
        order = sorted(range(pieces), key=lambda k: -k)
        total = cot_below[a * rows : (a + 1) * rows].astype(jnp.float32)
        for slot in order:
            total = total + returned(summed[slot], slot).astype(jnp.float32)
        finished.append(total.astype(jnp.bfloat16))
        vectors.append(jnp.concatenate([weight_here[a] * down_part[a], up_part], axis=1))

    mine = jnp.concatenate(finished, axis=0)
    theirs = jnp.concatenate([xored(f, "tensor", 1) for f in finished], axis=0)
    handed = jnp.concatenate(
        [jnp.where(core == 0, mine, theirs), jnp.where(core == 0, theirs, mine)], axis=0
    )

    vec = jnp.stack(vectors).reshape(CHUNKS, 2, pieces, rows, 2 * rank).transpose(2, 1, 0, 3, 4)
    vec = flipped(flipped(vec, 0, place), 1, core).reshape(pieces * tok_dev, 2 * rank)
    vec_mine = lax.psum_scatter(vec, ("dp", "tensor"), scatter_dimension=0, tiled=True)
    vec_theirs = xored(vec_mine, "tensor", 1)
    sketch_sum = jnp.concatenate(
        [jnp.where(core == 0, vec_mine, vec_theirs), jnp.where(core == 0, vec_theirs, vec_mine)],
        axis=0,
    )
    out_vec = jnp.dot(cot, model_sketch[0], preferred_element_type=jnp.float32)
    counts = lengths[0, 0]
    ends = jnp.cumsum(counts)
    starts = ends - counts
    position = jnp.arange(tok_dev, dtype=jnp.int32)
    member = ((position[None, :] >= starts[:, None]) & (position[None, :] < ends[:, None])).astype(
        jnp.float32
    )
    down_feat = jnp.einsum(
        "et,ta,tb->eab", member, out_vec, sketch_sum[:, :rank], precision=lax.Precision.HIGHEST
    )
    up_feat = jnp.einsum(
        "et,ta,tb->eab",
        member,
        sketch_sum[:, rank:],
        input_sketch[0],
        precision=lax.Precision.HIGHEST,
    )
    features = jnp.concatenate([down_feat, up_feat], axis=2)
    return (handed[None], features[None])


def solution(mesh):
    in_specs = (
        P("section", ("groups", "dp"), None),
        P("section", ("groups", "dp"), None),
        P("section", ("groups", "dp"), None),
        P("section", "dp", None, "tensor"),
        P("section", "dp", "tensor", None),
        P("section", ("groups", "dp"), None, None, "tensor"),
        P("section", ("groups", "dp"), None),
        P("section", None, None),
        P("section", "dp", "tensor", None),
        P("section", ("groups", "dp"), None),
    )
    out_specs = (P("section", ("groups", "dp"), None), P("section", ("groups", "dp"), None, None))
    return jax.shard_map(
        per_device, mesh=mesh, in_specs=in_specs, out_specs=out_specs, check_vma=False
    )
```

```python
import functools

import jax
import jax.numpy as jnp
from jax import lax
from jax.experimental import pallas as pl
from jax.experimental.pallas import tpu as pltpu
from jax.sharding import PartitionSpec as P

EXPERTS = 4
CHUNKS = 2
NT = (((1,), (1,)), ((), ()))


def xored(block, axis, bits):
    n = lax.axis_size(axis)
    return lax.ppermute(block, axis, [(i, i ^ bits) for i in range(n)])


def returned(block, bits):
    sections, pieces = lax.axis_size("section"), lax.axis_size("dp")
    route = []
    for s in range(sections):
        for z in range(pieces):
            route.append((z * sections + s, (z ^ bits) * sections + (s - 1) % sections))
    return lax.ppermute(block, ("dp", "section"), route)


ANYWHERE = pl.BlockSpec(memory_space=pl.ANY)


def held_kernel(block_ref, *refs):
    refs[-1][...] = block_ref[...]


def held(block, *events):
    spec = pl.BlockSpec(block.shape, lambda i: (0, 0))
    return pl.pallas_call(
        held_kernel,
        grid=(1,),
        in_specs=[spec] + [ANYWHERE] * len(events),
        out_specs=spec,
        out_shape=jax.ShapeDtypeStruct(block.shape, block.dtype),
        name="held",
    )(block, *events)


def merge_kernel(keep_ref, came_ref, *refs):
    sent_ref, vec_ref = refs[-2:]
    width = sent_ref.shape[1]
    total = keep_ref[...] + came_ref[...].astype(jnp.float32)
    sent_ref[...] = total[:, :width].astype(jnp.bfloat16)
    vec_ref[...] = total[:, width:]


def merged(keep, came, width, *events):
    count, wide = keep.shape
    spec = pl.BlockSpec((count, wide), lambda i: (0, 0))
    return pl.pallas_call(
        merge_kernel,
        grid=(1,),
        in_specs=[spec, spec] + [ANYWHERE] * len(events),
        out_specs=[
            pl.BlockSpec((count, width), lambda i: (0, 0)),
            pl.BlockSpec((count, wide - width), lambda i: (0, 0)),
        ],
        out_shape=[
            jax.ShapeDtypeStruct((count, width), jnp.bfloat16),
            jax.ShapeDtypeStruct((count, wide - width), jnp.float32),
        ],
        cost_estimate=pl.CostEstimate(
            flops=count * wide, bytes_accessed=8 * count * wide, transcendentals=0
        ),
        name="merge",
    )(keep, came, *events)


def tile_of(size, most):
    best = 128
    for tile in range(128, most + 1, 128):
        if size % tile == 0:
            best = tile
    return best


def slope_kernel(groups, index_ref, *refs):
    del index_ref
    pre_refs, sketch_ref = refs[:groups], refs[groups]
    slope_ref, down_ref = refs[-2:]
    pre = jnp.concatenate([r[0, 0, 0] for r in pre_refs], axis=0).astype(jnp.float32)
    sig = 0.5 + 0.5 * jnp.tanh(0.5 * pre)
    hidden = pre * sig
    slope = sig + hidden * (1.0 - sig)
    slope_ref[...] = slope.T.astype(slope_ref.dtype)
    term = jnp.dot(
        hidden.astype(jnp.bfloat16), sketch_ref[...], preferred_element_type=jnp.float32
    )

    @pl.when(pl.program_id(0) == 0)
    def _():
        down_ref[...] = jnp.zeros_like(down_ref)

    down_ref[...] += term


def slopes(chunk, pre, sketch, place, core, *events):
    n, _, _, rows, cols = pre.shape
    rank = sketch.shape[1]
    groups = 2 * n
    tile = tile_of(cols, 896)
    index = jnp.stack([place, core]).astype(jnp.int32)

    def spec_of(h, slot):
        return pl.BlockSpec(
            (1, 1, 1, rows, tile), lambda j, ix: (ix[0] ^ slot, ix[1] ^ h, chunk, 0, j)
        )

    return pl.pallas_call(
        functools.partial(slope_kernel, groups),
        grid_spec=pltpu.PrefetchScalarGridSpec(
            num_scalar_prefetch=1,
            grid=(cols // tile,),
            in_specs=[spec_of(h, slot) for h in range(2) for slot in range(n)]
            + [pl.BlockSpec((tile, rank), lambda j, ix: (j, 0))]
            + [ANYWHERE] * len(events),
            out_specs=[
                pl.BlockSpec((tile, groups * rows), lambda j, ix: (j, 0)),
                pl.BlockSpec((groups * rows, rank), lambda j, ix: (0, 0)),
            ],
        ),
        out_shape=[
            jax.ShapeDtypeStruct((cols, groups * rows), jnp.bfloat16),
            jax.ShapeDtypeStruct((groups * rows, rank), jnp.float32),
        ],
        cost_estimate=pl.CostEstimate(
            flops=2 * groups * rows * cols * rank,
            bytes_accessed=4 * groups * rows * cols,
            transcendentals=groups * rows * cols,
        ),
        name="slopes",
    )(index, *([pre] * groups), sketch, *events)


def expert_kernel(
    tile_f,
    tile_d,
    rows_ref,
    slope_ref,
    down_part_ref,
    sketch_ref,
    down_hbm,
    up_hbm,
    *refs,
):
    keep_ref, give_ref, down_buf, up_buf, grad_buf, down_sem, up_sem = refs[-7:]
    hidden_cols, width = down_buf.shape
    steps_f, steps_d = hidden_cols // tile_f, width // tile_d
    half = keep_ref.shape[0]

    def down_copy(j):
        part = pl.ds(pl.multiple_of(j * tile_f, tile_f), tile_f)
        return pltpu.make_async_copy(down_hbm.at[part], down_buf.at[part], down_sem.at[j])

    def up_copy(j):
        part = pl.ds(pl.multiple_of(j * tile_d, tile_d), tile_d)
        return pltpu.make_async_copy(up_hbm.at[part], up_buf.at[part], up_sem.at[j])

    for j in range(steps_f):
        down_copy(j).start()
    for j in range(steps_d):
        up_copy(j).start()

    def first(j, carry):
        down_copy(j).wait()
        part = pl.ds(pl.multiple_of(j * tile_f, tile_f), tile_f)
        grad_hidden = lax.dot_general(
            down_buf[part, :], rows_ref[...], NT, preferred_element_type=jnp.float32
        )
        slope = slope_ref[part, :].astype(jnp.float32)
        grad_buf[part, :] = (grad_hidden * slope).astype(jnp.bfloat16)
        return carry

    lax.fori_loop(0, steps_f, first, 0)

    up_part = jnp.dot(sketch_ref[...], grad_buf[...], preferred_element_type=jnp.float32).T
    vectors = jnp.concatenate([down_part_ref[...], up_part], axis=1)
    keep_ref[:, width:] = vectors[:half]
    give_ref[:, width:] = vectors[half:].astype(jnp.bfloat16)

    def second(j, carry):
        up_copy(j).wait()
        part = pl.ds(pl.multiple_of(j * tile_d, tile_d), tile_d)
        term = jnp.dot(up_buf[part, :], grad_buf[...], preferred_element_type=jnp.float32).T
        keep_ref[:, part] = term[:half]
        give_ref[:, part] = term[half:].astype(jnp.bfloat16)
        return carry

    lax.fori_loop(0, steps_d, second, 0)


def expert(rows, slope, down_part, sketch_t, down_local, up_local, *events):
    count, width = rows.shape
    hidden_cols = down_local.shape[0]
    rank = sketch_t.shape[0]
    tile_f, tile_d = tile_of(hidden_cols, 512), tile_of(width, 512)
    wide = width + 2 * rank
    return pl.pallas_call(
        functools.partial(expert_kernel, tile_f, tile_d),
        grid=(1,),
        in_specs=[
            pl.BlockSpec((count, width), lambda i: (0, 0)),
            pl.BlockSpec((hidden_cols, count), lambda i: (0, 0)),
            pl.BlockSpec((count, rank), lambda i: (0, 0)),
            pl.BlockSpec((rank, hidden_cols), lambda i: (0, 0)),
            ANYWHERE,
            ANYWHERE,
        ]
        + [ANYWHERE] * len(events),
        out_specs=[
            pl.BlockSpec((count // 2, wide), lambda i: (0, 0)),
            pl.BlockSpec((count // 2, wide), lambda i: (0, 0)),
        ],
        out_shape=[
            jax.ShapeDtypeStruct((count // 2, wide), jnp.float32),
            jax.ShapeDtypeStruct((count // 2, wide), jnp.bfloat16),
        ],
        scratch_shapes=[
            pltpu.VMEM((hidden_cols, width), jnp.bfloat16),
            pltpu.VMEM((width, hidden_cols), jnp.bfloat16),
            pltpu.VMEM((hidden_cols, count), jnp.bfloat16),
            pltpu.SemaphoreType.DMA((hidden_cols // tile_f,)),
            pltpu.SemaphoreType.DMA((width // tile_d,)),
        ],
        compiler_params=pltpu.CompilerParams(vmem_limit_bytes=50 << 20),
        cost_estimate=pl.CostEstimate(
            flops=4 * count * hidden_cols * width,
            bytes_accessed=4 * hidden_cols * width,
            transcendentals=0,
        ),
        name="expert",
    )(rows, slope, down_part, sketch_t, down_local, up_local, *events)


def per_device(
    cotangent,
    routes,
    gate_values,
    up_weight,
    down_weight,
    pre_activation,
    input_sketch,
    model_sketch,
    hidden_sketch,
    lengths,
):
    pieces = lax.axis_size("dp")
    sections = lax.axis_size("section")
    per_expert = pieces // EXPERTS
    place = lax.axis_index("dp")
    core = lax.axis_index("tensor")
    cot = cotangent[0]
    tok_dev, width = cot.shape
    half = tok_dev // 2
    rows = half // CHUNKS
    rank = model_sketch.shape[2]
    blocks = routes.shape[1]
    block_len = tok_dev // blocks
    sketch_local = hidden_sketch[0, 0]
    pre_all = pre_activation[0, 0]
    hidden_cols = pre_all.shape[2]
    pre_all = pre_all.reshape(pieces, 2, CHUNKS, rows, hidden_cols)

    def below(block):
        return lax.ppermute(block, "section", [(s, (s - 1) % sections) for s in range(sections)])

    cot_mine = lax.dynamic_slice_in_dim(cot, core * half, half, 0)
    cot_theirs = lax.dynamic_slice_in_dim(cot, (1 - core) * half, half, 0)
    order = sorted(range(1, pieces), key=lambda k: (bin(k).count("1"), -k))
    chunk_rows, marks = [], []
    for a in range(CHUNKS):
        part = slice(a * rows, (a + 1) * rows)
        first = cot_mine[part]
        if a > 0:
            first = held(first, marks[a - 1])
        mine, theirs = {0: first}, {0: cot_theirs[part]}
        for slot in order:
            low = slot & -slot
            mine[slot] = xored(mine[slot ^ low], "dp", low)
        marks.append(mine[order[0]])
        for level in range(1, pieces.bit_length()):
            slots = [k for k in order if bin(k).count("1") == level]
            traded = xored(jnp.concatenate([mine[k] for k in slots], axis=0), "tensor", 1)
            for at, slot in enumerate(slots):
                theirs[slot] = traded[at * rows : (at + 1) * rows]
        chunk_rows.append(
            jnp.concatenate(
                [mine[k] for k in range(pieces)] + [theirs[k] for k in range(pieces)], axis=0
            )
        )

    token_routes = jnp.broadcast_to(routes[0][:, None, :], (blocks, block_len, 2)).reshape(
        tok_dev, 2
    )
    half_routes = lax.dynamic_slice_in_dim(token_routes, core * half, half, 0)
    half_gates = lax.dynamic_slice_in_dim(gate_values[0], core * half, half, 0)
    slot_expert = (place ^ jnp.arange(pieces, dtype=jnp.int32)) // per_expert
    hits = half_routes[:, None, :] == slot_expert[None, :, None]
    weight = jnp.sum(jnp.where(hits, half_gates[:, None, :], 0.0), axis=2)
    weight_below = below(weight)
    cot_below = below(cot_mine)

    sketch_t = sketch_local.T
    finished, vectors = [], []
    events = (weight_below, cot_below)
    for a in range(CHUNKS):
        slope, down_part = slopes(a, pre_all, sketch_local, place, core, *marks[:a])
        keep, give = expert(
            chunk_rows[a], slope, down_part, sketch_t, down_weight[0, 0], up_weight[0, 0], *events
        )
        sent, vec = merged(keep, xored(give, "tensor", 1), width, *finished)
        events = (sent,)
        part = slice(a * rows, (a + 1) * rows)
        total = cot_below[part].astype(jnp.float32)
        for slot in reversed(range(pieces)):
            back = returned(sent[slot * rows : (slot + 1) * rows], slot)
            total = total + weight_below[part, slot : slot + 1] * back.astype(jnp.float32)
        finished.append(total.astype(jnp.bfloat16))
        vectors.append(vec.reshape(pieces, rows, 2 * rank))

    mine = jnp.concatenate(finished, axis=0)
    theirs = jnp.concatenate([xored(f, "tensor", 1) for f in finished], axis=0)
    handed = jnp.concatenate(
        [jnp.where(core == 0, mine, theirs), jnp.where(core == 0, theirs, mine)], axis=0
    )

    vec = jnp.concatenate(vectors, axis=1).reshape(pieces * half, 2 * rank)
    vec = held(vec, back).reshape(pieces, half, 2 * rank)
    vec_mine = jnp.zeros((half, 2 * rank), jnp.float32)
    for slot in range(pieces):
        back = vec[slot] if slot == 0 else xored(vec[slot], "dp", slot)
        vec_mine = vec_mine + weight[:, slot : slot + 1] * back
    vec_theirs = xored(vec_mine, "tensor", 1)
    sketch_sum = jnp.concatenate(
        [jnp.where(core == 0, vec_mine, vec_theirs), jnp.where(core == 0, vec_theirs, vec_mine)],
        axis=0,
    )
    out_vec = jnp.dot(cot, model_sketch[0], preferred_element_type=jnp.float32)
    counts = lengths[0, 0]
    ends = jnp.cumsum(counts)
    starts = ends - counts
    position = jnp.arange(tok_dev, dtype=jnp.int32)
    member = ((position[None, :] >= starts[:, None]) & (position[None, :] < ends[:, None])).astype(
        jnp.float32
    )
    down_feat = jnp.einsum(
        "et,ta,tb->eab", member, out_vec, sketch_sum[:, :rank], precision=lax.Precision.HIGHEST
    )
    up_feat = jnp.einsum(
        "et,ta,tb->eab",
        member,
        sketch_sum[:, rank:],
        input_sketch[0],
        precision=lax.Precision.HIGHEST,
    )
    features = jnp.concatenate([down_feat, up_feat], axis=2)
    return (handed[None], features[None])


def solution(mesh):
    in_specs = (
        P("section", ("groups", "dp"), None),
        P("section", ("groups", "dp"), None),
        P("section", ("groups", "dp"), None),
        P("section", "dp", None, "tensor"),
        P("section", "dp", "tensor", None),
        P("section", ("groups", "dp"), None, None, "tensor"),
        P("section", ("groups", "dp"), None),
        P("section", None, None),
        P("section", "dp", "tensor", None),
        P("section", ("groups", "dp"), None),
    )
    out_specs = (P("section", ("groups", "dp"), None), P("section", ("groups", "dp"), None, None))
    return jax.shard_map(
        per_device, mesh=mesh, in_specs=in_specs, out_specs=out_specs, check_vma=False
    )
```

```python
import functools

import jax
import jax.numpy as jnp
from jax import lax
from jax.experimental import pallas as pl
from jax.experimental.pallas import tpu as pltpu
from jax.sharding import PartitionSpec as P

EXPERTS = 4
CHUNKS = 2
NT = (((1,), (1,)), ((), ()))


def xored(block, axis, bits):
    n = lax.axis_size(axis)
    return lax.ppermute(block, axis, [(i, i ^ bits) for i in range(n)])


ANYWHERE = pl.BlockSpec(memory_space=pl.ANY)
RESIDENT = pl.BlockSpec(memory_space=pltpu.VMEM)


def held_kernel(block_ref, *refs):
    refs[-1][...] = block_ref[...]


def held(block, *events):
    return pl.pallas_call(
        held_kernel,
        in_specs=[RESIDENT] + [ANYWHERE] * len(events),
        out_specs=RESIDENT,
        out_shape=jax.ShapeDtypeStruct(block.shape, block.dtype),
        compiler_params=pltpu.CompilerParams(vmem_limit_bytes=1 << 20),
        name="held",
    )(block, *events)


def merge_kernel(keep_ref, came_ref, *refs):
    own_ref, sent_ref = refs[-2:]
    rows = own_ref.shape[0]
    own_ref[...] = keep_ref[:rows] + came_ref[:rows].astype(jnp.float32)
    sent_ref[...] = (keep_ref[rows:] + came_ref[rows:].astype(jnp.float32)).astype(jnp.bfloat16)


def merged(keep, came, rows, *events):
    count, wide = keep.shape
    return pl.pallas_call(
        merge_kernel,
        in_specs=[RESIDENT] * 2 + [ANYWHERE] * len(events),
        out_specs=[RESIDENT] * 2,
        out_shape=[
            jax.ShapeDtypeStruct((rows, wide), jnp.float32),
            jax.ShapeDtypeStruct((count - rows, wide), jnp.bfloat16),
        ],
        compiler_params=pltpu.CompilerParams(vmem_limit_bytes=4 << 20),
        cost_estimate=pl.CostEstimate(
            flops=count * wide, bytes_accessed=8 * count * wide, transcendentals=0
        ),
        name="merge",
    )(keep, came, *events)


def tile_of(size, most):
    best = 128
    for tile in range(128, most + 1, 128):
        if size % tile == 0:
            best = tile
    return best


def slope_kernel(groups, index_ref, *refs):
    del index_ref
    pre_refs, sketch_ref = refs[:groups], refs[groups]
    slope_ref, down_ref = refs[-2:]
    pre = jnp.concatenate([r[0, 0, 0] for r in pre_refs], axis=0).astype(jnp.float32)
    sig = 0.5 + 0.5 * jnp.tanh(0.5 * pre)
    hidden = pre * sig
    slope = sig + hidden * (1.0 - sig)
    slope_ref[...] = slope.T.astype(slope_ref.dtype)
    term = lax.dot_general(
        hidden.astype(jnp.bfloat16), sketch_ref[...], NT, preferred_element_type=jnp.float32
    )

    @pl.when(pl.program_id(0) == 0)
    def _():
        down_ref[...] = jnp.zeros_like(down_ref)

    down_ref[...] += term


def slopes(chunk, pre, sketch_t, place, core, *events):
    n, _, _, rows, cols = pre.shape
    rank = sketch_t.shape[0]
    groups = 2 * n
    tile = tile_of(cols, 896)
    index = jnp.stack([place, core]).astype(jnp.int32)

    def spec_of(h, slot):
        return pl.BlockSpec(
            (1, 1, 1, rows, tile), lambda j, ix: (ix[0] ^ slot, ix[1] ^ h, chunk, 0, j)
        )

    return pl.pallas_call(
        functools.partial(slope_kernel, groups),
        grid_spec=pltpu.PrefetchScalarGridSpec(
            num_scalar_prefetch=1,
            grid=(cols // tile,),
            in_specs=[spec_of(h, slot) for h in range(2) for slot in range(n)]
            + [pl.BlockSpec((rank, tile), lambda j, ix: (0, j))]
            + [ANYWHERE] * len(events),
            out_specs=[
                pl.BlockSpec((tile, groups * rows), lambda j, ix: (j, 0)),
                pl.BlockSpec((groups * rows, rank), lambda j, ix: (0, 0)),
            ],
        ),
        out_shape=[
            jax.ShapeDtypeStruct((cols, groups * rows), jnp.bfloat16),
            jax.ShapeDtypeStruct((groups * rows, rank), jnp.float32),
        ],
        cost_estimate=pl.CostEstimate(
            flops=2 * groups * rows * cols * rank,
            bytes_accessed=4 * groups * rows * cols,
            transcendentals=groups * rows * cols,
        ),
        compiler_params=pltpu.CompilerParams(vmem_limit_bytes=14 << 20),
        name="slopes",
    )(index, *([pre] * groups), sketch_t, *events)


def expert_kernel(
    tile_f, tile_d, rows_ref, slope_ref, down_part_ref, sketch_ref, down_ref, up_ref, *refs
):
    keep_ref, give_ref, grad_buf = refs[-3:]
    hidden_cols, width = down_ref.shape
    half = keep_ref.shape[0]

    def first(j, carry):
        part = pl.ds(pl.multiple_of(j * tile_f, tile_f), tile_f)
        grad_hidden = lax.dot_general(
            down_ref[part, :], rows_ref[...], NT, preferred_element_type=jnp.float32
        )
        slope = slope_ref[part, :].astype(jnp.float32)
        grad_buf[part, :] = (grad_hidden * slope).astype(jnp.bfloat16)
        return carry

    lax.fori_loop(0, hidden_cols // tile_f, first, 0)

    up_part = jnp.dot(sketch_ref[...], grad_buf[...], preferred_element_type=jnp.float32).T
    vectors = jnp.concatenate([down_part_ref[...], up_part], axis=1)
    keep_ref[:, width:] = vectors[:half]
    give_ref[:, width:] = vectors[half:].astype(jnp.bfloat16)

    def second(j, carry):
        part = pl.ds(pl.multiple_of(j * tile_d, tile_d), tile_d)
        term = jnp.dot(up_ref[part, :], grad_buf[...], preferred_element_type=jnp.float32).T
        keep_ref[:, part] = term[:half]
        give_ref[:, part] = term[half:].astype(jnp.bfloat16)
        return carry

    lax.fori_loop(0, width // tile_d, second, 0)


def expert(rows, slope, down_part, sketch_t, down_local, up_local, *events):
    count, width = rows.shape
    hidden_cols = down_local.shape[0]
    rank = sketch_t.shape[0]
    wide = width + 2 * rank
    return pl.pallas_call(
        functools.partial(expert_kernel, tile_of(hidden_cols, 512), tile_of(width, 512)),
        in_specs=[RESIDENT] * 6 + [ANYWHERE] * len(events),
        out_specs=[RESIDENT] * 2,
        out_shape=[
            jax.ShapeDtypeStruct((count // 2, wide), jnp.float32),
            jax.ShapeDtypeStruct((count // 2, wide), jnp.bfloat16),
        ],
        scratch_shapes=[pltpu.VMEM((hidden_cols, count), jnp.bfloat16)],
        compiler_params=pltpu.CompilerParams(vmem_limit_bytes=14 << 20),
        cost_estimate=pl.CostEstimate(
            flops=4 * count * hidden_cols * width,
            bytes_accessed=4 * hidden_cols * width,
            transcendentals=0,
        ),
        name="expert",
    )(rows, slope, down_part, sketch_t, down_local, up_local, *events)


def per_device(
    cotangent,
    routes,
    gate_values,
    up_weight,
    down_weight,
    pre_activation,
    input_sketch,
    model_sketch,
    hidden_sketch,
    lengths,
):
    pieces = lax.axis_size("dp")
    sections = lax.axis_size("section")
    per_expert = pieces // EXPERTS
    place = lax.axis_index("dp")
    core = lax.axis_index("tensor")
    cot = cotangent[0]
    tok_dev, width = cot.shape
    half = tok_dev // 2
    rows = half // CHUNKS
    rank = model_sketch.shape[2]
    blocks = routes.shape[1]
    block_len = tok_dev // blocks
    sketch_local = hidden_sketch[0, 0]
    pre_all = pre_activation[0, 0]
    hidden_cols = pre_all.shape[2]
    pre_all = pre_all.reshape(pieces, 2, CHUNKS, rows, hidden_cols)

    def below(block):
        return lax.ppermute(block, "section", [(s, (s - 1) % sections) for s in range(sections)])

    cot_mine = lax.dynamic_slice_in_dim(cot, core * half, half, 0)
    cot_theirs = lax.dynamic_slice_in_dim(cot, (1 - core) * half, half, 0)
    order = sorted(range(1, pieces), key=lambda k: (bin(k).count("1"), -k))
    chunk_rows, marks = [], []
    for a in range(CHUNKS):
        part = slice(a * rows, (a + 1) * rows)
        first = cot_mine[part]
        if a > 0:
            first = held(first, marks[a - 1])
        mine, theirs = {0: first}, {0: cot_theirs[part]}
        for slot in order:
            low = slot & -slot
            mine[slot] = xored(mine[slot ^ low], "dp", low)
        marks.append(mine[order[0]])
        for level in range(1, pieces.bit_length()):
            slots = [k for k in order if bin(k).count("1") == level]
            traded = xored(jnp.concatenate([mine[k] for k in slots], axis=0), "tensor", 1)
            for at, slot in enumerate(slots):
                theirs[slot] = traded[at * rows : (at + 1) * rows]
        chunk_rows.append(
            jnp.concatenate(
                [mine[k] for k in range(pieces)] + [theirs[k] for k in range(pieces)], axis=0
            )
        )

    token_routes = jnp.broadcast_to(routes[0][:, None, :], (blocks, block_len, 2)).reshape(
        tok_dev, 2
    )
    half_routes = lax.dynamic_slice_in_dim(token_routes, core * half, half, 0)
    half_gates = lax.dynamic_slice_in_dim(gate_values[0], core * half, half, 0)
    slot_expert = (place ^ jnp.arange(pieces, dtype=jnp.int32)) // per_expert
    hits = half_routes[:, None, :] == slot_expert[None, :, None]
    weight = jnp.sum(jnp.where(hits, half_gates[:, None, :], 0.0), axis=2)

    sketch_t = sketch_local.T
    below_mine, vectors, events, done = [], [], (), ()
    for a in range(CHUNKS):
        slope, down_part = slopes(a, pre_all, sketch_t, place, core, *marks[:a])
        keep, give = expert(
            chunk_rows[a], slope, down_part, sketch_t, down_weight[0, 0], up_weight[0, 0], *events
        )
        own, sent = merged(keep, xored(give, "tensor", 1), rows, *done)
        events = (sent,)
        part = slice(a * rows, (a + 1) * rows)
        total = weight[part, :1] * own
        for slot in reversed(range(1, pieces)):
            back = xored(sent[(slot - 1) * rows : slot * rows], "dp", slot)
            total = total + weight[part, slot : slot + 1] * back.astype(jnp.float32)
        grad = (cot_mine[part].astype(jnp.float32) + total[:, :width]).astype(jnp.bfloat16)
        done = (grad,)
        below_mine.append(below(grad))
        vectors.append(total[:, width:])

    mine = jnp.concatenate(below_mine, axis=0)
    theirs = jnp.concatenate([xored(f, "tensor", 1) for f in below_mine], axis=0)
    handed = jnp.concatenate(
        [jnp.where(core == 0, mine, theirs), jnp.where(core == 0, theirs, mine)], axis=0
    )

    vec_mine = jnp.concatenate(vectors, axis=0)
    vec_theirs = xored(vec_mine, "tensor", 1)
    sketch_sum = jnp.concatenate(
        [jnp.where(core == 0, vec_mine, vec_theirs), jnp.where(core == 0, vec_theirs, vec_mine)],
        axis=0,
    )
    out_vec = jnp.dot(cot, model_sketch[0], preferred_element_type=jnp.float32)
    counts = lengths[0, 0]
    ends = jnp.cumsum(counts)
    starts = ends - counts
    position = jnp.arange(tok_dev, dtype=jnp.int32)
    member = ((position[None, :] >= starts[:, None]) & (position[None, :] < ends[:, None])).astype(
        jnp.float32
    )
    down_feat = jnp.einsum(
        "et,ta,tb->eab", member, out_vec, sketch_sum[:, :rank], precision=lax.Precision.HIGHEST
    )
    up_feat = jnp.einsum(
        "et,ta,tb->eab",
        member,
        sketch_sum[:, rank:],
        input_sketch[0],
        precision=lax.Precision.HIGHEST,
    )
    features = jnp.concatenate([down_feat, up_feat], axis=2)
    return (handed[None], features[None])


def solution(mesh):
    in_specs = (
        P("section", ("groups", "dp"), None),
        P("section", ("groups", "dp"), None),
        P("section", ("groups", "dp"), None),
        P("section", "dp", None, "tensor"),
        P("section", "dp", "tensor", None),
        P("section", ("groups", "dp"), None, None, "tensor"),
        P("section", ("groups", "dp"), None),
        P("section", None, None),
        P("section", "dp", "tensor", None),
        P("section", ("groups", "dp"), None),
    )
    out_specs = (P("section", ("groups", "dp"), None), P("section", ("groups", "dp"), None, None))
    return jax.shard_map(
        per_device, mesh=mesh, in_specs=in_specs, out_specs=out_specs, check_vma=False
    )
```

```python
import functools

import jax
import jax.numpy as jnp
from jax import lax
from jax.experimental import pallas as pl
from jax.experimental.pallas import tpu as pltpu
from jax.sharding import PartitionSpec as P

EXPERTS = 4
CHUNKS = 2
AHEAD = 2
NT = (((1,), (1,)), ((), ()))


def xored(block, axis, bits):
    n = lax.axis_size(axis)
    return lax.ppermute(block, axis, [(i, i ^ bits) for i in range(n)])


ANYWHERE = pl.BlockSpec(memory_space=pl.ANY)
RESIDENT = pl.BlockSpec(memory_space=pltpu.VMEM)


def held_kernel(block_ref, *refs):
    refs[-1][...] = block_ref[...]


def held(block, *events):
    return pl.pallas_call(
        held_kernel,
        in_specs=[RESIDENT] + [ANYWHERE] * len(events),
        out_specs=RESIDENT,
        out_shape=jax.ShapeDtypeStruct(block.shape, block.dtype),
        compiler_params=pltpu.CompilerParams(vmem_limit_bytes=1 << 20),
        name="held",
    )(block, *events)


def merge_kernel(keep_ref, came_ref, own_ref, *sent_refs):
    rows = own_ref.shape[0]
    own_ref[...] = keep_ref[:rows] + came_ref[:rows].astype(jnp.float32)
    for at, sent_ref in enumerate(sent_refs):
        part = slice((at + 1) * rows, (at + 2) * rows)
        total = keep_ref[part] + came_ref[part].astype(jnp.float32)
        sent_ref[...] = total.astype(jnp.bfloat16)


def merged(keep, came, rows):
    count, wide = keep.shape
    others = count // rows - 1
    return pl.pallas_call(
        merge_kernel,
        in_specs=[RESIDENT] * 2,
        out_specs=[RESIDENT] * (1 + others),
        out_shape=[jax.ShapeDtypeStruct((rows, wide), jnp.float32)]
        + [jax.ShapeDtypeStruct((rows, wide), jnp.bfloat16)] * others,
        compiler_params=pltpu.CompilerParams(vmem_limit_bytes=4 << 20),
        cost_estimate=pl.CostEstimate(
            flops=count * wide, bytes_accessed=8 * count * wide, transcendentals=0
        ),
        name="merge",
    )(keep, came)


def finish_kernel(slots, own_ref, cot_ref, weight_ref, *refs):
    grad_ref, vec_ref = refs[-2:]
    width = grad_ref.shape[1]
    total = weight_ref[:, :1] * own_ref[...]
    for slot in range(1, slots):
        total += weight_ref[:, slot : slot + 1] * refs[slot - 1][...].astype(jnp.float32)
    grad_ref[...] = (cot_ref[...].astype(jnp.float32) + total[:, :width]).astype(jnp.bfloat16)
    vec_ref[...] = total[:, width:]


def finished(own, cot, weight, backs, *events):
    rows, wide = own.shape
    width = cot.shape[1]
    return pl.pallas_call(
        functools.partial(finish_kernel, 1 + len(backs)),
        in_specs=[RESIDENT] * (3 + len(backs)) + [ANYWHERE] * len(events),
        out_specs=[RESIDENT] * 2,
        out_shape=[
            jax.ShapeDtypeStruct((rows, width), jnp.bfloat16),
            jax.ShapeDtypeStruct((rows, wide - width), jnp.float32),
        ],
        compiler_params=pltpu.CompilerParams(vmem_limit_bytes=4 << 20),
        cost_estimate=pl.CostEstimate(
            flops=8 * rows * wide, bytes_accessed=12 * rows * wide, transcendentals=0
        ),
        name="finish",
    )(own, cot, weight, *backs, *events)


def tile_of(size, most):
    best = 128
    for tile in range(128, most + 1, 128):
        if size % tile == 0:
            best = tile
    return best


def slope_kernel(groups, index_ref, *refs):
    del index_ref
    pre_refs, sketch_ref = refs[:groups], refs[groups]
    slope_ref, down_ref = refs[-2:]
    pre = jnp.concatenate([r[0, 0, 0] for r in pre_refs], axis=0).astype(jnp.float32)
    sig = 0.5 + 0.5 * jnp.tanh(0.5 * pre)
    hidden = pre * sig
    slope = sig + hidden * (1.0 - sig)
    slope_ref[...] = slope.T.astype(slope_ref.dtype)
    term = lax.dot_general(
        hidden.astype(jnp.bfloat16), sketch_ref[...], NT, preferred_element_type=jnp.float32
    )

    @pl.when(pl.program_id(0) == 0)
    def _():
        down_ref[...] = jnp.zeros_like(down_ref)

    down_ref[...] += term


def slopes(chunk, pre, sketch_t, place, core, *events):
    n, _, _, rows, cols = pre.shape
    rank = sketch_t.shape[0]
    groups = 2 * n
    tile = tile_of(cols, 896)
    index = jnp.stack([place, core]).astype(jnp.int32)

    def spec_of(h, slot):
        return pl.BlockSpec(
            (1, 1, 1, rows, tile), lambda j, ix: (ix[0] ^ slot, ix[1] ^ h, chunk, 0, j)
        )

    return pl.pallas_call(
        functools.partial(slope_kernel, groups),
        grid_spec=pltpu.PrefetchScalarGridSpec(
            num_scalar_prefetch=1,
            grid=(cols // tile,),
            in_specs=[spec_of(h, slot) for h in range(2) for slot in range(n)]
            + [pl.BlockSpec((rank, tile), lambda j, ix: (0, j))]
            + [ANYWHERE] * len(events),
            out_specs=[
                pl.BlockSpec((tile, groups * rows), lambda j, ix: (j, 0)),
                pl.BlockSpec((groups * rows, rank), lambda j, ix: (0, 0)),
            ],
        ),
        out_shape=[
            jax.ShapeDtypeStruct((cols, groups * rows), jnp.bfloat16),
            jax.ShapeDtypeStruct((groups * rows, rank), jnp.float32),
        ],
        cost_estimate=pl.CostEstimate(
            flops=2 * groups * rows * cols * rank,
            bytes_accessed=4 * groups * rows * cols,
            transcendentals=groups * rows * cols,
        ),
        compiler_params=pltpu.CompilerParams(vmem_limit_bytes=7 << 20),
        name="slopes",
    )(index, *([pre] * groups), sketch_t, *events)


def expert_kernel(
    tile_f, tile_d, rows_ref, slope_ref, down_part_ref, sketch_ref, down_hbm, up_hbm, *refs
):
    keep_ref, give_ref, rows_buf, grad_buf, down_buf, up_buf, down_sem, up_sem = refs[-8:]
    hidden_cols, width = down_buf.shape
    steps_f, steps_d = hidden_cols // tile_f, width // tile_d
    half = keep_ref.shape[0]

    def tile(j, size):
        return pl.ds(pl.multiple_of(j * size, size), size)

    def down_copy(j):
        part = tile(j, tile_f)
        return pltpu.make_async_copy(down_hbm.at[part], down_buf.at[part], down_sem.at[j])

    def up_copy(j):
        part = tile(j, tile_d)
        return pltpu.make_async_copy(up_hbm.at[part], up_buf.at[part], up_sem.at[j])

    for j in range(min(AHEAD, steps_f)):
        down_copy(j).start()
    rows_buf[...] = rows_ref[...].T

    def first(j, carry):
        down_copy(j).wait()

        @pl.when(j + AHEAD < steps_f)
        def _():
            down_copy(j + AHEAD).start()

        @pl.when(j + AHEAD >= steps_f)
        def _():
            up_copy(j + AHEAD - steps_f).start()

        part = tile(j, tile_f)
        grad_hidden = jnp.dot(
            down_buf[part, :], rows_buf[...], preferred_element_type=jnp.float32
        )
        slope = slope_ref[part, :].astype(jnp.float32)
        grad_buf[part, :] = (grad_hidden * slope).astype(jnp.bfloat16)
        return carry

    lax.fori_loop(0, steps_f, first, 0)

    up_part = jnp.dot(sketch_ref[...], grad_buf[...], preferred_element_type=jnp.float32).T
    vectors = jnp.concatenate([down_part_ref[...], up_part], axis=1)
    keep_ref[:, width:] = vectors[:half]
    give_ref[:, width:] = vectors[half:].astype(jnp.bfloat16)

    def second(j, carry):
        up_copy(j).wait()

        @pl.when(j + AHEAD < steps_d)
        def _():
            up_copy(j + AHEAD).start()

        part = tile(j, tile_d)
        term = jnp.dot(up_buf[part, :], grad_buf[...], preferred_element_type=jnp.float32).T
        keep_ref[:, part] = term[:half]
        give_ref[:, part] = term[half:].astype(jnp.bfloat16)
        return carry

    lax.fori_loop(0, steps_d, second, 0)


def expert(rows, slope, down_part, sketch_t, down_local, up_local, *events):
    count, width = rows.shape
    hidden_cols = down_local.shape[0]
    rank = sketch_t.shape[0]
    wide = width + 2 * rank
    tile_f, tile_d = tile_of(hidden_cols, 512), tile_of(width, 512)
    return pl.pallas_call(
        functools.partial(expert_kernel, tile_f, tile_d),
        in_specs=[RESIDENT] * 4 + [ANYWHERE] * (2 + len(events)),
        out_specs=[RESIDENT] * 2,
        out_shape=[
            jax.ShapeDtypeStruct((count // 2, wide), jnp.float32),
            jax.ShapeDtypeStruct((count // 2, wide), jnp.bfloat16),
        ],
        scratch_shapes=[
            pltpu.VMEM((width, count), jnp.bfloat16),
            pltpu.VMEM((hidden_cols, count), jnp.bfloat16),
            pltpu.VMEM((hidden_cols, width), jnp.bfloat16),
            pltpu.VMEM((width, hidden_cols), jnp.bfloat16),
            pltpu.SemaphoreType.DMA((hidden_cols // tile_f,)),
            pltpu.SemaphoreType.DMA((width // tile_d,)),
        ],
        compiler_params=pltpu.CompilerParams(vmem_limit_bytes=38 << 20),
        cost_estimate=pl.CostEstimate(
            flops=4 * count * hidden_cols * width,
            bytes_accessed=4 * hidden_cols * width,
            transcendentals=0,
        ),
        name="expert",
    )(rows, slope, down_part, sketch_t, down_local, up_local, *events)


def per_device(
    cotangent,
    routes,
    gate_values,
    up_weight,
    down_weight,
    pre_activation,
    input_sketch,
    model_sketch,
    hidden_sketch,
    lengths,
):
    pieces = lax.axis_size("dp")
    sections = lax.axis_size("section")
    per_expert = pieces // EXPERTS
    place = lax.axis_index("dp")
    core = lax.axis_index("tensor")
    cot = cotangent[0]
    tok_dev, width = cot.shape
    half = tok_dev // 2
    rows = half // CHUNKS
    rank = model_sketch.shape[2]
    blocks = routes.shape[1]
    block_len = tok_dev // blocks
    sketch_local = hidden_sketch[0, 0]
    pre_all = pre_activation[0, 0]
    hidden_cols = pre_all.shape[2]
    pre_all = pre_all.reshape(pieces, 2, CHUNKS, rows, hidden_cols)

    def below(block):
        return lax.ppermute(block, "section", [(s, (s - 1) % sections) for s in range(sections)])

    token_routes = jnp.broadcast_to(routes[0][:, None, :], (blocks, block_len, 2)).reshape(
        tok_dev, 2
    )
    half_routes = lax.dynamic_slice_in_dim(token_routes, core * half, half, 0)
    half_gates = lax.dynamic_slice_in_dim(gate_values[0], core * half, half, 0)
    slot_expert = (place ^ jnp.arange(pieces, dtype=jnp.int32)) // per_expert
    hits = half_routes[:, None, :] == slot_expert[None, :, None]
    weight = jnp.sum(jnp.where(hits, half_gates[:, None, :], 0.0), axis=2)

    sketch_t = sketch_local.T
    cot_mine = lax.dynamic_slice_in_dim(cot, core * half, half, 0)
    cot_theirs = lax.dynamic_slice_in_dim(cot, (1 - core) * half, half, 0)
    order = sorted(range(1, pieces), key=lambda k: (bin(k).count("1"), -k))
    mark, keep, sent, grad, passed = (), (), (), (), ()
    below_mine, vectors = [], []
    for a in range(CHUNKS):
        part = slice(a * rows, (a + 1) * rows)
        mine, theirs = {0: cot_mine[part]}, {0: cot_theirs[part]}
        if mark:
            mine[0] = held(mine[0], *mark)
        for slot in order:
            low = slot & -slot
            mine[slot] = xored(mine[slot ^ low], "dp", low)
        slope, down_part = slopes(a, pre_all, sketch_t, place, core, *mark)
        mark = (mine[order[0]],)
        for level in range(1, pieces.bit_length()):
            slots = [k for k in order if bin(k).count("1") == level]
            if level > 1 and keep:
                for k in slots:
                    mine[k] = held(mine[k], *keep)
            traded = xored(jnp.concatenate([mine[k] for k in slots], axis=0), "tensor", 1)
            for at, slot in enumerate(slots):
                theirs[slot] = traded[at * rows : (at + 1) * rows]
        rows_in = jnp.concatenate(
            [mine[k] for k in range(pieces)] + [theirs[k] for k in range(pieces)], axis=0
        )

        kept, give = expert(
            rows_in, slope, down_part, sketch_t, down_weight[0, 0], up_weight[0, 0], *sent
        )
        keep = (kept,)
        if grad:
            give = held(give, *backs)
        own, *sent = merged(kept, xored(give, "tensor", 1), rows)
        backs = [xored(out, "dp", slot + 1) for slot, out in enumerate(sent)]
        if grad:
            passed = (below(held(*grad, backs[0])),)
            below_mine.append(*passed)
        new, vec = finished(own, cot_mine[part], weight[part], backs, *passed)
        grad = (new,)
        vectors.append(vec)
    below_mine.append(below(*grad))

    mine = jnp.concatenate(below_mine, axis=0)
    theirs = jnp.concatenate([xored(f, "tensor", 1) for f in below_mine], axis=0)
    handed = jnp.concatenate(
        [jnp.where(core == 0, mine, theirs), jnp.where(core == 0, theirs, mine)], axis=0
    )

    vec_mine = jnp.concatenate(vectors, axis=0)
    vec_theirs = xored(vec_mine, "tensor", 1)
    sketch_sum = jnp.concatenate(
        [jnp.where(core == 0, vec_mine, vec_theirs), jnp.where(core == 0, vec_theirs, vec_mine)],
        axis=0,
    )
    out_vec = jnp.dot(cot, model_sketch[0], preferred_element_type=jnp.float32)
    counts = lengths[0, 0]
    upto = jnp.arange(counts.shape[0])
    ends = jnp.sum(jnp.where(upto[None, :] <= upto[:, None], counts[None, :], 0), axis=1)
    starts = ends - counts
    position = jnp.arange(tok_dev, dtype=jnp.int32)
    member = ((position[None, :] >= starts[:, None]) & (position[None, :] < ends[:, None])).astype(
        jnp.float32
    )
    down_feat = jnp.einsum(
        "et,ta,tb->eab", member, out_vec, sketch_sum[:, :rank], precision=lax.Precision.HIGHEST
    )
    up_feat = jnp.einsum(
        "et,ta,tb->eab",
        member,
        sketch_sum[:, rank:],
        input_sketch[0],
        precision=lax.Precision.HIGHEST,
    )
    features = jnp.concatenate([down_feat, up_feat], axis=2)
    return (handed[None], features[None])


def solution(mesh):
    in_specs = (
        P("section", ("groups", "dp"), None),
        P("section", ("groups", "dp"), None),
        P("section", ("groups", "dp"), None),
        P("section", "dp", None, "tensor"),
        P("section", "dp", "tensor", None),
        P("section", ("groups", "dp"), None, None, "tensor"),
        P("section", ("groups", "dp"), None),
        P("section", None, None),
        P("section", "dp", "tensor", None),
        P("section", ("groups", "dp"), None),
    )
    out_specs = (P("section", ("groups", "dp"), None), P("section", ("groups", "dp"), None, None))
    return jax.shard_map(
        per_device, mesh=mesh, in_specs=in_specs, out_specs=out_specs, check_vma=False
    )
```

```python
import functools

import jax
import jax.numpy as jnp
from jax import lax
from jax.experimental import pallas as pl
from jax.experimental.pallas import tpu as pltpu
from jax.sharding import PartitionSpec as P

EXPERTS = 4
CHUNKS = 2
AHEAD = 2
NT = (((1,), (1,)), ((), ()))


def xored(block, axis, bits):
    n = lax.axis_size(axis)
    return lax.ppermute(block, axis, [(i, i ^ bits) for i in range(n)])


ANYWHERE = pl.BlockSpec(memory_space=pl.ANY)
RESIDENT = pl.BlockSpec(memory_space=pltpu.VMEM)


def held_kernel(block_ref, *refs):
    refs[-1][...] = block_ref[...]


def held(block, *events):
    return pl.pallas_call(
        held_kernel,
        in_specs=[RESIDENT] + [ANYWHERE] * len(events),
        out_specs=RESIDENT,
        out_shape=jax.ShapeDtypeStruct(block.shape, block.dtype),
        compiler_params=pltpu.CompilerParams(vmem_limit_bytes=1 << 20),
        name="held",
    )(block, *events)


def merge_kernel(keep_ref, came_ref, own_ref, *sent_refs):
    rows = own_ref.shape[0]
    own_ref[...] = keep_ref[:rows] + came_ref[:rows].astype(jnp.float32)
    for at, sent_ref in enumerate(sent_refs):
        part = slice((at + 1) * rows, (at + 2) * rows)
        total = keep_ref[part] + came_ref[part].astype(jnp.float32)
        sent_ref[...] = total.astype(jnp.bfloat16)


def merged(keep, came, rows):
    count, wide = keep.shape
    others = count // rows - 1
    return pl.pallas_call(
        merge_kernel,
        in_specs=[RESIDENT] * 2,
        out_specs=[RESIDENT] * (1 + others),
        out_shape=[jax.ShapeDtypeStruct((rows, wide), jnp.float32)]
        + [jax.ShapeDtypeStruct((rows, wide), jnp.bfloat16)] * others,
        compiler_params=pltpu.CompilerParams(vmem_limit_bytes=4 << 20),
        cost_estimate=pl.CostEstimate(
            flops=count * wide, bytes_accessed=8 * count * wide, transcendentals=0
        ),
        name="merge",
    )(keep, came)


def finish_kernel(slots, own_ref, cot_ref, weight_ref, *refs):
    grad_ref, vec_ref = refs[-2:]
    width = grad_ref.shape[1]
    total = weight_ref[:, :1] * own_ref[...]
    for slot in range(1, slots):
        total += weight_ref[:, slot : slot + 1] * refs[slot - 1][...].astype(jnp.float32)
    grad_ref[...] = (cot_ref[...].astype(jnp.float32) + total[:, :width]).astype(jnp.bfloat16)
    vec_ref[...] = total[:, width:]


def finished(own, cot, weight, backs, *events):
    rows, wide = own.shape
    width = cot.shape[1]
    return pl.pallas_call(
        functools.partial(finish_kernel, 1 + len(backs)),
        in_specs=[RESIDENT] * (3 + len(backs)) + [ANYWHERE] * len(events),
        out_specs=[RESIDENT] * 2,
        out_shape=[
            jax.ShapeDtypeStruct((rows, width), jnp.bfloat16),
            jax.ShapeDtypeStruct((rows, wide - width), jnp.float32),
        ],
        compiler_params=pltpu.CompilerParams(vmem_limit_bytes=4 << 20),
        cost_estimate=pl.CostEstimate(
            flops=8 * rows * wide, bytes_accessed=12 * rows * wide, transcendentals=0
        ),
        name="finish",
    )(own, cot, weight, *backs, *events)


def tile_of(size, most):
    best = 128
    for tile in range(128, most + 1, 128):
        if size % tile == 0:
            best = tile
    return best


def slope_kernel(groups, index_ref, *refs):
    del index_ref
    pre_refs, sketch_ref = refs[:groups], refs[groups]
    slope_ref, down_ref = refs[-2:]
    pre = jnp.concatenate([r[0, 0, 0] for r in pre_refs], axis=0).astype(jnp.float32)
    sig = 0.5 + 0.5 * jnp.tanh(0.5 * pre)
    hidden = pre * sig
    slope = sig + hidden * (1.0 - sig)
    slope_ref[...] = slope.T.astype(slope_ref.dtype)
    term = lax.dot_general(
        hidden.astype(jnp.bfloat16), sketch_ref[...], NT, preferred_element_type=jnp.float32
    )

    @pl.when(pl.program_id(0) == 0)
    def _():
        down_ref[...] = jnp.zeros_like(down_ref)

    down_ref[...] += term


def slopes(chunk, pre, sketch_t, place, core, *events):
    n, _, _, rows, cols = pre.shape
    rank = sketch_t.shape[0]
    groups = 2 * n
    tile = tile_of(cols, 896)
    index = jnp.stack([place, core]).astype(jnp.int32)

    def spec_of(h, slot):
        return pl.BlockSpec(
            (1, 1, 1, rows, tile), lambda j, ix: (ix[0] ^ slot, ix[1] ^ h, chunk, 0, j)
        )

    return pl.pallas_call(
        functools.partial(slope_kernel, groups),
        grid_spec=pltpu.PrefetchScalarGridSpec(
            num_scalar_prefetch=1,
            grid=(cols // tile,),
            in_specs=[spec_of(h, slot) for h in range(2) for slot in range(n)]
            + [pl.BlockSpec((rank, tile), lambda j, ix: (0, j))]
            + [ANYWHERE] * len(events),
            out_specs=[
                pl.BlockSpec((tile, groups * rows), lambda j, ix: (j, 0)),
                pl.BlockSpec((groups * rows, rank), lambda j, ix: (0, 0)),
            ],
        ),
        out_shape=[
            jax.ShapeDtypeStruct((cols, groups * rows), jnp.bfloat16),
            jax.ShapeDtypeStruct((groups * rows, rank), jnp.float32),
        ],
        cost_estimate=pl.CostEstimate(
            flops=2 * groups * rows * cols * rank,
            bytes_accessed=4 * groups * rows * cols,
            transcendentals=groups * rows * cols,
        ),
        compiler_params=pltpu.CompilerParams(vmem_limit_bytes=7 << 20),
        name="slopes",
    )(index, *([pre] * groups), sketch_t, *events)


def expert_kernel(
    tile_f, tile_d, rows_ref, slope_ref, down_part_ref, sketch_ref, down_hbm, up_hbm, *refs
):
    keep_ref, give_ref, rows_buf, grad_buf, down_buf, up_buf, down_sem, up_sem = refs[-8:]
    hidden_cols, width = down_buf.shape
    steps_f, steps_d = hidden_cols // tile_f, width // tile_d
    half = keep_ref.shape[0]

    def tile(j, size):
        return pl.ds(pl.multiple_of(j * size, size), size)

    def down_copy(j):
        part = tile(j, tile_f)
        return pltpu.make_async_copy(down_hbm.at[part], down_buf.at[part], down_sem.at[j])

    def up_copy(j):
        part = tile(j, tile_d)
        return pltpu.make_async_copy(up_hbm.at[part], up_buf.at[part], up_sem.at[j])

    for j in range(min(AHEAD, steps_f)):
        down_copy(j).start()
    rows_buf[...] = rows_ref[...].T

    def first(j, carry):
        down_copy(j).wait()

        @pl.when(j + AHEAD < steps_f)
        def _():
            down_copy(j + AHEAD).start()

        @pl.when(j + AHEAD >= steps_f)
        def _():
            up_copy(j + AHEAD - steps_f).start()

        part = tile(j, tile_f)
        grad_hidden = jnp.dot(
            down_buf[part, :], rows_buf[...], preferred_element_type=jnp.float32
        )
        slope = slope_ref[part, :].astype(jnp.float32)
        grad_buf[part, :] = (grad_hidden * slope).astype(jnp.bfloat16)
        return carry

    lax.fori_loop(0, steps_f, first, 0)

    up_part = jnp.dot(sketch_ref[...], grad_buf[...], preferred_element_type=jnp.float32).T
    vectors = jnp.concatenate([down_part_ref[...], up_part], axis=1)
    keep_ref[:, width:] = vectors[:half]
    give_ref[:, width:] = vectors[half:].astype(jnp.bfloat16)

    def second(j, carry):
        up_copy(j).wait()

        @pl.when(j + AHEAD < steps_d)
        def _():
            up_copy(j + AHEAD).start()

        part = tile(j, tile_d)
        term = jnp.dot(up_buf[part, :], grad_buf[...], preferred_element_type=jnp.float32).T
        keep_ref[:, part] = term[:half]
        give_ref[:, part] = term[half:].astype(jnp.bfloat16)
        return carry

    lax.fori_loop(0, steps_d, second, 0)


def expert(rows, slope, down_part, sketch_t, down_local, up_local, *events):
    count, width = rows.shape
    hidden_cols = down_local.shape[0]
    rank = sketch_t.shape[0]
    wide = width + 2 * rank
    tile_f, tile_d = tile_of(hidden_cols, 896), tile_of(width, 512)
    return pl.pallas_call(
        functools.partial(expert_kernel, tile_f, tile_d),
        in_specs=[RESIDENT] * 4 + [ANYWHERE] * (2 + len(events)),
        out_specs=[RESIDENT] * 2,
        out_shape=[
            jax.ShapeDtypeStruct((count // 2, wide), jnp.float32),
            jax.ShapeDtypeStruct((count // 2, wide), jnp.bfloat16),
        ],
        scratch_shapes=[
            pltpu.VMEM((width, count), jnp.bfloat16),
            pltpu.VMEM((hidden_cols, count), jnp.bfloat16),
            pltpu.VMEM((hidden_cols, width), jnp.bfloat16),
            pltpu.VMEM((width, hidden_cols), jnp.bfloat16),
            pltpu.SemaphoreType.DMA((hidden_cols // tile_f,)),
            pltpu.SemaphoreType.DMA((width // tile_d,)),
        ],
        compiler_params=pltpu.CompilerParams(vmem_limit_bytes=38 << 20),
        cost_estimate=pl.CostEstimate(
            flops=4 * count * hidden_cols * width,
            bytes_accessed=4 * hidden_cols * width,
            transcendentals=0,
        ),
        name="expert",
    )(rows, slope, down_part, sketch_t, down_local, up_local, *events)


def per_device(
    cotangent,
    routes,
    gate_values,
    up_weight,
    down_weight,
    pre_activation,
    input_sketch,
    model_sketch,
    hidden_sketch,
    lengths,
):
    pieces = lax.axis_size("dp")
    sections = lax.axis_size("section")
    per_expert = pieces // EXPERTS
    place = lax.axis_index("dp")
    core = lax.axis_index("tensor")
    cot = cotangent[0]
    tok_dev, width = cot.shape
    half = tok_dev // 2
    rows = half // CHUNKS
    rank = model_sketch.shape[2]
    blocks = routes.shape[1]
    block_len = tok_dev // blocks
    sketch_local = hidden_sketch[0, 0]
    pre_all = pre_activation[0, 0]
    hidden_cols = pre_all.shape[2]
    pre_all = pre_all.reshape(pieces, 2, CHUNKS, rows, hidden_cols)

    def below(block):
        return lax.ppermute(block, "section", [(s, (s - 1) % sections) for s in range(sections)])

    token_routes = jnp.broadcast_to(routes[0][:, None, :], (blocks, block_len, 2)).reshape(
        tok_dev, 2
    )
    half_routes = lax.dynamic_slice_in_dim(token_routes, core * half, half, 0)
    half_gates = lax.dynamic_slice_in_dim(gate_values[0], core * half, half, 0)
    slot_expert = (place ^ jnp.arange(pieces, dtype=jnp.int32)) // per_expert
    hits = half_routes[:, None, :] == slot_expert[None, :, None]
    weight = jnp.sum(jnp.where(hits, half_gates[:, None, :], 0.0), axis=2)

    sketch_t = sketch_local.T
    cot_mine = lax.dynamic_slice_in_dim(cot, core * half, half, 0)
    cot_theirs = lax.dynamic_slice_in_dim(cot, (1 - core) * half, half, 0)
    order = sorted(range(1, pieces), reverse=True)
    mark, keep, sent, grad, passed = (), (), (), (), ()
    below_mine, vectors = [], []
    for a in range(CHUNKS):
        part = slice(a * rows, (a + 1) * rows)
        mine, theirs = {0: cot_mine[part]}, {0: cot_theirs[part]}
        if mark:
            mine[0] = held(mine[0], *mark)
        for slot in order:
            mine[slot] = xored(mine[0], "dp", slot)
        slope, down_part = slopes(a, pre_all, sketch_t, place, core)
        mark = (mine[1],)
        if keep:
            for slot in order:
                mine[slot] = held(mine[slot], *keep)
        traded = xored(jnp.concatenate([mine[slot] for slot in order], axis=0), "tensor", 1)
        for at, slot in enumerate(order):
            theirs[slot] = traded[at * rows : (at + 1) * rows]
        rows_in = jnp.concatenate(
            [mine[k] for k in range(pieces)] + [theirs[k] for k in range(pieces)], axis=0
        )

        kept, give = expert(
            rows_in, slope, down_part, sketch_t, down_weight[0, 0], up_weight[0, 0], *sent
        )
        keep = (kept,)
        if grad:
            give = held(give, *backs)
        own, *sent = merged(kept, xored(give, "tensor", 1), rows)
        backs = [xored(out, "dp", slot + 1) for slot, out in enumerate(sent)]
        if grad:
            passed = (below(held(*grad, backs[0])),)
            below_mine.append(*passed)
        new, vec = finished(own, cot_mine[part], weight[part], backs, *passed)
        grad = (new,)
        vectors.append(vec)
    below_mine.append(below(*grad))

    mine = jnp.concatenate(below_mine, axis=0)
    theirs = jnp.concatenate([xored(f, "tensor", 1) for f in below_mine], axis=0)
    handed = jnp.concatenate(
        [jnp.where(core == 0, mine, theirs), jnp.where(core == 0, theirs, mine)], axis=0
    )

    vec_mine = jnp.concatenate(vectors, axis=0)
    vec_theirs = xored(vec_mine, "tensor", 1)
    sketch_sum = jnp.concatenate(
        [jnp.where(core == 0, vec_mine, vec_theirs), jnp.where(core == 0, vec_theirs, vec_mine)],
        axis=0,
    )
    out_vec = jnp.dot(cot, model_sketch[0], preferred_element_type=jnp.float32)
    counts = lengths[0, 0]
    upto = jnp.arange(counts.shape[0])
    ends = jnp.sum(jnp.where(upto[None, :] <= upto[:, None], counts[None, :], 0), axis=1)
    starts = ends - counts
    position = jnp.arange(tok_dev, dtype=jnp.int32)
    member = ((position[None, :] >= starts[:, None]) & (position[None, :] < ends[:, None])).astype(
        jnp.float32
    )
    down_feat = jnp.einsum(
        "et,ta,tb->eab", member, out_vec, sketch_sum[:, :rank], precision=lax.Precision.HIGHEST
    )
    up_feat = jnp.einsum(
        "et,ta,tb->eab",
        member,
        sketch_sum[:, rank:],
        input_sketch[0],
        precision=lax.Precision.HIGHEST,
    )
    features = jnp.concatenate([down_feat, up_feat], axis=2)
    return (handed[None], features[None])


def solution(mesh):
    in_specs = (
        P("section", ("groups", "dp"), None),
        P("section", ("groups", "dp"), None),
        P("section", ("groups", "dp"), None),
        P("section", "dp", None, "tensor"),
        P("section", "dp", "tensor", None),
        P("section", ("groups", "dp"), None, None, "tensor"),
        P("section", ("groups", "dp"), None),
        P("section", None, None),
        P("section", "dp", "tensor", None),
        P("section", ("groups", "dp"), None),
    )
    out_specs = (P("section", ("groups", "dp"), None), P("section", ("groups", "dp"), None, None))
    return jax.shard_map(
        per_device, mesh=mesh, in_specs=in_specs, out_specs=out_specs, check_vma=False
    )
```

```python
import functools

import jax
import jax.numpy as jnp
from jax import lax
from jax.experimental import pallas as pl
from jax.experimental.pallas import tpu as pltpu
from jax.sharding import PartitionSpec as P

EXPERTS = 4
CHUNKS = 2
NT = (((1,), (1,)), ((), ()))


def xored(block, axis, bits):
    n = lax.axis_size(axis)
    return lax.ppermute(block, axis, [(i, i ^ bits) for i in range(n)])


ANYWHERE = pl.BlockSpec(memory_space=pl.ANY)
RESIDENT = pl.BlockSpec(memory_space=pltpu.VMEM)


def held_kernel(block_ref, *refs):
    refs[-1][...] = block_ref[...]


def held(block, *events):
    return pl.pallas_call(
        held_kernel,
        in_specs=[RESIDENT] + [ANYWHERE] * len(events),
        out_specs=RESIDENT,
        out_shape=jax.ShapeDtypeStruct(block.shape, block.dtype),
        compiler_params=pltpu.CompilerParams(vmem_limit_bytes=1 << 20),
        name="held",
    )(block, *events)


def merge_kernel(keep_ref, came_ref, own_ref, *sent_refs):
    rows = own_ref.shape[0]
    own_ref[...] = keep_ref[:rows] + came_ref[:rows].astype(jnp.float32)
    for at, sent_ref in enumerate(sent_refs):
        part = slice((at + 1) * rows, (at + 2) * rows)
        total = keep_ref[part] + came_ref[part].astype(jnp.float32)
        sent_ref[...] = total.astype(jnp.bfloat16)


def merged(keep, came, rows):
    count, wide = keep.shape
    others = count // rows - 1
    return pl.pallas_call(
        merge_kernel,
        in_specs=[RESIDENT] * 2,
        out_specs=[RESIDENT] * (1 + others),
        out_shape=[jax.ShapeDtypeStruct((rows, wide), jnp.float32)]
        + [jax.ShapeDtypeStruct((rows, wide), jnp.bfloat16)] * others,
        compiler_params=pltpu.CompilerParams(vmem_limit_bytes=4 << 20),
        cost_estimate=pl.CostEstimate(
            flops=count * wide, bytes_accessed=8 * count * wide, transcendentals=0
        ),
        name="merge",
    )(keep, came)


def finish_kernel(slots, own_ref, cot_ref, weight_ref, *refs):
    grad_ref, vec_ref = refs[-2:]
    width = grad_ref.shape[1]
    total = weight_ref[:, :1] * own_ref[...]
    for slot in range(1, slots):
        total += weight_ref[:, slot : slot + 1] * refs[slot - 1][...].astype(jnp.float32)
    grad_ref[...] = (cot_ref[...].astype(jnp.float32) + total[:, :width]).astype(jnp.bfloat16)
    vec_ref[...] = total[:, width:]


def finished(own, cot, weight, backs, *events):
    rows, wide = own.shape
    width = cot.shape[1]
    return pl.pallas_call(
        functools.partial(finish_kernel, 1 + len(backs)),
        in_specs=[RESIDENT] * (3 + len(backs)) + [ANYWHERE] * len(events),
        out_specs=[RESIDENT] * 2,
        out_shape=[
            jax.ShapeDtypeStruct((rows, width), jnp.bfloat16),
            jax.ShapeDtypeStruct((rows, wide - width), jnp.float32),
        ],
        compiler_params=pltpu.CompilerParams(vmem_limit_bytes=4 << 20),
        cost_estimate=pl.CostEstimate(
            flops=8 * rows * wide, bytes_accessed=12 * rows * wide, transcendentals=0
        ),
        name="finish",
    )(own, cot, weight, *backs, *events)


def tile_of(size, most):
    best = 128
    for tile in range(128, most + 1, 128):
        if size % tile == 0:
            best = tile
    return best


def slope_kernel(groups, index_ref, *refs):
    del index_ref
    pre_refs, sketch_ref = refs[:groups], refs[groups]
    slope_ref, down_ref = refs[-2:]
    pre = jnp.concatenate([r[0, 0, 0] for r in pre_refs], axis=0).astype(jnp.float32)
    sig = 0.5 + 0.5 * jnp.tanh(0.5 * pre)
    hidden = pre * sig
    slope = sig + hidden * (1.0 - sig)
    slope_ref[0] = slope.T.astype(slope_ref.dtype)
    term = lax.dot_general(
        hidden.astype(jnp.bfloat16), sketch_ref[...], NT, preferred_element_type=jnp.float32
    )

    @pl.when(pl.program_id(1) == 0)
    def _():
        down_ref[...] = jnp.zeros_like(down_ref)

    down_ref[0] += term


def slopes(pre, sketch_t, place, core):
    n, _, chunks, rows, cols = pre.shape
    rank = sketch_t.shape[0]
    groups = 2 * n
    tile = tile_of(cols, 896)
    index = jnp.stack([place, core]).astype(jnp.int32)

    def spec_of(h, slot):
        return pl.BlockSpec(
            (1, 1, 1, rows, tile), lambda a, j, ix: (ix[0] ^ slot, ix[1] ^ h, a, 0, j)
        )

    return pl.pallas_call(
        functools.partial(slope_kernel, groups),
        grid_spec=pltpu.PrefetchScalarGridSpec(
            num_scalar_prefetch=1,
            grid=(chunks, cols // tile),
            in_specs=[spec_of(h, slot) for h in range(2) for slot in range(n)]
            + [pl.BlockSpec((rank, tile), lambda a, j, ix: (0, j))],
            out_specs=[
                pl.BlockSpec((1, tile, groups * rows), lambda a, j, ix: (a, j, 0)),
                pl.BlockSpec((1, groups * rows, rank), lambda a, j, ix: (a, 0, 0)),
            ],
        ),
        out_shape=[
            jax.ShapeDtypeStruct((chunks, cols, groups * rows), jnp.bfloat16),
            jax.ShapeDtypeStruct((chunks, groups * rows, rank), jnp.float32),
        ],
        cost_estimate=pl.CostEstimate(
            flops=2 * chunks * groups * rows * cols * rank,
            bytes_accessed=4 * chunks * groups * rows * cols,
            transcendentals=chunks * groups * rows * cols,
        ),
        compiler_params=pltpu.CompilerParams(vmem_limit_bytes=7 << 20),
        name="slopes",
    )(index, *([pre] * groups), sketch_t)


def expert_kernel(
    tile_f, tile_d, rows_ref, slope_ref, down_part_ref, sketch_ref, down_ref, up_ref, *refs
):
    keep_ref, give_ref, rows_buf, grad_buf = refs[-4:]
    hidden_cols, width = down_ref.shape
    half = keep_ref.shape[0]
    rows_buf[...] = rows_ref[...].T

    def tile(j, size):
        return pl.ds(pl.multiple_of(j * size, size), size)

    def first(j, carry):
        part = tile(j, tile_f)
        grad_hidden = jnp.dot(
            down_ref[part, :], rows_buf[...], preferred_element_type=jnp.float32
        )
        slope = slope_ref[0, part, :].astype(jnp.float32)
        grad_buf[part, :] = (grad_hidden * slope).astype(jnp.bfloat16)
        return carry

    lax.fori_loop(0, hidden_cols // tile_f, first, 0)

    up_part = jnp.dot(sketch_ref[...], grad_buf[...], preferred_element_type=jnp.float32).T
    vectors = jnp.concatenate([down_part_ref[0], up_part], axis=1)
    keep_ref[:, width:] = vectors[:half]
    give_ref[:, width:] = vectors[half:].astype(jnp.bfloat16)

    def second(j, carry):
        part = tile(j, tile_d)
        term = jnp.dot(up_ref[part, :], grad_buf[...], preferred_element_type=jnp.float32).T
        keep_ref[:, part] = term[:half]
        give_ref[:, part] = term[half:].astype(jnp.bfloat16)
        return carry

    lax.fori_loop(0, width // tile_d, second, 0)


def expert(chunk, rows, slope, down_part, sketch_t, down_local, up_local, *events):
    count, width = rows.shape
    hidden_cols = down_local.shape[0]
    rank = sketch_t.shape[0]
    wide = width + 2 * rank
    return pl.pallas_call(
        functools.partial(expert_kernel, tile_of(hidden_cols, 1792), tile_of(width, 1024)),
        grid=(1,),
        in_specs=[
            RESIDENT,
            pl.BlockSpec((1, hidden_cols, count), lambda i: (chunk, 0, 0)),
            pl.BlockSpec((1, count, rank), lambda i: (chunk, 0, 0)),
        ]
        + [RESIDENT] * 3
        + [ANYWHERE] * len(events),
        out_specs=[RESIDENT] * 2,
        out_shape=[
            jax.ShapeDtypeStruct((count // 2, wide), jnp.float32),
            jax.ShapeDtypeStruct((count // 2, wide), jnp.bfloat16),
        ],
        scratch_shapes=[
            pltpu.VMEM((width, count), jnp.bfloat16),
            pltpu.VMEM((hidden_cols, count), jnp.bfloat16),
        ],
        compiler_params=pltpu.CompilerParams(vmem_limit_bytes=12 << 20),
        cost_estimate=pl.CostEstimate(
            flops=4 * count * hidden_cols * width,
            bytes_accessed=4 * hidden_cols * width,
            transcendentals=0,
        ),
        name="expert",
    )(rows, slope, down_part, sketch_t, down_local, up_local, *events)


def per_device(
    cotangent,
    routes,
    gate_values,
    up_weight,
    down_weight,
    pre_activation,
    input_sketch,
    model_sketch,
    hidden_sketch,
    lengths,
):
    pieces = lax.axis_size("dp")
    sections = lax.axis_size("section")
    per_expert = pieces // EXPERTS
    place = lax.axis_index("dp")
    core = lax.axis_index("tensor")
    cot = cotangent[0]
    tok_dev, width = cot.shape
    half = tok_dev // 2
    rows = half // CHUNKS
    rank = model_sketch.shape[2]
    blocks = routes.shape[1]
    block_len = tok_dev // blocks
    sketch_local = hidden_sketch[0, 0]
    pre_all = pre_activation[0, 0]
    hidden_cols = pre_all.shape[2]
    pre_all = pre_all.reshape(pieces, 2, CHUNKS, rows, hidden_cols)

    def below(block):
        return lax.ppermute(block, "section", [(s, (s - 1) % sections) for s in range(sections)])

    token_routes = jnp.broadcast_to(routes[0][:, None, :], (blocks, block_len, 2)).reshape(
        tok_dev, 2
    )
    half_routes = lax.dynamic_slice_in_dim(token_routes, core * half, half, 0)
    half_gates = lax.dynamic_slice_in_dim(gate_values[0], core * half, half, 0)
    slot_expert = (place ^ jnp.arange(pieces, dtype=jnp.int32)) // per_expert
    hits = half_routes[:, None, :] == slot_expert[None, :, None]
    weight = jnp.sum(jnp.where(hits, half_gates[:, None, :], 0.0), axis=2)

    sketch_t = sketch_local.T
    cot_mine = lax.dynamic_slice_in_dim(cot, core * half, half, 0)
    cot_theirs = lax.dynamic_slice_in_dim(cot, (1 - core) * half, half, 0)
    order = sorted(range(1, pieces), reverse=True)
    slope, down_part = slopes(pre_all, sketch_t, place, core)
    mark, keep, sent, grad, passed = (), (), (), (), ()
    below_mine, vectors = [], []
    for a in range(CHUNKS):
        part = slice(a * rows, (a + 1) * rows)
        mine, theirs = {0: cot_mine[part]}, {0: cot_theirs[part]}
        if mark:
            mine[0] = held(mine[0], *mark)
        for slot in order:
            mine[slot] = xored(mine[0], "dp", slot)
        mark = (mine[1],)
        if keep:
            for slot in order:
                mine[slot] = held(mine[slot], *keep)
        traded = xored(jnp.concatenate([mine[slot] for slot in order], axis=0), "tensor", 1)
        for at, slot in enumerate(order):
            theirs[slot] = traded[at * rows : (at + 1) * rows]
        rows_in = jnp.concatenate(
            [mine[k] for k in range(pieces)] + [theirs[k] for k in range(pieces)], axis=0
        )

        kept, give = expert(
            a, rows_in, slope, down_part, sketch_t, down_weight[0, 0], up_weight[0, 0], *sent
        )
        keep = (kept,)
        if grad:
            give = held(give, *backs)
        own, *sent = merged(kept, xored(give, "tensor", 1), rows)
        backs = [xored(out, "dp", slot + 1) for slot, out in enumerate(sent)]
        if grad:
            passed = (below(held(*grad, backs[0])),)
            below_mine.append(*passed)
        new, vec = finished(own, cot_mine[part], weight[part], backs, *passed)
        grad = (new,)
        vectors.append(vec)
    below_mine.append(below(*grad))

    mine = jnp.concatenate(below_mine, axis=0)
    theirs = jnp.concatenate([xored(f, "tensor", 1) for f in below_mine], axis=0)
    handed = jnp.concatenate(
        [jnp.where(core == 0, mine, theirs), jnp.where(core == 0, theirs, mine)], axis=0
    )

    vec_mine = jnp.concatenate(vectors, axis=0)
    vec_theirs = xored(vec_mine, "tensor", 1)
    sketch_sum = jnp.concatenate(
        [jnp.where(core == 0, vec_mine, vec_theirs), jnp.where(core == 0, vec_theirs, vec_mine)],
        axis=0,
    )
    out_vec = jnp.dot(cot, model_sketch[0], preferred_element_type=jnp.float32)
    counts = lengths[0, 0]
    upto = jnp.arange(counts.shape[0])
    ends = jnp.sum(jnp.where(upto[None, :] <= upto[:, None], counts[None, :], 0), axis=1)
    starts = ends - counts
    position = jnp.arange(tok_dev, dtype=jnp.int32)
    member = ((position[None, :] >= starts[:, None]) & (position[None, :] < ends[:, None])).astype(
        jnp.float32
    )
    down_feat = jnp.einsum(
        "et,ta,tb->eab", member, out_vec, sketch_sum[:, :rank], precision=lax.Precision.HIGHEST
    )
    up_feat = jnp.einsum(
        "et,ta,tb->eab",
        member,
        sketch_sum[:, rank:],
        input_sketch[0],
        precision=lax.Precision.HIGHEST,
    )
    features = jnp.concatenate([down_feat, up_feat], axis=2)
    return (handed[None], features[None])


def solution(mesh):
    in_specs = (
        P("section", ("groups", "dp"), None),
        P("section", ("groups", "dp"), None),
        P("section", ("groups", "dp"), None),
        P("section", "dp", None, "tensor"),
        P("section", "dp", "tensor", None),
        P("section", ("groups", "dp"), None, None, "tensor"),
        P("section", ("groups", "dp"), None),
        P("section", None, None),
        P("section", "dp", "tensor", None),
        P("section", ("groups", "dp"), None),
    )
    out_specs = (P("section", ("groups", "dp"), None), P("section", ("groups", "dp"), None, None))
    return jax.shard_map(
        per_device, mesh=mesh, in_specs=in_specs, out_specs=out_specs, check_vma=False
    )
```

```python
import functools

import jax
import jax.numpy as jnp
from jax import lax
from jax.experimental import pallas as pl
from jax.experimental.pallas import tpu as pltpu
from jax.sharding import PartitionSpec as P

EXPERTS = 4
CHUNKS = 2
NT = (((1,), (1,)), ((), ()))


def xored(block, axis, bits):
    n = lax.axis_size(axis)
    return lax.ppermute(block, axis, [(i, i ^ bits) for i in range(n)])


ANYWHERE = pl.BlockSpec(memory_space=pl.ANY)
RESIDENT = pl.BlockSpec(memory_space=pltpu.VMEM)


def held_kernel(block_ref, *refs):
    refs[-1][...] = block_ref[...]


def held(block, *events):
    return pl.pallas_call(
        held_kernel,
        in_specs=[RESIDENT] + [ANYWHERE] * len(events),
        out_specs=RESIDENT,
        out_shape=jax.ShapeDtypeStruct(block.shape, block.dtype),
        compiler_params=pltpu.CompilerParams(vmem_limit_bytes=1 << 20),
        name="held",
    )(block, *events)


def merge_kernel(keep_ref, came_ref, own_ref, *sent_refs):
    rows = own_ref.shape[0]
    own_ref[...] = keep_ref[:rows] + came_ref[:rows].astype(jnp.float32)
    for at, sent_ref in enumerate(sent_refs):
        part = slice((at + 1) * rows, (at + 2) * rows)
        total = keep_ref[part] + came_ref[part].astype(jnp.float32)
        sent_ref[...] = total.astype(jnp.bfloat16)


def merged(keep, came, rows):
    count, wide = keep.shape
    others = count // rows - 1
    return pl.pallas_call(
        merge_kernel,
        in_specs=[RESIDENT] * 2,
        out_specs=[RESIDENT] * (1 + others),
        out_shape=[jax.ShapeDtypeStruct((rows, wide), jnp.float32)]
        + [jax.ShapeDtypeStruct((rows, wide), jnp.bfloat16)] * others,
        compiler_params=pltpu.CompilerParams(vmem_limit_bytes=4 << 20),
        cost_estimate=pl.CostEstimate(
            flops=count * wide, bytes_accessed=8 * count * wide, transcendentals=0
        ),
        name="merge",
    )(keep, came)


def finish_kernel(slots, own_ref, cot_ref, weight_ref, *refs):
    grad_ref, vec_ref = refs[-2:]
    width = grad_ref.shape[1]
    total = weight_ref[:, :1] * own_ref[...]
    for slot in range(1, slots):
        total += weight_ref[:, slot : slot + 1] * refs[slot - 1][...].astype(jnp.float32)
    grad_ref[...] = (cot_ref[...].astype(jnp.float32) + total[:, :width]).astype(jnp.bfloat16)
    vec_ref[...] = total[:, width:]


def finished(own, cot, weight, backs, *events):
    rows, wide = own.shape
    width = cot.shape[1]
    return pl.pallas_call(
        functools.partial(finish_kernel, 1 + len(backs)),
        in_specs=[RESIDENT] * (3 + len(backs)) + [ANYWHERE] * len(events),
        out_specs=[RESIDENT] * 2,
        out_shape=[
            jax.ShapeDtypeStruct((rows, width), jnp.bfloat16),
            jax.ShapeDtypeStruct((rows, wide - width), jnp.float32),
        ],
        compiler_params=pltpu.CompilerParams(vmem_limit_bytes=4 << 20),
        cost_estimate=pl.CostEstimate(
            flops=8 * rows * wide, bytes_accessed=12 * rows * wide, transcendentals=0
        ),
        name="finish",
    )(own, cot, weight, *backs, *events)


def tile_of(size, most):
    best = 128
    for tile in range(128, most + 1, 128):
        if size % tile == 0:
            best = tile
    return best


def slope_kernel(groups, index_ref, *refs):
    del index_ref
    pre_refs, sketch_ref = refs[:groups], refs[groups]
    slope_ref, down_ref = refs[-2:]
    pre = jnp.concatenate([r[0, 0, 0] for r in pre_refs], axis=0).astype(jnp.float32)
    sig = 0.5 + 0.5 * jnp.tanh(0.5 * pre)
    hidden = pre * sig
    slope = sig + hidden * (1.0 - sig)
    slope_ref[0] = slope.T.astype(slope_ref.dtype)
    term = lax.dot_general(
        hidden.astype(jnp.bfloat16), sketch_ref[...], NT, preferred_element_type=jnp.float32
    )

    @pl.when(pl.program_id(1) == 0)
    def _():
        down_ref[...] = jnp.zeros_like(down_ref)

    down_ref[0] += term


def slopes(pre, sketch_t, place, core):
    n, _, chunks, rows, cols = pre.shape
    rank = sketch_t.shape[0]
    groups = 2 * n
    tile = tile_of(cols, 896)
    index = jnp.stack([place, core]).astype(jnp.int32)

    def spec_of(h, slot):
        return pl.BlockSpec(
            (1, 1, 1, rows, tile), lambda a, j, ix: (ix[0] ^ slot, ix[1] ^ h, a, 0, j)
        )

    return pl.pallas_call(
        functools.partial(slope_kernel, groups),
        grid_spec=pltpu.PrefetchScalarGridSpec(
            num_scalar_prefetch=1,
            grid=(chunks, cols // tile),
            in_specs=[spec_of(h, slot) for h in range(2) for slot in range(n)]
            + [pl.BlockSpec((rank, tile), lambda a, j, ix: (0, j))],
            out_specs=[
                pl.BlockSpec((1, tile, groups * rows), lambda a, j, ix: (a, j, 0)),
                pl.BlockSpec((1, groups * rows, rank), lambda a, j, ix: (a, 0, 0)),
            ],
        ),
        out_shape=[
            jax.ShapeDtypeStruct((chunks, cols, groups * rows), jnp.bfloat16),
            jax.ShapeDtypeStruct((chunks, groups * rows, rank), jnp.float32),
        ],
        cost_estimate=pl.CostEstimate(
            flops=2 * chunks * groups * rows * cols * rank,
            bytes_accessed=4 * chunks * groups * rows * cols,
            transcendentals=chunks * groups * rows * cols,
        ),
        compiler_params=pltpu.CompilerParams(vmem_limit_bytes=7 << 20),
        name="slopes",
    )(index, *([pre] * groups), sketch_t)


def expert_kernel(
    tile_f, tile_d, rows_ref, slope_ref, down_part_ref, sketch_ref, down_ref, up_hbm, *refs
):
    keep_ref, give_ref, rows_buf, grad_buf, up_buf, up_sem = refs[-6:]
    hidden_cols, width = down_ref.shape
    steps_f, steps_d = hidden_cols // tile_f, width // tile_d
    half = keep_ref.shape[0]

    def tile(j, size):
        return pl.ds(pl.multiple_of(j * size, size), size)

    def up_copy(j):
        part = tile(j, tile_d)
        return pltpu.make_async_copy(up_hbm.at[part], up_buf.at[part], up_sem.at[j])

    for j in range(steps_d):
        if j == 0 or j > steps_f:
            up_copy(j).start()
    rows_buf[...] = rows_ref[...].T

    def first(j, carry):
        @pl.when(j + 1 < steps_d)
        def _():
            up_copy(j + 1).start()

        part = tile(j, tile_f)
        grad_hidden = jnp.dot(
            down_ref[part, :], rows_buf[...], preferred_element_type=jnp.float32
        )
        slope = slope_ref[0, part, :].astype(jnp.float32)
        grad_buf[part, :] = (grad_hidden * slope).astype(jnp.bfloat16)
        return carry

    lax.fori_loop(0, steps_f, first, 0)

    up_part = jnp.dot(sketch_ref[...], grad_buf[...], preferred_element_type=jnp.float32).T
    vectors = jnp.concatenate([down_part_ref[0], up_part], axis=1)
    keep_ref[:, width:] = vectors[:half]
    give_ref[:, width:] = vectors[half:].astype(jnp.bfloat16)

    def second(j, carry):
        up_copy(j).wait()
        part = tile(j, tile_d)
        term = jnp.dot(up_buf[part, :], grad_buf[...], preferred_element_type=jnp.float32).T
        keep_ref[:, part] = term[:half]
        give_ref[:, part] = term[half:].astype(jnp.bfloat16)
        return carry

    lax.fori_loop(0, steps_d, second, 0)


def expert(chunk, rows, slope, down_part, sketch_t, down_local, up_local, *events):
    count, width = rows.shape
    hidden_cols = down_local.shape[0]
    rank = sketch_t.shape[0]
    wide = width + 2 * rank
    tile_f, tile_d = tile_of(hidden_cols, 1792), tile_of(width, 1024)
    return pl.pallas_call(
        functools.partial(expert_kernel, tile_f, tile_d),
        grid=(1,),
        in_specs=[
            RESIDENT,
            pl.BlockSpec((1, hidden_cols, count), lambda i: (chunk, 0, 0)),
            pl.BlockSpec((1, count, rank), lambda i: (chunk, 0, 0)),
        ]
        + [RESIDENT] * 2
        + [pl.BlockSpec(memory_space=pltpu.HBM)]
        + [ANYWHERE] * len(events),
        out_specs=[RESIDENT] * 2,
        out_shape=[
            jax.ShapeDtypeStruct((count // 2, wide), jnp.float32),
            jax.ShapeDtypeStruct((count // 2, wide), jnp.bfloat16),
        ],
        scratch_shapes=[
            pltpu.VMEM((width, count), jnp.bfloat16),
            pltpu.VMEM((hidden_cols, count), jnp.bfloat16),
            pltpu.VMEM((width, hidden_cols), jnp.bfloat16),
            pltpu.SemaphoreType.DMA((width // tile_d,)),
        ],
        compiler_params=pltpu.CompilerParams(vmem_limit_bytes=26 << 20),
        cost_estimate=pl.CostEstimate(
            flops=4 * count * hidden_cols * width,
            bytes_accessed=4 * hidden_cols * width,
            transcendentals=0,
        ),
        name="expert",
    )(rows, slope, down_part, sketch_t, down_local, up_local, *events)


def per_device(
    cotangent,
    routes,
    gate_values,
    up_weight,
    down_weight,
    pre_activation,
    input_sketch,
    model_sketch,
    hidden_sketch,
    lengths,
):
    pieces = lax.axis_size("dp")
    sections = lax.axis_size("section")
    per_expert = pieces // EXPERTS
    place = lax.axis_index("dp")
    core = lax.axis_index("tensor")
    cot = cotangent[0]
    tok_dev, width = cot.shape
    half = tok_dev // 2
    rows = half // CHUNKS
    rank = model_sketch.shape[2]
    blocks = routes.shape[1]
    block_len = tok_dev // blocks
    sketch_local = hidden_sketch[0, 0]
    pre_all = pre_activation[0, 0]
    hidden_cols = pre_all.shape[2]
    pre_all = pre_all.reshape(pieces, 2, CHUNKS, rows, hidden_cols)

    def below(block):
        return lax.ppermute(block, "section", [(s, (s - 1) % sections) for s in range(sections)])

    token_routes = jnp.broadcast_to(routes[0][:, None, :], (blocks, block_len, 2)).reshape(
        tok_dev, 2
    )
    half_routes = lax.dynamic_slice_in_dim(token_routes, core * half, half, 0)
    half_gates = lax.dynamic_slice_in_dim(gate_values[0], core * half, half, 0)
    slot_expert = (place ^ jnp.arange(pieces, dtype=jnp.int32)) // per_expert
    hits = half_routes[:, None, :] == slot_expert[None, :, None]
    weight = jnp.sum(jnp.where(hits, half_gates[:, None, :], 0.0), axis=2)

    sketch_t = sketch_local.T
    cot_mine = lax.dynamic_slice_in_dim(cot, core * half, half, 0)
    cot_theirs = lax.dynamic_slice_in_dim(cot, (1 - core) * half, half, 0)
    order = sorted(range(1, pieces), reverse=True)
    slope, down_part = slopes(pre_all, sketch_t, place, core)
    mark, keep, sent, grad, passed = (), (), (), (), ()
    below_mine, vectors = [], []
    for a in range(CHUNKS):
        part = slice(a * rows, (a + 1) * rows)
        mine, theirs = {0: cot_mine[part]}, {0: cot_theirs[part]}
        if mark:
            mine[0] = held(mine[0], *mark)
        for slot in order:
            mine[slot] = xored(mine[0], "dp", slot)
        mark = (mine[1],)
        if keep:
            for slot in order:
                mine[slot] = held(mine[slot], *keep)
        traded = xored(jnp.concatenate([mine[slot] for slot in order], axis=0), "tensor", 1)
        for at, slot in enumerate(order):
            theirs[slot] = traded[at * rows : (at + 1) * rows]
        rows_in = jnp.concatenate(
            [mine[k] for k in range(pieces)] + [theirs[k] for k in range(pieces)], axis=0
        )

        kept, give = expert(
            a, rows_in, slope, down_part, sketch_t, down_weight[0, 0], up_weight[0, 0], *sent
        )
        keep = (kept,)
        if grad:
            give = held(give, *backs)
        own, *sent = merged(kept, xored(give, "tensor", 1), rows)
        backs = [xored(out, "dp", slot + 1) for slot, out in enumerate(sent)]
        if grad:
            passed = (below(held(*grad, backs[0])),)
            below_mine.append(*passed)
        new, vec = finished(own, cot_mine[part], weight[part], backs, *passed)
        grad = (new,)
        vectors.append(vec)
    below_mine.append(below(*grad))

    mine = jnp.concatenate(below_mine, axis=0)
    theirs = jnp.concatenate([xored(f, "tensor", 1) for f in below_mine], axis=0)
    handed = jnp.concatenate(
        [jnp.where(core == 0, mine, theirs), jnp.where(core == 0, theirs, mine)], axis=0
    )

    vec_mine = jnp.concatenate(vectors, axis=0)
    vec_theirs = xored(vec_mine, "tensor", 1)
    sketch_sum = jnp.concatenate(
        [jnp.where(core == 0, vec_mine, vec_theirs), jnp.where(core == 0, vec_theirs, vec_mine)],
        axis=0,
    )
    out_vec = jnp.dot(cot, model_sketch[0], preferred_element_type=jnp.float32)
    counts = lengths[0, 0]
    upto = jnp.arange(counts.shape[0])
    ends = jnp.sum(jnp.where(upto[None, :] <= upto[:, None], counts[None, :], 0), axis=1)
    starts = ends - counts
    position = jnp.arange(tok_dev, dtype=jnp.int32)
    member = ((position[None, :] >= starts[:, None]) & (position[None, :] < ends[:, None])).astype(
        jnp.float32
    )
    down_feat = jnp.einsum(
        "et,ta,tb->eab", member, out_vec, sketch_sum[:, :rank], precision=lax.Precision.HIGHEST
    )
    up_feat = jnp.einsum(
        "et,ta,tb->eab",
        member,
        sketch_sum[:, rank:],
        input_sketch[0],
        precision=lax.Precision.HIGHEST,
    )
    features = jnp.concatenate([down_feat, up_feat], axis=2)
    return (handed[None], features[None])


def solution(mesh):
    in_specs = (
        P("section", ("groups", "dp"), None),
        P("section", ("groups", "dp"), None),
        P("section", ("groups", "dp"), None),
        P("section", "dp", None, "tensor"),
        P("section", "dp", "tensor", None),
        P("section", ("groups", "dp"), None, None, "tensor"),
        P("section", ("groups", "dp"), None),
        P("section", None, None),
        P("section", "dp", "tensor", None),
        P("section", ("groups", "dp"), None),
    )
    out_specs = (P("section", ("groups", "dp"), None), P("section", ("groups", "dp"), None, None))
    return jax.shard_map(
        per_device, mesh=mesh, in_specs=in_specs, out_specs=out_specs, check_vma=False
    )
```

```python
import functools

import jax
import jax.numpy as jnp
from jax import lax
from jax.experimental import pallas as pl
from jax.experimental.pallas import tpu as pltpu
from jax.sharding import PartitionSpec as P

EXPERTS = 4
CHUNKS = 2
NT = (((1,), (1,)), ((), ()))


def xored(block, axis, bits):
    n = lax.axis_size(axis)
    return lax.ppermute(block, axis, [(i, i ^ bits) for i in range(n)])


ANYWHERE = pl.BlockSpec(memory_space=pl.ANY)
RESIDENT = pl.BlockSpec(memory_space=pltpu.VMEM)


def held_kernel(block_ref, *refs):
    refs[-1][...] = block_ref[...]


def held(block, *events, beside=0):
    return pl.pallas_call(
        held_kernel,
        in_specs=[RESIDENT] + [ANYWHERE] * len(events),
        out_specs=RESIDENT,
        out_shape=jax.ShapeDtypeStruct(block.shape, block.dtype),
        compiler_params=pltpu.CompilerParams(vmem_limit_bytes=1 << 20),
        cost_estimate=pl.CostEstimate(
            flops=0, bytes_accessed=4 * block.size + beside, transcendentals=0
        ),
        name="held",
    )(block, *events)


def merge_kernel(keep_ref, came_ref, own_ref, *sent_refs):
    rows = own_ref.shape[0]
    own_ref[...] = keep_ref[:rows] + came_ref[:rows].astype(jnp.float32)
    for at, sent_ref in enumerate(sent_refs):
        part = slice((at + 1) * rows, (at + 2) * rows)
        total = keep_ref[part] + came_ref[part].astype(jnp.float32)
        sent_ref[...] = total.astype(jnp.bfloat16)


def merged(keep, came, rows):
    count, wide = keep.shape
    others = count // rows - 1
    return pl.pallas_call(
        merge_kernel,
        in_specs=[RESIDENT] * 2,
        out_specs=[RESIDENT] * (1 + others),
        out_shape=[jax.ShapeDtypeStruct((rows, wide), jnp.float32)]
        + [jax.ShapeDtypeStruct((rows, wide), jnp.bfloat16)] * others,
        compiler_params=pltpu.CompilerParams(vmem_limit_bytes=4 << 20),
        cost_estimate=pl.CostEstimate(
            flops=count * wide, bytes_accessed=8 * count * wide, transcendentals=0
        ),
        name="merge",
    )(keep, came)


def finish_kernel(slots, own_ref, cot_ref, weight_ref, *refs):
    grad_ref, vec_ref = refs[-2:]
    width = grad_ref.shape[1]
    total = weight_ref[:, :1] * own_ref[...]
    for slot in range(1, slots):
        total += weight_ref[:, slot : slot + 1] * refs[slot - 1][...].astype(jnp.float32)
    grad_ref[...] = (cot_ref[...].astype(jnp.float32) + total[:, :width]).astype(jnp.bfloat16)
    vec_ref[...] = total[:, width:]


def finished(own, cot, weight, backs, *events):
    rows, wide = own.shape
    width = cot.shape[1]
    return pl.pallas_call(
        functools.partial(finish_kernel, 1 + len(backs)),
        in_specs=[RESIDENT] * (3 + len(backs)) + [ANYWHERE] * len(events),
        out_specs=[RESIDENT] * 2,
        out_shape=[
            jax.ShapeDtypeStruct((rows, width), jnp.bfloat16),
            jax.ShapeDtypeStruct((rows, wide - width), jnp.float32),
        ],
        compiler_params=pltpu.CompilerParams(vmem_limit_bytes=4 << 20),
        cost_estimate=pl.CostEstimate(
            flops=8 * rows * wide, bytes_accessed=12 * rows * wide, transcendentals=0
        ),
        name="finish",
    )(own, cot, weight, *backs, *events)


def tile_of(size, most):
    best = 128
    for tile in range(128, most + 1, 128):
        if size % tile == 0:
            best = tile
    return best


def slope_kernel(groups, index_ref, *refs):
    del index_ref
    pre_refs, sketch_ref = refs[:groups], refs[groups]
    slope_ref, down_ref = refs[-2:]
    pre = jnp.concatenate([r[0, 0, 0] for r in pre_refs], axis=0).astype(jnp.float32)
    sig = 0.5 + 0.5 * jnp.tanh(0.5 * pre)
    hidden = pre * sig
    slope = sig + hidden * (1.0 - sig)
    slope_ref[0] = slope.T.astype(slope_ref.dtype)
    term = lax.dot_general(
        hidden.astype(jnp.bfloat16), sketch_ref[...], NT, preferred_element_type=jnp.float32
    )

    @pl.when(pl.program_id(1) == 0)
    def _():
        down_ref[...] = jnp.zeros_like(down_ref)

    down_ref[0] += term


def slopes(pre, sketch_t, place, core):
    n, _, chunks, rows, cols = pre.shape
    rank = sketch_t.shape[0]
    groups = 2 * n
    tile = tile_of(cols, 896)
    index = jnp.stack([place, core]).astype(jnp.int32)
    pre = pltpu.with_memory_space_constraint(pre, pltpu.HBM)
    sketch_t = pltpu.with_memory_space_constraint(sketch_t, pltpu.HBM)

    def spec_of(h, slot):
        return pl.BlockSpec(
            (1, 1, 1, rows, tile), lambda a, j, ix: (ix[0] ^ slot, ix[1] ^ h, a, 0, j)
        )

    return pl.pallas_call(
        functools.partial(slope_kernel, groups),
        grid_spec=pltpu.PrefetchScalarGridSpec(
            num_scalar_prefetch=1,
            grid=(chunks, cols // tile),
            in_specs=[spec_of(h, slot) for h in range(2) for slot in range(n)]
            + [pl.BlockSpec((rank, tile), lambda a, j, ix: (0, j))],
            out_specs=[
                pl.BlockSpec((1, tile, groups * rows), lambda a, j, ix: (a, j, 0)),
                pl.BlockSpec((1, groups * rows, rank), lambda a, j, ix: (a, 0, 0)),
            ],
        ),
        out_shape=[
            jax.ShapeDtypeStruct((chunks, cols, groups * rows), jnp.bfloat16),
            jax.ShapeDtypeStruct((chunks, groups * rows, rank), jnp.float32),
        ],
        cost_estimate=pl.CostEstimate(
            flops=2 * chunks * groups * rows * cols * rank,
            bytes_accessed=4 * chunks * groups * rows * cols,
            transcendentals=chunks * groups * rows * cols,
        ),
        compiler_params=pltpu.CompilerParams(vmem_limit_bytes=7 << 20),
        name="slopes",
    )(index, *([pre] * groups), sketch_t)


def expert_kernel(
    tile_f, tile_d, rows_ref, slope_ref, down_part_ref, sketch_ref, down_ref, up_hbm, *refs
):
    keep_ref, give_ref, rows_buf, grad_buf, up_buf, up_sem = refs[-6:]
    hidden_cols, width = down_ref.shape
    steps_f, steps_d = hidden_cols // tile_f, width // tile_d
    half = keep_ref.shape[0]

    def tile(j, size):
        return pl.ds(pl.multiple_of(j * size, size), size)

    def up_copy(j):
        part = tile(j, tile_d)
        return pltpu.make_async_copy(up_hbm.at[part], up_buf.at[part], up_sem.at[j])

    for j in range(steps_d):
        if j == 0 or j > steps_f:
            up_copy(j).start()
    rows_buf[...] = rows_ref[...].T

    def first(j, carry):
        @pl.when(j + 1 < steps_d)
        def _():
            up_copy(j + 1).start()

        part = tile(j, tile_f)
        grad_hidden = jnp.dot(
            down_ref[part, :], rows_buf[...], preferred_element_type=jnp.float32
        )
        slope = slope_ref[0, part, :].astype(jnp.float32)
        grad_buf[part, :] = (grad_hidden * slope).astype(jnp.bfloat16)
        return carry

    lax.fori_loop(0, steps_f, first, 0)

    up_part = jnp.dot(sketch_ref[...], grad_buf[...], preferred_element_type=jnp.float32).T
    vectors = jnp.concatenate([down_part_ref[0], up_part], axis=1)
    keep_ref[:, width:] = vectors[:half]
    give_ref[:, width:] = vectors[half:].astype(jnp.bfloat16)

    def second(j, carry):
        up_copy(j).wait()
        part = tile(j, tile_d)
        term = jnp.dot(up_buf[part, :], grad_buf[...], preferred_element_type=jnp.float32).T
        keep_ref[:, part] = term[:half]
        give_ref[:, part] = term[half:].astype(jnp.bfloat16)
        return carry

    lax.fori_loop(0, steps_d, second, 0)


def expert(chunk, rows, slope, down_part, sketch_t, down_local, up_local, *events):
    count, width = rows.shape
    hidden_cols = down_local.shape[0]
    rank = sketch_t.shape[0]
    wide = width + 2 * rank
    tile_f, tile_d = tile_of(hidden_cols, 1792), tile_of(width, 1024)
    return pl.pallas_call(
        functools.partial(expert_kernel, tile_f, tile_d),
        grid=(1,),
        in_specs=[
            RESIDENT,
            pl.BlockSpec((1, hidden_cols, count), lambda i: (chunk, 0, 0)),
            pl.BlockSpec((1, count, rank), lambda i: (chunk, 0, 0)),
        ]
        + [RESIDENT] * 2
        + [pl.BlockSpec(memory_space=pltpu.HBM)]
        + [ANYWHERE] * len(events),
        out_specs=[RESIDENT] * 2,
        out_shape=[
            jax.ShapeDtypeStruct((count // 2, wide), jnp.float32),
            jax.ShapeDtypeStruct((count // 2, wide), jnp.bfloat16),
        ],
        scratch_shapes=[
            pltpu.VMEM((width, count), jnp.bfloat16),
            pltpu.VMEM((hidden_cols, count), jnp.bfloat16),
            pltpu.VMEM((width, hidden_cols), jnp.bfloat16),
            pltpu.SemaphoreType.DMA((width // tile_d,)),
        ],
        compiler_params=pltpu.CompilerParams(vmem_limit_bytes=26 << 20),
        cost_estimate=pl.CostEstimate(
            flops=4 * count * hidden_cols * width,
            bytes_accessed=4 * hidden_cols * width,
            transcendentals=0,
        ),
        name="expert",
    )(rows, slope, down_part, sketch_t, down_local, up_local, *events)


def per_device(
    cotangent,
    routes,
    gate_values,
    up_weight,
    down_weight,
    pre_activation,
    input_sketch,
    model_sketch,
    hidden_sketch,
    lengths,
):
    pieces = lax.axis_size("dp")
    sections = lax.axis_size("section")
    per_expert = pieces // EXPERTS
    place = lax.axis_index("dp")
    core = lax.axis_index("tensor")
    cot = cotangent[0]
    tok_dev, width = cot.shape
    half = tok_dev // 2
    rows = half // CHUNKS
    rank = model_sketch.shape[2]
    blocks = routes.shape[1]
    block_len = tok_dev // blocks
    sketch_local = hidden_sketch[0, 0]
    pre_all = pre_activation[0, 0]
    hidden_cols = pre_all.shape[2]
    pre_all = pre_all.reshape(pieces, 2, CHUNKS, rows, hidden_cols)

    def below(block):
        return lax.ppermute(block, "section", [(s, (s - 1) % sections) for s in range(sections)])

    token_routes = jnp.broadcast_to(routes[0][:, None, :], (blocks, block_len, 2)).reshape(
        tok_dev, 2
    )
    half_routes = lax.dynamic_slice_in_dim(token_routes, core * half, half, 0)
    half_gates = lax.dynamic_slice_in_dim(gate_values[0], core * half, half, 0)
    slot_expert = (place ^ jnp.arange(pieces, dtype=jnp.int32)) // per_expert
    hits = half_routes[:, None, :] == slot_expert[None, :, None]
    weight = jnp.sum(jnp.where(hits, half_gates[:, None, :], 0.0), axis=2)

    sketch_t = sketch_local.T
    cot_mine = lax.dynamic_slice_in_dim(cot, core * half, half, 0)
    cot_theirs = lax.dynamic_slice_in_dim(cot, (1 - core) * half, half, 0)
    order = sorted(range(1, pieces), reverse=True)
    slope, down_part = slopes(pre_all, sketch_t, place, core)
    mark, keep, sent, grad, passed = (), (), (), (), ()
    below_mine, vectors = [], []
    for a in range(CHUNKS):
        part = slice(a * rows, (a + 1) * rows)
        mine, theirs = {0: cot_mine[part]}, {0: cot_theirs[part]}
        if mark:
            mine[0] = held(mine[0], *mark)
        for slot in order:
            mine[slot] = xored(mine[0], "dp", slot)
        mark = (mine[1],)
        if keep:
            for slot in order:
                mine[slot] = held(mine[slot], *keep, beside=2 * down_weight.size)
        traded = xored(jnp.concatenate([mine[slot] for slot in order], axis=0), "tensor", 1)
        for at, slot in enumerate(order):
            theirs[slot] = traded[at * rows : (at + 1) * rows]
        rows_in = jnp.concatenate(
            [mine[k] for k in range(pieces)] + [theirs[k] for k in range(pieces)], axis=0
        )

        kept, give = expert(
            a, rows_in, slope, down_part, sketch_t, down_weight[0, 0], up_weight[0, 0], *sent
        )
        keep = (kept,)
        if grad:
            give = held(give, *backs)
        own, *sent = merged(kept, xored(give, "tensor", 1), rows)
        backs = [xored(out, "dp", slot + 1) for slot, out in enumerate(sent)]
        if grad:
            passed = (below(held(*grad, backs[0])),)
            below_mine.append(*passed)
        new, vec = finished(own, cot_mine[part], weight[part], backs, *passed)
        grad = (new,)
        vectors.append(vec)
    below_mine.append(below(*grad))

    mine = jnp.concatenate(below_mine, axis=0)
    theirs = jnp.concatenate([xored(f, "tensor", 1) for f in below_mine], axis=0)
    handed = jnp.concatenate(
        [jnp.where(core == 0, mine, theirs), jnp.where(core == 0, theirs, mine)], axis=0
    )

    vec_mine = jnp.concatenate(vectors, axis=0)
    vec_theirs = xored(vec_mine, "tensor", 1)
    sketch_sum = jnp.concatenate(
        [jnp.where(core == 0, vec_mine, vec_theirs), jnp.where(core == 0, vec_theirs, vec_mine)],
        axis=0,
    )
    out_vec = jnp.dot(cot, model_sketch[0], preferred_element_type=jnp.float32)
    counts = lengths[0, 0]
    upto = jnp.arange(counts.shape[0])
    ends = jnp.sum(jnp.where(upto[None, :] <= upto[:, None], counts[None, :], 0), axis=1)
    starts = ends - counts
    position = jnp.arange(tok_dev, dtype=jnp.int32)
    member = ((position[None, :] >= starts[:, None]) & (position[None, :] < ends[:, None])).astype(
        jnp.float32
    )
    down_feat = jnp.einsum(
        "et,ta,tb->eab", member, out_vec, sketch_sum[:, :rank], precision=lax.Precision.HIGHEST
    )
    up_feat = jnp.einsum(
        "et,ta,tb->eab",
        member,
        sketch_sum[:, rank:],
        input_sketch[0],
        precision=lax.Precision.HIGHEST,
    )
    features = jnp.concatenate([down_feat, up_feat], axis=2)
    return (handed[None], features[None])


def solution(mesh):
    in_specs = (
        P("section", ("groups", "dp"), None),
        P("section", ("groups", "dp"), None),
        P("section", ("groups", "dp"), None),
        P("section", "dp", None, "tensor"),
        P("section", "dp", "tensor", None),
        P("section", ("groups", "dp"), None, None, "tensor"),
        P("section", ("groups", "dp"), None),
        P("section", None, None),
        P("section", "dp", "tensor", None),
        P("section", ("groups", "dp"), None),
    )
    out_specs = (P("section", ("groups", "dp"), None), P("section", ("groups", "dp"), None, None))
    return jax.shard_map(
        per_device, mesh=mesh, in_specs=in_specs, out_specs=out_specs, check_vma=False
    )
```

```python
import functools

import jax
import jax.numpy as jnp
from jax import lax
from jax.experimental import pallas as pl
from jax.experimental.pallas import tpu as pltpu
from jax.sharding import PartitionSpec as P

EXPERTS = 4
CHUNKS = 2
NT = (((1,), (1,)), ((), ()))


def xored(block, axis, bits):
    n = lax.axis_size(axis)
    return lax.ppermute(block, axis, [(i, i ^ bits) for i in range(n)])


ANYWHERE = pl.BlockSpec(memory_space=pl.ANY)
RESIDENT = pl.BlockSpec(memory_space=pltpu.VMEM)


def held_kernel(block_ref, *refs):
    refs[-1][...] = block_ref[...]


def held(block, *events, beside=()):
    return pl.pallas_call(
        held_kernel,
        in_specs=[RESIDENT]
        + [ANYWHERE] * len(events)
        + [pl.BlockSpec(memory_space=pltpu.HBM)] * len(beside),
        out_specs=RESIDENT,
        out_shape=jax.ShapeDtypeStruct(block.shape, block.dtype),
        compiler_params=pltpu.CompilerParams(vmem_limit_bytes=1 << 20),
        name="held",
    )(block, *events, *beside)


def merge_kernel(keep_ref, came_ref, own_ref, *sent_refs):
    rows = own_ref.shape[0]
    own_ref[...] = keep_ref[:rows] + came_ref[:rows].astype(jnp.float32)
    for at, sent_ref in enumerate(sent_refs):
        part = slice((at + 1) * rows, (at + 2) * rows)
        total = keep_ref[part] + came_ref[part].astype(jnp.float32)
        sent_ref[...] = total.astype(jnp.bfloat16)


def merged(keep, came, rows):
    count, wide = keep.shape
    others = count // rows - 1
    return pl.pallas_call(
        merge_kernel,
        in_specs=[RESIDENT] * 2,
        out_specs=[RESIDENT] * (1 + others),
        out_shape=[jax.ShapeDtypeStruct((rows, wide), jnp.float32)]
        + [jax.ShapeDtypeStruct((rows, wide), jnp.bfloat16)] * others,
        compiler_params=pltpu.CompilerParams(vmem_limit_bytes=4 << 20),
        cost_estimate=pl.CostEstimate(
            flops=count * wide, bytes_accessed=8 * count * wide, transcendentals=0
        ),
        name="merge",
    )(keep, came)


def finish_kernel(slots, own_ref, cot_ref, weight_ref, *refs):
    grad_ref, vec_ref = refs[-2:]
    width = grad_ref.shape[1]
    total = weight_ref[:, :1] * own_ref[...]
    for slot in range(1, slots):
        total += weight_ref[:, slot : slot + 1] * refs[slot - 1][...].astype(jnp.float32)
    grad_ref[...] = (cot_ref[...].astype(jnp.float32) + total[:, :width]).astype(jnp.bfloat16)
    vec_ref[...] = total[:, width:]


def finished(own, cot, weight, backs, *events):
    rows, wide = own.shape
    width = cot.shape[1]
    return pl.pallas_call(
        functools.partial(finish_kernel, 1 + len(backs)),
        in_specs=[RESIDENT] * (3 + len(backs)) + [ANYWHERE] * len(events),
        out_specs=[RESIDENT] * 2,
        out_shape=[
            jax.ShapeDtypeStruct((rows, width), jnp.bfloat16),
            jax.ShapeDtypeStruct((rows, wide - width), jnp.float32),
        ],
        compiler_params=pltpu.CompilerParams(vmem_limit_bytes=4 << 20),
        cost_estimate=pl.CostEstimate(
            flops=8 * rows * wide, bytes_accessed=12 * rows * wide, transcendentals=0
        ),
        name="finish",
    )(own, cot, weight, *backs, *events)


def tile_of(size, most):
    best = 128
    for tile in range(128, most + 1, 128):
        if size % tile == 0:
            best = tile
    return best


def slope_kernel(groups, index_ref, *refs):
    del index_ref
    pre_refs, sketch_ref = refs[:groups], refs[groups]
    slope_ref, down_ref = refs[-2:]
    pre = jnp.concatenate([r[0, 0, 0] for r in pre_refs], axis=0).astype(jnp.float32)
    sig = 0.5 + 0.5 * jnp.tanh(0.5 * pre)
    hidden = pre * sig
    slope = sig + hidden * (1.0 - sig)
    slope_ref[0] = slope.T.astype(slope_ref.dtype)
    term = lax.dot_general(
        hidden.astype(jnp.bfloat16), sketch_ref[...], NT, preferred_element_type=jnp.float32
    )

    @pl.when(pl.program_id(1) == 0)
    def _():
        down_ref[...] = jnp.zeros_like(down_ref)

    down_ref[0] += term


def slopes(pre, sketch_t, place, core):
    n, _, chunks, rows, cols = pre.shape
    rank = sketch_t.shape[0]
    groups = 2 * n
    tile = tile_of(cols, 896)
    index = jnp.stack([place, core]).astype(jnp.int32)

    def spec_of(h, slot):
        return pl.BlockSpec(
            (1, 1, 1, rows, tile), lambda a, j, ix: (ix[0] ^ slot, ix[1] ^ h, a, 0, j)
        )

    return pl.pallas_call(
        functools.partial(slope_kernel, groups),
        grid_spec=pltpu.PrefetchScalarGridSpec(
            num_scalar_prefetch=1,
            grid=(chunks, cols // tile),
            in_specs=[spec_of(h, slot) for h in range(2) for slot in range(n)]
            + [pl.BlockSpec((rank, tile), lambda a, j, ix: (0, j))],
            out_specs=[
                pl.BlockSpec((1, tile, groups * rows), lambda a, j, ix: (a, j, 0)),
                pl.BlockSpec((1, groups * rows, rank), lambda a, j, ix: (a, 0, 0)),
            ],
        ),
        out_shape=[
            jax.ShapeDtypeStruct((chunks, cols, groups * rows), jnp.bfloat16),
            jax.ShapeDtypeStruct((chunks, groups * rows, rank), jnp.float32),
        ],
        cost_estimate=pl.CostEstimate(
            flops=2 * chunks * groups * rows * cols * rank,
            bytes_accessed=4 * chunks * groups * rows * cols,
            transcendentals=chunks * groups * rows * cols,
        ),
        compiler_params=pltpu.CompilerParams(vmem_limit_bytes=7 << 20),
        name="slopes",
    )(index, *([pre] * groups), sketch_t)


def expert_kernel(
    tile_f, tile_d, rows_ref, slope_ref, down_part_ref, sketch_ref, down_ref, up_hbm, *refs
):
    keep_ref, give_ref, rows_buf, grad_buf, up_buf, up_sem = refs[-6:]
    hidden_cols, width = down_ref.shape
    steps_f, steps_d = hidden_cols // tile_f, width // tile_d
    half = keep_ref.shape[0]

    def tile(j, size):
        return pl.ds(pl.multiple_of(j * size, size), size)

    def up_copy(j):
        part = tile(j, tile_d)
        return pltpu.make_async_copy(up_hbm.at[part], up_buf.at[part], up_sem.at[j])

    for j in range(steps_d):
        if j == 0 or j > steps_f:
            up_copy(j).start()
    rows_buf[...] = rows_ref[...].T

    def first(j, carry):
        @pl.when(j + 1 < steps_d)
        def _():
            up_copy(j + 1).start()

        part = tile(j, tile_f)
        grad_hidden = jnp.dot(
            down_ref[part, :], rows_buf[...], preferred_element_type=jnp.float32
        )
        slope = slope_ref[0, part, :].astype(jnp.float32)
        grad_buf[part, :] = (grad_hidden * slope).astype(jnp.bfloat16)
        return carry

    lax.fori_loop(0, steps_f, first, 0)

    up_part = jnp.dot(sketch_ref[...], grad_buf[...], preferred_element_type=jnp.float32).T
    vectors = jnp.concatenate([down_part_ref[0], up_part], axis=1)
    keep_ref[:, width:] = vectors[:half]
    give_ref[:, width:] = vectors[half:].astype(jnp.bfloat16)

    def second(j, carry):
        up_copy(j).wait()
        part = tile(j, tile_d)
        term = jnp.dot(up_buf[part, :], grad_buf[...], preferred_element_type=jnp.float32).T
        keep_ref[:, part] = term[:half]
        give_ref[:, part] = term[half:].astype(jnp.bfloat16)
        return carry

    lax.fori_loop(0, steps_d, second, 0)


def expert(chunk, rows, slope, down_part, sketch_t, down_local, up_local, *events):
    count, width = rows.shape
    hidden_cols = down_local.shape[0]
    rank = sketch_t.shape[0]
    wide = width + 2 * rank
    tile_f, tile_d = tile_of(hidden_cols, 1792), tile_of(width, 1024)
    return pl.pallas_call(
        functools.partial(expert_kernel, tile_f, tile_d),
        grid=(1,),
        in_specs=[
            RESIDENT,
            pl.BlockSpec((1, hidden_cols, count), lambda i: (chunk, 0, 0)),
            pl.BlockSpec((1, count, rank), lambda i: (chunk, 0, 0)),
        ]
        + [RESIDENT] * 2
        + [pl.BlockSpec(memory_space=pltpu.HBM)]
        + [ANYWHERE] * len(events),
        out_specs=[RESIDENT] * 2,
        out_shape=[
            jax.ShapeDtypeStruct((count // 2, wide), jnp.float32),
            jax.ShapeDtypeStruct((count // 2, wide), jnp.bfloat16),
        ],
        scratch_shapes=[
            pltpu.VMEM((width, count), jnp.bfloat16),
            pltpu.VMEM((hidden_cols, count), jnp.bfloat16),
            pltpu.VMEM((width, hidden_cols), jnp.bfloat16),
            pltpu.SemaphoreType.DMA((width // tile_d,)),
        ],
        compiler_params=pltpu.CompilerParams(vmem_limit_bytes=26 << 20),
        cost_estimate=pl.CostEstimate(
            flops=4 * count * hidden_cols * width,
            bytes_accessed=4 * hidden_cols * width,
            transcendentals=0,
        ),
        name="expert",
    )(rows, slope, down_part, sketch_t, down_local, up_local, *events)


def per_device(
    cotangent,
    routes,
    gate_values,
    up_weight,
    down_weight,
    pre_activation,
    input_sketch,
    model_sketch,
    hidden_sketch,
    lengths,
):
    pieces = lax.axis_size("dp")
    sections = lax.axis_size("section")
    per_expert = pieces // EXPERTS
    place = lax.axis_index("dp")
    core = lax.axis_index("tensor")
    cot = cotangent[0]
    tok_dev, width = cot.shape
    half = tok_dev // 2
    rows = half // CHUNKS
    rank = model_sketch.shape[2]
    blocks = routes.shape[1]
    block_len = tok_dev // blocks
    sketch_local = hidden_sketch[0, 0]
    pre_all = pre_activation[0, 0]
    hidden_cols = pre_all.shape[2]
    pre_all = pre_all.reshape(pieces, 2, CHUNKS, rows, hidden_cols)

    def below(block):
        return lax.ppermute(block, "section", [(s, (s - 1) % sections) for s in range(sections)])

    token_routes = jnp.broadcast_to(routes[0][:, None, :], (blocks, block_len, 2)).reshape(
        tok_dev, 2
    )
    half_routes = lax.dynamic_slice_in_dim(token_routes, core * half, half, 0)
    half_gates = lax.dynamic_slice_in_dim(gate_values[0], core * half, half, 0)
    slot_expert = (place ^ jnp.arange(pieces, dtype=jnp.int32)) // per_expert
    hits = half_routes[:, None, :] == slot_expert[None, :, None]
    weight = jnp.sum(jnp.where(hits, half_gates[:, None, :], 0.0), axis=2)

    sketch_t = sketch_local.T
    cot_mine = lax.dynamic_slice_in_dim(cot, core * half, half, 0)
    cot_theirs = lax.dynamic_slice_in_dim(cot, (1 - core) * half, half, 0)
    order = sorted(range(1, pieces), reverse=True)
    slope, down_part = slopes(pre_all, sketch_t, place, core)
    mark, keep, sent, grad, passed = (), (), (), (), ()
    below_mine, vectors = [], []
    for a in range(CHUNKS):
        part = slice(a * rows, (a + 1) * rows)
        mine, theirs = {0: cot_mine[part]}, {0: cot_theirs[part]}
        if mark:
            mine[0] = held(mine[0], *mark)
        for slot in order:
            mine[slot] = xored(mine[0], "dp", slot)
        mark = (mine[1],)
        if keep:
            for slot in order:
                mine[slot] = held(
                    mine[slot], *keep, beside=(up_weight[0, 0], down_weight[0, 0])
                )
        traded = xored(jnp.concatenate([mine[slot] for slot in order], axis=0), "tensor", 1)
        for at, slot in enumerate(order):
            theirs[slot] = traded[at * rows : (at + 1) * rows]
        rows_in = jnp.concatenate(
            [mine[k] for k in range(pieces)] + [theirs[k] for k in range(pieces)], axis=0
        )

        kept, give = expert(
            a, rows_in, slope, down_part, sketch_t, down_weight[0, 0], up_weight[0, 0], *sent
        )
        keep = (kept,)
        if grad:
            give = held(give, *backs)
        own, *sent = merged(kept, xored(give, "tensor", 1), rows)
        backs = [xored(out, "dp", slot + 1) for slot, out in enumerate(sent)]
        if grad:
            passed = (below(held(*grad, backs[0])),)
            below_mine.append(*passed)
        new, vec = finished(own, cot_mine[part], weight[part], backs, *passed)
        grad = (new,)
        vectors.append(vec)
    below_mine.append(below(*grad))

    mine = jnp.concatenate(below_mine, axis=0)
    theirs = jnp.concatenate([xored(f, "tensor", 1) for f in below_mine], axis=0)
    handed = jnp.concatenate(
        [jnp.where(core == 0, mine, theirs), jnp.where(core == 0, theirs, mine)], axis=0
    )

    vec_mine = jnp.concatenate(vectors, axis=0)
    vec_theirs = xored(vec_mine, "tensor", 1)
    sketch_sum = jnp.concatenate(
        [jnp.where(core == 0, vec_mine, vec_theirs), jnp.where(core == 0, vec_theirs, vec_mine)],
        axis=0,
    )
    out_vec = jnp.dot(cot, model_sketch[0], preferred_element_type=jnp.float32)
    counts = lengths[0, 0]
    upto = jnp.arange(counts.shape[0])
    ends = jnp.sum(jnp.where(upto[None, :] <= upto[:, None], counts[None, :], 0), axis=1)
    starts = ends - counts
    position = jnp.arange(tok_dev, dtype=jnp.int32)
    member = ((position[None, :] >= starts[:, None]) & (position[None, :] < ends[:, None])).astype(
        jnp.float32
    )
    down_feat = jnp.einsum(
        "et,ta,tb->eab", member, out_vec, sketch_sum[:, :rank], precision=lax.Precision.HIGHEST
    )
    up_feat = jnp.einsum(
        "et,ta,tb->eab",
        member,
        sketch_sum[:, rank:],
        input_sketch[0],
        precision=lax.Precision.HIGHEST,
    )
    features = jnp.concatenate([down_feat, up_feat], axis=2)
    return (handed[None], features[None])


def solution(mesh):
    in_specs = (
        P("section", ("groups", "dp"), None),
        P("section", ("groups", "dp"), None),
        P("section", ("groups", "dp"), None),
        P("section", "dp", None, "tensor"),
        P("section", "dp", "tensor", None),
        P("section", ("groups", "dp"), None, None, "tensor"),
        P("section", ("groups", "dp"), None),
        P("section", None, None),
        P("section", "dp", "tensor", None),
        P("section", ("groups", "dp"), None),
    )
    out_specs = (P("section", ("groups", "dp"), None), P("section", ("groups", "dp"), None, None))
    return jax.shard_map(
        per_device, mesh=mesh, in_specs=in_specs, out_specs=out_specs, check_vma=False
    )
```

```python
import functools

import jax
import jax.numpy as jnp
from jax import lax
from jax.experimental import pallas as pl
from jax.experimental.pallas import tpu as pltpu
from jax.sharding import PartitionSpec as P

EXPERTS = 4
CHUNKS = 2
NT = (((1,), (1,)), ((), ()))


def xored(block, axis, bits):
    n = lax.axis_size(axis)
    return lax.ppermute(block, axis, [(i, i ^ bits) for i in range(n)])


ANYWHERE = pl.BlockSpec(memory_space=pl.ANY)
RESIDENT = pl.BlockSpec(memory_space=pltpu.VMEM)


def held_kernel(block_ref, *refs):
    refs[-1][...] = block_ref[...]


def held(block, *events):
    return pl.pallas_call(
        held_kernel,
        in_specs=[RESIDENT] + [ANYWHERE] * len(events),
        out_specs=RESIDENT,
        out_shape=jax.ShapeDtypeStruct(block.shape, block.dtype),
        compiler_params=pltpu.CompilerParams(vmem_limit_bytes=1 << 20),
        name="held",
    )(block, *events)


def merge_kernel(keep_ref, came_ref, own_ref, *sent_refs):
    rows = own_ref.shape[0]
    own_ref[...] = keep_ref[:rows] + came_ref[:rows].astype(jnp.float32)
    for at, sent_ref in enumerate(sent_refs):
        part = slice((at + 1) * rows, (at + 2) * rows)
        total = keep_ref[part] + came_ref[part].astype(jnp.float32)
        sent_ref[...] = total.astype(jnp.bfloat16)


def merged(keep, came, rows):
    count, wide = keep.shape
    others = count // rows - 1
    return pl.pallas_call(
        merge_kernel,
        in_specs=[RESIDENT] * 2,
        out_specs=[RESIDENT] * (1 + others),
        out_shape=[jax.ShapeDtypeStruct((rows, wide), jnp.float32)]
        + [jax.ShapeDtypeStruct((rows, wide), jnp.bfloat16)] * others,
        compiler_params=pltpu.CompilerParams(vmem_limit_bytes=4 << 20),
        cost_estimate=pl.CostEstimate(
            flops=count * wide, bytes_accessed=8 * count * wide, transcendentals=0
        ),
        name="merge",
    )(keep, came)


def finish_kernel(slots, own_ref, cot_ref, weight_ref, *refs):
    grad_ref, vec_ref = refs[-2:]
    width = grad_ref.shape[1]
    total = weight_ref[:, :1] * own_ref[...]
    for slot in range(1, slots):
        total += weight_ref[:, slot : slot + 1] * refs[slot - 1][...].astype(jnp.float32)
    grad_ref[...] = (cot_ref[...].astype(jnp.float32) + total[:, :width]).astype(jnp.bfloat16)
    vec_ref[...] = total[:, width:]


def finished(own, cot, weight, backs, *events):
    rows, wide = own.shape
    width = cot.shape[1]
    return pl.pallas_call(
        functools.partial(finish_kernel, 1 + len(backs)),
        in_specs=[RESIDENT] * (3 + len(backs)) + [ANYWHERE] * len(events),
        out_specs=[RESIDENT] * 2,
        out_shape=[
            jax.ShapeDtypeStruct((rows, width), jnp.bfloat16),
            jax.ShapeDtypeStruct((rows, wide - width), jnp.float32),
        ],
        compiler_params=pltpu.CompilerParams(vmem_limit_bytes=4 << 20),
        cost_estimate=pl.CostEstimate(
            flops=8 * rows * wide, bytes_accessed=12 * rows * wide, transcendentals=0
        ),
        name="finish",
    )(own, cot, weight, *backs, *events)


def tile_of(size, most):
    best = 128
    for tile in range(128, most + 1, 128):
        if size % tile == 0:
            best = tile
    return best


def slope_kernel(groups, index_ref, *refs):
    del index_ref
    pre_refs, sketch_ref, weight_hbm = refs[:groups], refs[groups], refs[groups + 1]
    slope_ref, down_ref, weight_ref, weight_sem = refs[-4:]
    load = pltpu.make_async_copy(weight_hbm, weight_ref, weight_sem)

    @pl.when((pl.program_id(0) == 0) & (pl.program_id(1) == 0))
    def _():
        load.start()

    pre = jnp.concatenate([r[0, 0, 0] for r in pre_refs], axis=0).astype(jnp.float32)
    sig = 0.5 + 0.5 * jnp.tanh(0.5 * pre)
    hidden = pre * sig
    slope = sig + hidden * (1.0 - sig)
    slope_ref[0] = slope.T.astype(slope_ref.dtype)
    term = lax.dot_general(
        hidden.astype(jnp.bfloat16), sketch_ref[...], NT, preferred_element_type=jnp.float32
    )

    @pl.when(pl.program_id(1) == 0)
    def _():
        down_ref[...] = jnp.zeros_like(down_ref)

    down_ref[0] += term

    @pl.when(
        (pl.program_id(0) == pl.num_programs(0) - 1) & (pl.program_id(1) == pl.num_programs(1) - 1)
    )
    def _():
        load.wait()


def slopes(pre, sketch_t, weight, place, core):
    n, _, chunks, rows, cols = pre.shape
    rank = sketch_t.shape[0]
    groups = 2 * n
    tile = tile_of(cols, 896)
    index = jnp.stack([place, core]).astype(jnp.int32)
    weight = pltpu.with_memory_space_constraint(weight, pltpu.HBM)

    def spec_of(h, slot):
        return pl.BlockSpec(
            (1, 1, 1, rows, tile), lambda a, j, ix: (ix[0] ^ slot, ix[1] ^ h, a, 0, j)
        )

    return pl.pallas_call(
        functools.partial(slope_kernel, groups),
        grid_spec=pltpu.PrefetchScalarGridSpec(
            num_scalar_prefetch=1,
            grid=(chunks, cols // tile),
            in_specs=[spec_of(h, slot) for h in range(2) for slot in range(n)]
            + [pl.BlockSpec((rank, tile), lambda a, j, ix: (0, j))]
            + [pl.BlockSpec(memory_space=pltpu.HBM)],
            out_specs=[
                pl.BlockSpec((1, tile, groups * rows), lambda a, j, ix: (a, j, 0)),
                pl.BlockSpec((1, groups * rows, rank), lambda a, j, ix: (a, 0, 0)),
                RESIDENT,
            ],
            scratch_shapes=[pltpu.SemaphoreType.DMA],
        ),
        out_shape=[
            jax.ShapeDtypeStruct((chunks, cols, groups * rows), jnp.bfloat16),
            jax.ShapeDtypeStruct((chunks, groups * rows, rank), jnp.float32),
            jax.ShapeDtypeStruct(weight.shape, weight.dtype),
        ],
        cost_estimate=pl.CostEstimate(
            flops=2 * chunks * groups * rows * cols * rank,
            bytes_accessed=4 * chunks * groups * rows * cols,
            transcendentals=chunks * groups * rows * cols,
        ),
        compiler_params=pltpu.CompilerParams(vmem_limit_bytes=7 << 20),
        name="slopes",
    )(index, *([pre] * groups), sketch_t, weight)


def expert_kernel(
    tile_f, tile_d, rows_ref, slope_ref, down_part_ref, sketch_ref, down_ref, up_hbm, *refs
):
    keep_ref, give_ref, rows_buf, grad_buf, up_buf, up_sem = refs[-6:]
    hidden_cols, width = down_ref.shape
    steps_f, steps_d = hidden_cols // tile_f, width // tile_d
    half = keep_ref.shape[0]

    def tile(j, size):
        return pl.ds(pl.multiple_of(j * size, size), size)

    def up_copy(j):
        part = tile(j, tile_d)
        return pltpu.make_async_copy(up_hbm.at[part], up_buf.at[part], up_sem.at[j])

    for j in range(steps_d):
        if j == 0 or j > steps_f:
            up_copy(j).start()
    rows_buf[...] = rows_ref[...].T

    def first(j, carry):
        @pl.when(j + 1 < steps_d)
        def _():
            up_copy(j + 1).start()

        part = tile(j, tile_f)
        grad_hidden = jnp.dot(
            down_ref[part, :], rows_buf[...], preferred_element_type=jnp.float32
        )
        slope = slope_ref[0, part, :].astype(jnp.float32)
        grad_buf[part, :] = (grad_hidden * slope).astype(jnp.bfloat16)
        return carry

    lax.fori_loop(0, steps_f, first, 0)

    up_part = jnp.dot(sketch_ref[...], grad_buf[...], preferred_element_type=jnp.float32).T
    vectors = jnp.concatenate([down_part_ref[0], up_part], axis=1)
    keep_ref[:, width:] = vectors[:half]
    give_ref[:, width:] = vectors[half:].astype(jnp.bfloat16)

    def second(j, carry):
        up_copy(j).wait()
        part = tile(j, tile_d)
        term = jnp.dot(up_buf[part, :], grad_buf[...], preferred_element_type=jnp.float32).T
        keep_ref[:, part] = term[:half]
        give_ref[:, part] = term[half:].astype(jnp.bfloat16)
        return carry

    lax.fori_loop(0, steps_d, second, 0)


def expert(chunk, rows, slope, down_part, sketch_t, down_local, up_local, *events):
    count, width = rows.shape
    hidden_cols = down_local.shape[0]
    rank = sketch_t.shape[0]
    wide = width + 2 * rank
    tile_f, tile_d = tile_of(hidden_cols, 1792), tile_of(width, 1024)
    up_local = pltpu.with_memory_space_constraint(up_local, pltpu.HBM)
    return pl.pallas_call(
        functools.partial(expert_kernel, tile_f, tile_d),
        grid=(1,),
        in_specs=[
            RESIDENT,
            pl.BlockSpec((1, hidden_cols, count), lambda i: (chunk, 0, 0)),
            pl.BlockSpec((1, count, rank), lambda i: (chunk, 0, 0)),
        ]
        + [RESIDENT] * 2
        + [pl.BlockSpec(memory_space=pltpu.HBM)]
        + [ANYWHERE] * len(events),
        out_specs=[RESIDENT] * 2,
        out_shape=[
            jax.ShapeDtypeStruct((count // 2, wide), jnp.float32),
            jax.ShapeDtypeStruct((count // 2, wide), jnp.bfloat16),
        ],
        scratch_shapes=[
            pltpu.VMEM((width, count), jnp.bfloat16),
            pltpu.VMEM((hidden_cols, count), jnp.bfloat16),
            pltpu.VMEM((width, hidden_cols), jnp.bfloat16),
            pltpu.SemaphoreType.DMA((width // tile_d,)),
        ],
        compiler_params=pltpu.CompilerParams(vmem_limit_bytes=26 << 20),
        cost_estimate=pl.CostEstimate(
            flops=4 * count * hidden_cols * width,
            bytes_accessed=4 * hidden_cols * width,
            transcendentals=0,
        ),
        name="expert",
    )(rows, slope, down_part, sketch_t, down_local, up_local, *events)


def per_device(
    cotangent,
    routes,
    gate_values,
    up_weight,
    down_weight,
    pre_activation,
    input_sketch,
    model_sketch,
    hidden_sketch,
    lengths,
):
    pieces = lax.axis_size("dp")
    sections = lax.axis_size("section")
    per_expert = pieces // EXPERTS
    place = lax.axis_index("dp")
    core = lax.axis_index("tensor")
    cot = cotangent[0]
    tok_dev, width = cot.shape
    half = tok_dev // 2
    rows = half // CHUNKS
    rank = model_sketch.shape[2]
    blocks = routes.shape[1]
    block_len = tok_dev // blocks
    sketch_local = hidden_sketch[0, 0]
    pre_all = pre_activation[0, 0]
    hidden_cols = pre_all.shape[2]
    pre_all = pre_all.reshape(pieces, 2, CHUNKS, rows, hidden_cols)

    def below(block):
        return lax.ppermute(block, "section", [(s, (s - 1) % sections) for s in range(sections)])

    token_routes = jnp.broadcast_to(routes[0][:, None, :], (blocks, block_len, 2)).reshape(
        tok_dev, 2
    )
    half_routes = lax.dynamic_slice_in_dim(token_routes, core * half, half, 0)
    half_gates = lax.dynamic_slice_in_dim(gate_values[0], core * half, half, 0)
    slot_expert = (place ^ jnp.arange(pieces, dtype=jnp.int32)) // per_expert
    hits = half_routes[:, None, :] == slot_expert[None, :, None]
    weight = jnp.sum(jnp.where(hits, half_gates[:, None, :], 0.0), axis=2)

    sketch_t = sketch_local.T
    cot_mine = lax.dynamic_slice_in_dim(cot, core * half, half, 0)
    cot_theirs = lax.dynamic_slice_in_dim(cot, (1 - core) * half, half, 0)
    order = sorted(range(1, pieces), reverse=True)
    slope, down_part, down_here = slopes(pre_all, sketch_t, down_weight[0, 0], place, core)
    mark, keep, sent, grad, passed = (), (), (), (), ()
    below_mine, vectors = [], []
    for a in range(CHUNKS):
        part = slice(a * rows, (a + 1) * rows)
        mine, theirs = {0: cot_mine[part]}, {0: cot_theirs[part]}
        if mark:
            mine[0] = held(mine[0], *mark)
        for slot in order:
            mine[slot] = xored(mine[0], "dp", slot)
        mark = (mine[1],)
        if keep:
            for slot in order:
                mine[slot] = held(mine[slot], *keep)
        traded = xored(jnp.concatenate([mine[slot] for slot in order], axis=0), "tensor", 1)
        for at, slot in enumerate(order):
            theirs[slot] = traded[at * rows : (at + 1) * rows]
        rows_in = jnp.concatenate(
            [mine[k] for k in range(pieces)] + [theirs[k] for k in range(pieces)], axis=0
        )

        kept, give = expert(
            a, rows_in, slope, down_part, sketch_t, down_here, up_weight[0, 0], *sent
        )
        keep = (kept,)
        if grad:
            give = held(give, *backs)
        own, *sent = merged(kept, xored(give, "tensor", 1), rows)
        backs = [xored(out, "dp", slot + 1) for slot, out in enumerate(sent)]
        if grad:
            passed = (below(held(*grad, backs[0])),)
            below_mine.append(*passed)
        new, vec = finished(own, cot_mine[part], weight[part], backs, *passed)
        grad = (new,)
        vectors.append(vec)
    below_mine.append(below(*grad))

    mine = jnp.concatenate(below_mine, axis=0)
    theirs = jnp.concatenate([xored(f, "tensor", 1) for f in below_mine], axis=0)
    handed = jnp.concatenate(
        [jnp.where(core == 0, mine, theirs), jnp.where(core == 0, theirs, mine)], axis=0
    )

    vec_mine = jnp.concatenate(vectors, axis=0)
    vec_theirs = xored(vec_mine, "tensor", 1)
    sketch_sum = jnp.concatenate(
        [jnp.where(core == 0, vec_mine, vec_theirs), jnp.where(core == 0, vec_theirs, vec_mine)],
        axis=0,
    )
    out_vec = jnp.dot(cot, model_sketch[0], preferred_element_type=jnp.float32)
    counts = lengths[0, 0]
    upto = jnp.arange(counts.shape[0])
    ends = jnp.sum(jnp.where(upto[None, :] <= upto[:, None], counts[None, :], 0), axis=1)
    starts = ends - counts
    position = jnp.arange(tok_dev, dtype=jnp.int32)
    member = ((position[None, :] >= starts[:, None]) & (position[None, :] < ends[:, None])).astype(
        jnp.float32
    )
    down_feat = jnp.einsum(
        "et,ta,tb->eab", member, out_vec, sketch_sum[:, :rank], precision=lax.Precision.HIGHEST
    )
    up_feat = jnp.einsum(
        "et,ta,tb->eab",
        member,
        sketch_sum[:, rank:],
        input_sketch[0],
        precision=lax.Precision.HIGHEST,
    )
    features = jnp.concatenate([down_feat, up_feat], axis=2)
    return (handed[None], features[None])


def solution(mesh):
    in_specs = (
        P("section", ("groups", "dp"), None),
        P("section", ("groups", "dp"), None),
        P("section", ("groups", "dp"), None),
        P("section", "dp", None, "tensor"),
        P("section", "dp", "tensor", None),
        P("section", ("groups", "dp"), None, None, "tensor"),
        P("section", ("groups", "dp"), None),
        P("section", None, None),
        P("section", "dp", "tensor", None),
        P("section", ("groups", "dp"), None),
    )
    out_specs = (P("section", ("groups", "dp"), None), P("section", ("groups", "dp"), None, None))
    return jax.shard_map(
        per_device, mesh=mesh, in_specs=in_specs, out_specs=out_specs, check_vma=False
    )
```

```python
import functools

import jax
import jax.numpy as jnp
from jax import lax
from jax.experimental import pallas as pl
from jax.experimental.pallas import tpu as pltpu
from jax.sharding import PartitionSpec as P

EXPERTS = 4
LANES = 128
PARTS = 3
NT = (((1,), (1,)), ((), ()))


def xored(block, axis, bits):
    n = lax.axis_size(axis)
    return lax.ppermute(block, axis, [(i, i ^ bits) for i in range(n)])


ANYWHERE = pl.BlockSpec(memory_space=pl.ANY)
RESIDENT = pl.BlockSpec(memory_space=pltpu.VMEM)


def pack_kernel(
    pieces, per_expert, place_ref, routes_ref, cot_ref, gate_ref, mine_ref, theirs_ref, table_ref
):
    core = place_ref[1]
    tok_dev, width = cot_ref.shape
    half = tok_dev // 2
    blocks = routes_ref.shape[0] // 2
    column = lax.broadcasted_iota(jnp.int32, (LANES, tok_dev), 0)
    block = lax.broadcasted_iota(jnp.int32, (1, tok_dev), 1) // (tok_dev // blocks)
    table = jnp.zeros((LANES, tok_dev), jnp.float32)
    for piece in range(pieces):
        rest = jnp.zeros((1, tok_dev), jnp.float32)
        for k in range(2):
            for b in range(blocks):
                hit = (routes_ref[2 * b + k] == piece // per_expert).astype(jnp.float32)
                rest += jnp.where(block == b, hit * gate_ref[k : k + 1, :], 0.0)
        for j in range(PARTS):
            rounded = rest.astype(jnp.bfloat16).astype(jnp.float32)
            table = jnp.where(column == PARTS * piece + j, rounded, table)
            rest -= rounded
    table_ref[...] = table.T.astype(jnp.bfloat16)
    for h, out_ref in enumerate((mine_ref, theirs_ref)):
        part = pl.ds(pl.multiple_of((core ^ h) * half, half), half)
        out_ref[:, :width] = cot_ref[part, :]
        out_ref[:, width:] = table_ref[part, :]


def packed_rows(cot, gates, routes, index, pieces):
    tok_dev, width = cot.shape
    wide = width + LANES
    cot = pltpu.with_memory_space_constraint(cot, pltpu.HBM)
    return pl.pallas_call(
        functools.partial(pack_kernel, pieces, pieces // EXPERTS),
        grid_spec=pltpu.PrefetchScalarGridSpec(
            num_scalar_prefetch=2,
            grid=(1,),
            in_specs=[
                pl.BlockSpec((tok_dev, width), lambda i, *_: (0, 0)),
                pl.BlockSpec((2, tok_dev), lambda i, *_: (0, 0)),
            ],
            out_specs=[RESIDENT] * 2,
            scratch_shapes=[pltpu.VMEM((tok_dev, LANES), jnp.bfloat16)],
        ),
        out_shape=[jax.ShapeDtypeStruct((tok_dev // 2, wide), jnp.bfloat16)] * 2,
        compiler_params=pltpu.CompilerParams(vmem_limit_bytes=4 << 20),
        name="pack",
    )(index, routes, cot, gates)


def held_kernel(block_ref, *refs):
    refs[-1][...] = block_ref[...]


def held(block, *events):
    return pl.pallas_call(
        held_kernel,
        in_specs=[RESIDENT] + [ANYWHERE] * len(events),
        out_specs=RESIDENT,
        out_shape=jax.ShapeDtypeStruct(block.shape, block.dtype),
        compiler_params=pltpu.CompilerParams(vmem_limit_bytes=1 << 20),
        name="held",
    )(block, *events)


def merge_kernel(keep_ref, came_ref, near_ref, *sent_refs):
    near = near_ref.shape[0]
    near_ref[...] = keep_ref[:near] + came_ref[:near].astype(jnp.float32)
    rows = near // len(sent_refs)
    for i, sent_ref in enumerate(sent_refs):
        part = slice(near + i * rows, near + (i + 1) * rows)
        total = keep_ref[part] + came_ref[part].astype(jnp.float32)
        sent_ref[...] = total.astype(jnp.bfloat16)


def merged(keep, came, cuts):
    count, wide = keep.shape
    half = count // 2
    return pl.pallas_call(
        merge_kernel,
        in_specs=[RESIDENT] * 2,
        out_specs=[RESIDENT] * (1 + cuts),
        out_shape=[jax.ShapeDtypeStruct((half, wide), jnp.float32)]
        + [jax.ShapeDtypeStruct((half // cuts, wide), jnp.bfloat16)] * cuts,
        compiler_params=pltpu.CompilerParams(vmem_limit_bytes=4 << 20),
        cost_estimate=pl.CostEstimate(
            flops=count * wide, bytes_accessed=8 * count * wide, transcendentals=0
        ),
        name="merge",
    )(keep, came)


def join_kernel(cut, near_ref, came_ref, out_ref):
    rows = out_ref.shape[0]
    total = near_ref[cut * rows : (cut + 1) * rows] + came_ref[...].astype(jnp.float32)
    out_ref[...] = total.astype(jnp.bfloat16)


def joined(cut, near, came):
    return pl.pallas_call(
        functools.partial(join_kernel, cut),
        in_specs=[RESIDENT] * 2,
        out_specs=RESIDENT,
        out_shape=jax.ShapeDtypeStruct(came.shape, jnp.bfloat16),
        compiler_params=pltpu.CompilerParams(vmem_limit_bytes=4 << 20),
        name="join",
    )(near, came)


def finish_kernel(cut, backs, near_ref, came_ref, rows_ref, *refs):
    grad_ref, vec_ref = refs[-2:]
    rows, width = grad_ref.shape
    part = slice(cut * rows, (cut + 1) * rows)
    total = near_ref[part] + came_ref[part].astype(jnp.float32)
    for back_ref in refs[:backs]:
        total += back_ref[...].astype(jnp.float32)
    grad = rows_ref[part, :width].astype(jnp.float32) + total[:, :width]
    grad_ref[...] = grad.astype(jnp.bfloat16)
    vec_ref[...] = total[:, width:]


def finished(cut, near, came, own_rows, width, backs, *events):
    rows, wide = backs[0].shape
    return pl.pallas_call(
        functools.partial(finish_kernel, cut, len(backs)),
        in_specs=[RESIDENT] * (3 + len(backs)) + [ANYWHERE] * len(events),
        out_specs=[RESIDENT] * 2,
        out_shape=[
            jax.ShapeDtypeStruct((rows, width), jnp.bfloat16),
            jax.ShapeDtypeStruct((rows, wide - width), jnp.float32),
        ],
        compiler_params=pltpu.CompilerParams(vmem_limit_bytes=4 << 20),
        cost_estimate=pl.CostEstimate(
            flops=8 * rows * wide, bytes_accessed=12 * rows * wide, transcendentals=0
        ),
        name="finish",
    )(near, came, own_rows, *backs, *events)


def tile_of(size, most):
    best = 128
    for tile in range(128, most + 1, 128):
        if size % tile == 0:
            best = tile
    return best


def slope_kernel(groups, loads, index_ref, *refs):
    del index_ref
    pre_refs, sketch_ref = refs[:groups], refs[groups]
    outs = refs[groups + 1 + loads :]
    slope_ref, down_ref = outs[:2]
    if loads:
        load = pltpu.make_async_copy(refs[groups + 1], outs[2], outs[3])

        @pl.when(pl.program_id(0) == 0)
        def _():
            load.start()

    pre = jnp.concatenate([r[0, 0] for r in pre_refs], axis=0).astype(jnp.float32)
    sig = 0.5 + 0.5 * jnp.tanh(0.5 * pre)
    hidden = pre * sig
    slope = sig + hidden * (1.0 - sig)
    slope_ref[...] = slope.T.astype(slope_ref.dtype)
    term = lax.dot_general(
        hidden.astype(jnp.bfloat16), sketch_ref[...], NT, preferred_element_type=jnp.float32
    )

    @pl.when(pl.program_id(0) == 0)
    def _():
        down_ref[...] = jnp.zeros_like(down_ref)

    down_ref[...] += term
    if loads:

        @pl.when(pl.program_id(0) == pl.num_programs(0) - 1)
        def _():
            load.wait()


def slopes(chunk, pre, sketch_t, index, *weights):
    n, _, rows, cols = pre.shape
    rank = sketch_t.shape[0]
    groups, loads = 4, len(weights)
    tile = tile_of(cols, 896)
    weights = [pltpu.with_memory_space_constraint(w, pltpu.HBM) for w in weights]

    def spec_of(h, slot):
        return pl.BlockSpec(
            (1, 1, rows, tile), lambda j, ix: (ix[0] ^ (2 * chunk + slot), ix[1] ^ h, 0, j)
        )

    return pl.pallas_call(
        functools.partial(slope_kernel, groups, loads),
        grid_spec=pltpu.PrefetchScalarGridSpec(
            num_scalar_prefetch=1,
            grid=(cols // tile,),
            in_specs=[spec_of(h, slot) for h in range(2) for slot in range(2)]
            + [pl.BlockSpec((rank, tile), lambda j, ix: (0, j))]
            + [pl.BlockSpec(memory_space=pltpu.HBM)] * loads,
            out_specs=[
                pl.BlockSpec((tile, groups * rows), lambda j, ix: (j, 0)),
                pl.BlockSpec((groups * rows, rank), lambda j, ix: (0, 0)),
            ]
            + [RESIDENT] * loads,
            scratch_shapes=[pltpu.SemaphoreType.DMA] * loads,
        ),
        out_shape=[
            jax.ShapeDtypeStruct((cols, groups * rows), jnp.bfloat16),
            jax.ShapeDtypeStruct((groups * rows, rank), jnp.float32),
        ]
        + [jax.ShapeDtypeStruct(w.shape, w.dtype) for w in weights],
        compiler_params=pltpu.CompilerParams(vmem_limit_bytes=7 << 20),
        name="slopes",
    )(index, *([pre] * groups), sketch_t, *weights)


def expert_kernel(
    tile_f, tile_d, place_ref, rows_ref, slope_ref, down_part_ref, sketch_ref, down_ref, up_hbm, *refs
):
    keep_ref, give_ref, rows_buf, grad_buf, up_buf, up_sem = refs[-6:]
    hidden_cols, width = down_ref.shape
    steps_f, steps_d = hidden_cols // tile_f, width // tile_d
    half = keep_ref.shape[0]

    def tile(j, size):
        return pl.ds(pl.multiple_of(j * size, size), size)

    def up_copy(j):
        part = tile(j, tile_d)
        return pltpu.make_async_copy(up_hbm.at[part], up_buf.at[part], up_sem.at[j])

    for j in range(steps_d):
        if j == 0 or j > steps_f:
            up_copy(j).start()
    rows_buf[...] = rows_ref[:, :width].T
    piece = lax.broadcasted_iota(jnp.int32, (rows_ref.shape[0], LANES), 1) // PARTS
    parts = jnp.where(piece == place_ref[0], rows_ref[:, width:].astype(jnp.float32), 0.0)
    weight = jnp.sum(parts, axis=1, keepdims=True)

    def first(j, carry):
        @pl.when(j + 1 < steps_d)
        def _():
            up_copy(j + 1).start()

        part = tile(j, tile_f)
        grad_hidden = jnp.dot(
            down_ref[part, :], rows_buf[...], preferred_element_type=jnp.float32
        )
        slope = slope_ref[part, :].astype(jnp.float32)
        grad_buf[part, :] = (grad_hidden * slope).astype(jnp.bfloat16)
        return carry

    lax.fori_loop(0, steps_f, first, 0)

    up_part = jnp.dot(sketch_ref[...], grad_buf[...], preferred_element_type=jnp.float32).T
    vectors = weight * jnp.concatenate([down_part_ref[...], up_part], axis=1)
    keep_ref[:, width:] = vectors[:half]
    give_ref[:, width:] = vectors[half:].astype(jnp.bfloat16)

    def second(j, carry):
        up_copy(j).wait()
        part = tile(j, tile_d)
        term = jnp.dot(up_buf[part, :], grad_buf[...], preferred_element_type=jnp.float32).T
        term = weight * term
        keep_ref[:, part] = term[:half]
        give_ref[:, part] = term[half:].astype(jnp.bfloat16)
        return carry

    lax.fori_loop(0, steps_d, second, 0)


def expert(index, rows, slope, down_part, sketch_t, down_local, up_local, *events):
    count = rows.shape[0]
    hidden_cols, width = down_local.shape
    rank = sketch_t.shape[0]
    wide = width + 2 * rank
    tile_f, tile_d = tile_of(hidden_cols, 1792), tile_of(width, 1024)
    up_local = pltpu.with_memory_space_constraint(up_local, pltpu.HBM)
    return pl.pallas_call(
        functools.partial(expert_kernel, tile_f, tile_d),
        in_specs=[pl.BlockSpec(memory_space=pltpu.SMEM), RESIDENT]
        + [RESIDENT] * 4
        + [pl.BlockSpec(memory_space=pltpu.HBM)]
        + [ANYWHERE] * len(events),
        out_specs=[RESIDENT] * 2,
        out_shape=[
            jax.ShapeDtypeStruct((count // 2, wide), jnp.float32),
            jax.ShapeDtypeStruct((count // 2, wide), jnp.bfloat16),
        ],
        scratch_shapes=[
            pltpu.VMEM((width, count), jnp.bfloat16),
            pltpu.VMEM((hidden_cols, count), jnp.bfloat16),
            pltpu.VMEM((width, hidden_cols), jnp.bfloat16),
            pltpu.SemaphoreType.DMA((width // tile_d,)),
        ],
        compiler_params=pltpu.CompilerParams(vmem_limit_bytes=26 << 20),
        name="expert",
    )(index, rows, slope, down_part, sketch_t, down_local, up_local, *events)


def per_device(
    cotangent,
    routes,
    gate_values,
    up_weight,
    down_weight,
    pre_activation,
    input_sketch,
    model_sketch,
    hidden_sketch,
    lengths,
):
    pieces = lax.axis_size("dp")
    sections = lax.axis_size("section")
    place = lax.axis_index("dp")
    core = lax.axis_index("tensor")
    index = jnp.stack([place, core]).astype(jnp.int32)
    cot = cotangent[0]
    tok_dev, width = cot.shape
    half = tok_dev // 2
    rank = model_sketch.shape[2]
    sketch_t = hidden_sketch[0, 0].T
    up_local = up_weight[0, 0]
    pre_all = pre_activation[0, 0]
    pre_all = pre_all.reshape(pieces, 2, half, pre_all.shape[2])

    def below(block):
        return lax.ppermute(block, "section", [(s, (s - 1) % sections) for s in range(sections)])

    own_rows, other_rows = packed_rows(cot, gate_values[0].T, routes[0].reshape(-1), index, pieces)
    cut_rows = half // 2
    near_rows = xored(own_rows, "dp", 1)
    far = [[xored(own_rows[:cut_rows], "dp", slot) for slot in range(2, pieces)]]
    late = held(own_rows[cut_rows:], *far[0])
    far.append([xored(late, "dp", slot) for slot in range(2, pieces)])
    slope, down_part, down_here = slopes(0, pre_all, sketch_t, index, down_weight[0, 0])
    sloped = [(slope, down_part)]
    for c in range(1, pieces // 2):
        sloped.append(slopes(c, pre_all, sketch_t, index))

    keep, came, backs = (), (), ([], [])
    sent = tuple(far[0]) + tuple(part for _, part in sloped[1:])
    for c in range(pieces // 2):
        if c == 0:
            got = [own_rows, near_rows]
            theirs = [other_rows, xored(near_rows, "tensor", 1)]
        else:
            cuts = [far[0][2 * c - 2 : 2 * c]]
            cuts.append([held(block, *keep) for block in far[1][2 * c - 2 : 2 * c]])
            traded = [xored(jnp.concatenate(blocks, axis=0), "tensor", 1) for blocks in cuts]
            got, theirs = [], []
            for i in range(2):
                got += [cuts[0][i], cuts[1][i]]
                theirs += [t[i * cut_rows : (i + 1) * cut_rows] for t in traded]
        kept, give = expert(
            index,
            jnp.concatenate(got + theirs, axis=0),
            *sloped[c],
            sketch_t,
            down_here,
            up_local,
            *sent,
        )
        keep = (kept,)
        if came:
            give = held(give, *came)
        near, *sent = merged(kept, xored(give, "tensor", 1), 1 if c == 0 else 2)
        came = [xored(block, "dp", 1) for block in sent]
        if c == 0:
            own_near, own_came = near, came[0]
        else:
            for cut in range(2):
                backs[cut].append(xored(joined(cut, near, came[cut]), "dp", 2 * c))

    below_mine, vectors, passed = [], [], ()
    for cut in range(2):
        grad, vec = finished(cut, own_near, own_came, own_rows, width, backs[cut], *passed)
        passed = (below(grad),)
        below_mine.append(*passed)
        vectors.append(vec)

    mine = jnp.concatenate(below_mine, axis=0)
    theirs = jnp.concatenate([xored(f, "tensor", 1) for f in below_mine], axis=0)
    handed = jnp.concatenate(
        [jnp.where(core == 0, mine, theirs), jnp.where(core == 0, theirs, mine)], axis=0
    )

    vec_mine = jnp.concatenate(vectors, axis=0)
    vec_theirs = xored(vec_mine, "tensor", 1)
    sketch_sum = jnp.concatenate(
        [jnp.where(core == 0, vec_mine, vec_theirs), jnp.where(core == 0, vec_theirs, vec_mine)],
        axis=0,
    )
    out_vec = jnp.dot(cot, model_sketch[0], preferred_element_type=jnp.float32)
    counts = lengths[0, 0]
    upto = jnp.arange(counts.shape[0])
    ends = jnp.sum(jnp.where(upto[None, :] <= upto[:, None], counts[None, :], 0), axis=1)
    starts = ends - counts
    position = jnp.arange(tok_dev, dtype=jnp.int32)
    member = ((position[None, :] >= starts[:, None]) & (position[None, :] < ends[:, None])).astype(
        jnp.float32
    )
    down_feat = jnp.einsum(
        "et,ta,tb->eab", member, out_vec, sketch_sum[:, :rank], precision=lax.Precision.HIGHEST
    )
    up_feat = jnp.einsum(
        "et,ta,tb->eab",
        member,
        sketch_sum[:, rank:],
        input_sketch[0],
        precision=lax.Precision.HIGHEST,
    )
    features = jnp.concatenate([down_feat, up_feat], axis=2)
    return (handed[None], features[None])


def solution(mesh):
    in_specs = (
        P("section", ("groups", "dp"), None),
        P("section", ("groups", "dp"), None),
        P("section", ("groups", "dp"), None),
        P("section", "dp", None, "tensor"),
        P("section", "dp", "tensor", None),
        P("section", ("groups", "dp"), None, None, "tensor"),
        P("section", ("groups", "dp"), None),
        P("section", None, None),
        P("section", "dp", "tensor", None),
        P("section", ("groups", "dp"), None),
    )
    out_specs = (P("section", ("groups", "dp"), None), P("section", ("groups", "dp"), None, None))
    return jax.shard_map(
        per_device, mesh=mesh, in_specs=in_specs, out_specs=out_specs, check_vma=False
    )
```

```python
import functools

import jax
import jax.numpy as jnp
from jax import lax
from jax.experimental import pallas as pl
from jax.experimental.pallas import tpu as pltpu
from jax.sharding import PartitionSpec as P

EXPERTS = 4
CHUNKS = 2
NT = (((1,), (1,)), ((), ()))


def xored(block, axis, bits):
    n = lax.axis_size(axis)
    return lax.ppermute(block, axis, [(i, i ^ bits) for i in range(n)])


ANYWHERE = pl.BlockSpec(memory_space=pl.ANY)
RESIDENT = pl.BlockSpec(memory_space=pltpu.VMEM)


def held_kernel(block_ref, *refs):
    refs[-1][...] = block_ref[...]


def held(block, *events):
    return pl.pallas_call(
        held_kernel,
        in_specs=[RESIDENT] + [ANYWHERE] * len(events),
        out_specs=RESIDENT,
        out_shape=jax.ShapeDtypeStruct(block.shape, block.dtype),
        compiler_params=pltpu.CompilerParams(vmem_limit_bytes=1 << 20),
        name="held",
    )(block, *events)


def merge_kernel(keep_ref, came_ref, own_ref, *sent_refs):
    rows = own_ref.shape[0]
    own_ref[...] = keep_ref[:rows] + came_ref[:rows].astype(jnp.float32)
    for at, sent_ref in enumerate(sent_refs):
        part = slice((at + 1) * rows, (at + 2) * rows)
        total = keep_ref[part] + came_ref[part].astype(jnp.float32)
        sent_ref[...] = total.astype(jnp.bfloat16)


def merged(keep, came, rows):
    count, wide = keep.shape
    others = count // rows - 1
    return pl.pallas_call(
        merge_kernel,
        in_specs=[RESIDENT] * 2,
        out_specs=[RESIDENT] * (1 + others),
        out_shape=[jax.ShapeDtypeStruct((rows, wide), jnp.float32)]
        + [jax.ShapeDtypeStruct((rows, wide), jnp.bfloat16)] * others,
        compiler_params=pltpu.CompilerParams(vmem_limit_bytes=4 << 20),
        cost_estimate=pl.CostEstimate(
            flops=count * wide, bytes_accessed=8 * count * wide, transcendentals=0
        ),
        name="merge",
    )(keep, came)


def finish_kernel(slots, own_ref, cot_ref, weight_ref, *refs):
    grad_ref, vec_ref = refs[-2:]
    width = grad_ref.shape[1]
    total = weight_ref[:, :1] * own_ref[...]
    for slot in range(1, slots):
        total += weight_ref[:, slot : slot + 1] * refs[slot - 1][...].astype(jnp.float32)
    grad_ref[...] = (cot_ref[...].astype(jnp.float32) + total[:, :width]).astype(jnp.bfloat16)
    vec_ref[...] = total[:, width:]


def finished(own, cot, weight, backs, *events):
    rows, wide = own.shape
    width = cot.shape[1]
    return pl.pallas_call(
        functools.partial(finish_kernel, 1 + len(backs)),
        in_specs=[RESIDENT] * (3 + len(backs)) + [ANYWHERE] * len(events),
        out_specs=[RESIDENT] * 2,
        out_shape=[
            jax.ShapeDtypeStruct((rows, width), jnp.bfloat16),
            jax.ShapeDtypeStruct((rows, wide - width), jnp.float32),
        ],
        compiler_params=pltpu.CompilerParams(vmem_limit_bytes=4 << 20),
        cost_estimate=pl.CostEstimate(
            flops=8 * rows * wide, bytes_accessed=12 * rows * wide, transcendentals=0
        ),
        name="finish",
    )(own, cot, weight, *backs, *events)


def tile_of(size, most):
    best = 128
    for tile in range(128, most + 1, 128):
        if size % tile == 0:
            best = tile
    return best


def slope_kernel(groups, index_ref, *refs):
    del index_ref
    pre_refs, sketch_ref, weight_hbm = refs[:groups], refs[groups], refs[groups + 1]
    slope_ref, down_ref, weight_ref, weight_sem = refs[-4:]
    load = pltpu.make_async_copy(weight_hbm, weight_ref, weight_sem)

    @pl.when((pl.program_id(0) == 0) & (pl.program_id(1) == 0))
    def _():
        load.start()

    pre = jnp.concatenate([r[0, 0, 0] for r in pre_refs], axis=0).astype(jnp.float32)
    sig = 0.5 + 0.5 * jnp.tanh(0.5 * pre)
    hidden = pre * sig
    slope = sig + hidden * (1.0 - sig)
    slope_ref[0] = slope.T.astype(slope_ref.dtype)
    term = lax.dot_general(
        hidden.astype(jnp.bfloat16), sketch_ref[...], NT, preferred_element_type=jnp.float32
    )

    @pl.when(pl.program_id(1) == 0)
    def _():
        down_ref[...] = jnp.zeros_like(down_ref)

    down_ref[0] += term

    @pl.when(
        (pl.program_id(0) == pl.num_programs(0) - 1) & (pl.program_id(1) == pl.num_programs(1) - 1)
    )
    def _():
        load.wait()


def slopes(pre, sketch_t, weight, place, core):
    n, _, chunks, rows, cols = pre.shape
    rank = sketch_t.shape[0]
    groups = 2 * n
    tile = tile_of(cols, 896)
    index = jnp.stack([place, core]).astype(jnp.int32)
    weight = pltpu.with_memory_space_constraint(weight, pltpu.HBM)

    def spec_of(h, slot):
        return pl.BlockSpec(
            (1, 1, 1, rows, tile), lambda a, j, ix: (ix[0] ^ slot, ix[1] ^ h, a, 0, j)
        )

    return pl.pallas_call(
        functools.partial(slope_kernel, groups),
        grid_spec=pltpu.PrefetchScalarGridSpec(
            num_scalar_prefetch=1,
            grid=(chunks, cols // tile),
            in_specs=[spec_of(h, slot) for h in range(2) for slot in range(n)]
            + [pl.BlockSpec((rank, tile), lambda a, j, ix: (0, j))]
            + [pl.BlockSpec(memory_space=pltpu.HBM)],
            out_specs=[
                pl.BlockSpec((1, tile, groups * rows), lambda a, j, ix: (a, j, 0)),
                pl.BlockSpec((1, groups * rows, rank), lambda a, j, ix: (a, 0, 0)),
                RESIDENT,
            ],
            scratch_shapes=[pltpu.SemaphoreType.DMA],
        ),
        out_shape=[
            jax.ShapeDtypeStruct((chunks, cols, groups * rows), jnp.bfloat16),
            jax.ShapeDtypeStruct((chunks, groups * rows, rank), jnp.float32),
            jax.ShapeDtypeStruct(weight.shape, weight.dtype),
        ],
        cost_estimate=pl.CostEstimate(
            flops=2 * chunks * groups * rows * cols * rank,
            bytes_accessed=4 * chunks * groups * rows * cols,
            transcendentals=chunks * groups * rows * cols,
        ),
        compiler_params=pltpu.CompilerParams(vmem_limit_bytes=7 << 20),
        name="slopes",
    )(index, *([pre] * groups), sketch_t, weight)


def expert_kernel(
    tile_f, tile_d, rows_ref, slope_ref, down_part_ref, sketch_ref, down_ref, up_hbm, *refs
):
    keep_ref, give_ref, rows_buf, grad_buf, up_buf, up_sem = refs[-6:]
    hidden_cols, width = down_ref.shape
    steps_f, steps_d = hidden_cols // tile_f, width // tile_d
    half = keep_ref.shape[0]

    def tile(j, size):
        return pl.ds(pl.multiple_of(j * size, size), size)

    def up_copy(j):
        part = tile(j, tile_d)
        return pltpu.make_async_copy(up_hbm.at[part], up_buf.at[part], up_sem.at[j])

    for j in range(steps_d):
        if j == 0 or j > steps_f:
            up_copy(j).start()
    rows_buf[...] = rows_ref[...].T
    up_buf[width:, :] = sketch_ref[...]

    def first(j, carry):
        @pl.when(j + 1 < steps_d)
        def _():
            up_copy(j + 1).start()

        part = tile(j, tile_f)
        grad_hidden = jnp.dot(
            down_ref[part, :], rows_buf[...], preferred_element_type=jnp.float32
        )
        slope = slope_ref[0, part, :].astype(jnp.float32)
        grad_buf[part, :] = (grad_hidden * slope).astype(jnp.bfloat16)
        return carry

    lax.fori_loop(0, steps_f, first, 0)

    for j in range(steps_d):
        up_copy(j).wait()
        last = j == steps_d - 1
        end = up_buf.shape[0] if last else (j + 1) * tile_d
        term = jnp.dot(
            up_buf[j * tile_d : end, :], grad_buf[...], preferred_element_type=jnp.float32
        ).T
        if last:
            term = jnp.concatenate(
                [term[:, :tile_d], down_part_ref[0], term[:, tile_d:]], axis=1
            )
        start = j * tile_d
        keep_ref[:, start : start + term.shape[1]] = term[:half]
        give_ref[:, start : start + term.shape[1]] = term[half:].astype(jnp.bfloat16)


def expert(chunk, rows, slope, down_part, sketch_t, down_local, up_local, *events):
    count, width = rows.shape
    hidden_cols = down_local.shape[0]
    rank = sketch_t.shape[0]
    wide = width + 2 * rank
    tile_f, tile_d = tile_of(hidden_cols, 1792), tile_of(width, 1024)
    up_local = pltpu.with_memory_space_constraint(up_local, pltpu.HBM)
    return pl.pallas_call(
        functools.partial(expert_kernel, tile_f, tile_d),
        grid=(1,),
        in_specs=[
            RESIDENT,
            pl.BlockSpec((1, hidden_cols, count), lambda i: (chunk, 0, 0)),
            pl.BlockSpec((1, count, rank), lambda i: (chunk, 0, 0)),
        ]
        + [RESIDENT] * 2
        + [pl.BlockSpec(memory_space=pltpu.HBM)]
        + [ANYWHERE] * len(events),
        out_specs=[RESIDENT] * 2,
        out_shape=[
            jax.ShapeDtypeStruct((count // 2, wide), jnp.float32),
            jax.ShapeDtypeStruct((count // 2, wide), jnp.bfloat16),
        ],
        scratch_shapes=[
            pltpu.VMEM((width, count), jnp.bfloat16),
            pltpu.VMEM((hidden_cols, count), jnp.bfloat16),
            pltpu.VMEM((width + rank, hidden_cols), jnp.bfloat16),
            pltpu.SemaphoreType.DMA((width // tile_d,)),
        ],
        compiler_params=pltpu.CompilerParams(vmem_limit_bytes=26 << 20),
        cost_estimate=pl.CostEstimate(
            flops=4 * count * hidden_cols * width,
            bytes_accessed=4 * hidden_cols * width,
            transcendentals=0,
        ),
        name="expert",
    )(rows, slope, down_part, sketch_t, down_local, up_local, *events)


def per_device(
    cotangent,
    routes,
    gate_values,
    up_weight,
    down_weight,
    pre_activation,
    input_sketch,
    model_sketch,
    hidden_sketch,
    lengths,
):
    pieces = lax.axis_size("dp")
    sections = lax.axis_size("section")
    per_expert = pieces // EXPERTS
    place = lax.axis_index("dp")
    core = lax.axis_index("tensor")
    cot = cotangent[0]
    tok_dev, width = cot.shape
    half = tok_dev // 2
    rows = half // CHUNKS
    rank = model_sketch.shape[2]
    blocks = routes.shape[1]
    block_len = tok_dev // blocks
    sketch_local = hidden_sketch[0, 0]
    pre_all = pre_activation[0, 0]
    hidden_cols = pre_all.shape[2]
    pre_all = pre_all.reshape(pieces, 2, CHUNKS, rows, hidden_cols)

    def below(block):
        return lax.ppermute(block, "section", [(s, (s - 1) % sections) for s in range(sections)])

    token_routes = jnp.broadcast_to(routes[0][:, None, :], (blocks, block_len, 2)).reshape(
        tok_dev, 2
    )
    half_routes = lax.dynamic_slice_in_dim(token_routes, core * half, half, 0)
    half_gates = lax.dynamic_slice_in_dim(gate_values[0], core * half, half, 0)
    slot_expert = (place ^ jnp.arange(pieces, dtype=jnp.int32)) // per_expert
    hits = half_routes[:, None, :] == slot_expert[None, :, None]
    weight = jnp.sum(jnp.where(hits, half_gates[:, None, :], 0.0), axis=2)

    sketch_t = sketch_local.T
    cot_mine = lax.dynamic_slice_in_dim(cot, core * half, half, 0)
    cot_theirs = lax.dynamic_slice_in_dim(cot, (1 - core) * half, half, 0)
    order = sorted(range(2, pieces), reverse=True)
    slope, down_part, down_here = slopes(pre_all, sketch_t, down_weight[0, 0], place, core)
    near_rows = xored(cot_mine, "dp", 1)
    fetched = {slot: xored(cot_mine[:rows], "dp", slot) for slot in order}
    own, sent, grad, passed, backs = (), (), (), (), ()
    below_mine, vectors = [], []
    for a in range(CHUNKS):
        part = slice(a * rows, (a + 1) * rows)
        blocks = [fetched[slot] for slot in order] + [near_rows] * (a == 0)
        blocks = jnp.concatenate(blocks, axis=0)
        if a > 0:
            blocks = held(blocks, own)
        traded = xored(blocks, "tensor", 1)
        mine = dict(fetched)
        theirs = {slot: traded[at * rows : (at + 1) * rows] for at, slot in enumerate(order)}
        if a == 0:
            near_theirs = traded[len(order) * rows :]
        mine[0], mine[1] = cot_mine[part], near_rows[part]
        theirs[0], theirs[1] = cot_theirs[part], near_theirs[part]
        rows_in = jnp.concatenate(
            [mine[k] for k in range(pieces)] + [theirs[k] for k in range(pieces)], axis=0
        )

        kept, give = expert(
            a, rows_in, slope, down_part, sketch_t, down_here, up_weight[0, 0], *sent
        )
        if a + 1 < CHUNKS:
            coming = held(cot_mine[(a + 1) * rows : (a + 2) * rows], near_rows)
            fetched = {slot: held(xored(coming, "dp", slot), kept) for slot in order}
            give = held(give, *fetched.values(), *backs)
        else:
            give = held(give, *backs)
        own, *sent = merged(kept, xored(give, "tensor", 1), rows)
        backs = [xored(out, "dp", slot + 1) for slot, out in enumerate(sent)]
        if grad:
            passed = (below(held(*grad, backs[0])),)
            below_mine.append(*passed)
        new, vec = finished(own, cot_mine[part], weight[part], backs, *passed)
        grad = (new,)
        vectors.append(vec)
    below_mine.append(below(*grad))

    mine = jnp.concatenate(below_mine, axis=0)
    theirs = jnp.concatenate([xored(f, "tensor", 1) for f in below_mine], axis=0)
    handed = jnp.concatenate(
        [jnp.where(core == 0, mine, theirs), jnp.where(core == 0, theirs, mine)], axis=0
    )

    vec_mine = jnp.concatenate(vectors, axis=0)
    vec_theirs = xored(vec_mine, "tensor", 1)
    sketch_sum = jnp.concatenate(
        [jnp.where(core == 0, vec_mine, vec_theirs), jnp.where(core == 0, vec_theirs, vec_mine)],
        axis=0,
    )
    out_vec = jnp.dot(cot, model_sketch[0], preferred_element_type=jnp.float32)
    counts = lengths[0, 0]
    upto = jnp.arange(counts.shape[0])
    ends = jnp.sum(jnp.where(upto[None, :] <= upto[:, None], counts[None, :], 0), axis=1)
    starts = ends - counts
    position = jnp.arange(tok_dev, dtype=jnp.int32)
    member = ((position[None, :] >= starts[:, None]) & (position[None, :] < ends[:, None])).astype(
        jnp.float32
    )
    down_feat = jnp.einsum(
        "et,ta,tb->eab", member, out_vec, sketch_sum[:, :rank], precision=lax.Precision.HIGHEST
    )
    up_feat = jnp.einsum(
        "et,ta,tb->eab",
        member,
        sketch_sum[:, rank:],
        input_sketch[0],
        precision=lax.Precision.HIGHEST,
    )
    features = jnp.concatenate([down_feat, up_feat], axis=2)
    return (handed[None], features[None])


def solution(mesh):
    in_specs = (
        P("section", ("groups", "dp"), None),
        P("section", ("groups", "dp"), None),
        P("section", ("groups", "dp"), None),
        P("section", "dp", None, "tensor"),
        P("section", "dp", "tensor", None),
        P("section", ("groups", "dp"), None, None, "tensor"),
        P("section", ("groups", "dp"), None),
        P("section", None, None),
        P("section", "dp", "tensor", None),
        P("section", ("groups", "dp"), None),
    )
    out_specs = (P("section", ("groups", "dp"), None), P("section", ("groups", "dp"), None, None))
    return jax.shard_map(
        per_device, mesh=mesh, in_specs=in_specs, out_specs=out_specs, check_vma=False
    )
```

```python
import functools

import jax
import jax.numpy as jnp
from jax import lax
from jax.experimental import pallas as pl
from jax.experimental.pallas import tpu as pltpu
from jax.sharding import PartitionSpec as P

EXPERTS = 4
CHUNKS = 2
NT = (((1,), (1,)), ((), ()))


def xored(block, axis, bits):
    n = lax.axis_size(axis)
    return lax.ppermute(block, axis, [(i, i ^ bits) for i in range(n)])


ANYWHERE = pl.BlockSpec(memory_space=pl.ANY)
RESIDENT = pl.BlockSpec(memory_space=pltpu.VMEM)


def held_kernel(block_ref, *refs):
    refs[-1][...] = block_ref[...]


def held(block, *events):
    return pl.pallas_call(
        held_kernel,
        in_specs=[RESIDENT] + [ANYWHERE] * len(events),
        out_specs=RESIDENT,
        out_shape=jax.ShapeDtypeStruct(block.shape, block.dtype),
        compiler_params=pltpu.CompilerParams(vmem_limit_bytes=1 << 20),
        name="held",
    )(block, *events)


def merge_kernel(keep_ref, came_ref, own_ref, *sent_refs):
    rows = own_ref.shape[0]
    own_ref[...] = keep_ref[:rows] + came_ref[:rows].astype(jnp.float32)
    for at, sent_ref in enumerate(sent_refs):
        part = slice((at + 1) * rows, (at + 2) * rows)
        total = keep_ref[part] + came_ref[part].astype(jnp.float32)
        sent_ref[...] = total.astype(jnp.bfloat16)


def merged(keep, came, rows):
    count, wide = keep.shape
    others = count // rows - 1
    return pl.pallas_call(
        merge_kernel,
        in_specs=[RESIDENT] * 2,
        out_specs=[RESIDENT] * (1 + others),
        out_shape=[jax.ShapeDtypeStruct((rows, wide), jnp.float32)]
        + [jax.ShapeDtypeStruct((rows, wide), jnp.bfloat16)] * others,
        compiler_params=pltpu.CompilerParams(vmem_limit_bytes=4 << 20),
        cost_estimate=pl.CostEstimate(
            flops=count * wide, bytes_accessed=8 * count * wide, transcendentals=0
        ),
        name="merge",
    )(keep, came)


def finish_kernel(slots, own_ref, cot_ref, weight_ref, *refs):
    grad_ref, vec_ref = refs[-2:]
    width = grad_ref.shape[1]
    total = weight_ref[:, :1] * own_ref[...]
    for slot in range(1, slots):
        total += weight_ref[:, slot : slot + 1] * refs[slot - 1][...].astype(jnp.float32)
    grad_ref[...] = (cot_ref[...].astype(jnp.float32) + total[:, :width]).astype(jnp.bfloat16)
    vec_ref[...] = total[:, width:]


def finished(own, cot, weight, backs, *events):
    rows, wide = own.shape
    width = cot.shape[1]
    return pl.pallas_call(
        functools.partial(finish_kernel, 1 + len(backs)),
        in_specs=[RESIDENT] * (3 + len(backs)) + [ANYWHERE] * len(events),
        out_specs=[RESIDENT] * 2,
        out_shape=[
            jax.ShapeDtypeStruct((rows, width), jnp.bfloat16),
            jax.ShapeDtypeStruct((rows, wide - width), jnp.float32),
        ],
        compiler_params=pltpu.CompilerParams(vmem_limit_bytes=4 << 20),
        cost_estimate=pl.CostEstimate(
            flops=8 * rows * wide, bytes_accessed=12 * rows * wide, transcendentals=0
        ),
        name="finish",
    )(own, cot, weight, *backs, *events)


def tile_of(size, most):
    best = 128
    for tile in range(128, most + 1, 128):
        if size % tile == 0:
            best = tile
    return best


def slope_kernel(groups, index_ref, *refs):
    del index_ref
    pre_refs, sketch_ref, weight_hbm = refs[:groups], refs[groups], refs[groups + 1]
    slope_ref, down_ref, weight_ref, weight_sem = refs[-4:]
    load = pltpu.make_async_copy(weight_hbm, weight_ref, weight_sem)

    @pl.when((pl.program_id(0) == 0) & (pl.program_id(1) == 0))
    def _():
        load.start()

    pre = jnp.concatenate([r[0, 0, 0] for r in pre_refs], axis=0).astype(jnp.float32)
    sig = 0.5 + 0.5 * jnp.tanh(0.5 * pre)
    hidden = pre * sig
    slope = sig + hidden * (1.0 - sig)
    slope_ref[0] = slope.T.astype(slope_ref.dtype)
    term = lax.dot_general(
        hidden.astype(jnp.bfloat16), sketch_ref[...], NT, preferred_element_type=jnp.float32
    )

    @pl.when(pl.program_id(1) == 0)
    def _():
        down_ref[...] = jnp.zeros_like(down_ref)

    down_ref[0] += term

    @pl.when(
        (pl.program_id(0) == pl.num_programs(0) - 1) & (pl.program_id(1) == pl.num_programs(1) - 1)
    )
    def _():
        load.wait()


def slopes(pre, sketch_t, weight, place, core):
    n, _, chunks, rows, cols = pre.shape
    rank = sketch_t.shape[0]
    groups = 2 * n
    tile = tile_of(cols, 896)
    index = jnp.stack([place, core]).astype(jnp.int32)
    weight = pltpu.with_memory_space_constraint(weight, pltpu.HBM)

    def spec_of(h, slot):
        return pl.BlockSpec(
            (1, 1, 1, rows, tile), lambda a, j, ix: (ix[0] ^ slot, ix[1] ^ h, a, 0, j)
        )

    return pl.pallas_call(
        functools.partial(slope_kernel, groups),
        grid_spec=pltpu.PrefetchScalarGridSpec(
            num_scalar_prefetch=1,
            grid=(chunks, cols // tile),
            in_specs=[spec_of(h, slot) for h in range(2) for slot in range(n)]
            + [pl.BlockSpec((rank, tile), lambda a, j, ix: (0, j))]
            + [pl.BlockSpec(memory_space=pltpu.HBM)],
            out_specs=[
                pl.BlockSpec((1, tile, groups * rows), lambda a, j, ix: (a, j, 0)),
                pl.BlockSpec((1, groups * rows, rank), lambda a, j, ix: (a, 0, 0)),
                RESIDENT,
            ],
            scratch_shapes=[pltpu.SemaphoreType.DMA],
        ),
        out_shape=[
            jax.ShapeDtypeStruct((chunks, cols, groups * rows), jnp.bfloat16),
            jax.ShapeDtypeStruct((chunks, groups * rows, rank), jnp.float32),
            jax.ShapeDtypeStruct(weight.shape, weight.dtype),
        ],
        cost_estimate=pl.CostEstimate(
            flops=2 * chunks * groups * rows * cols * rank,
            bytes_accessed=4 * chunks * groups * rows * cols,
            transcendentals=chunks * groups * rows * cols,
        ),
        compiler_params=pltpu.CompilerParams(vmem_limit_bytes=7 << 20),
        name="slopes",
    )(index, *([pre] * groups), sketch_t, weight)


def expert_kernel(
    tile_f, tile_d, rows_ref, slope_ref, down_part_ref, sketch_ref, down_ref, up_hbm, *refs
):
    keep_ref, give_ref, rows_buf, grad_buf, up_buf, up_sem = refs[-6:]
    hidden_cols, width = down_ref.shape
    steps_f, steps_d = hidden_cols // tile_f, width // tile_d
    half = keep_ref.shape[0]

    def tile(j, size):
        return pl.ds(pl.multiple_of(j * size, size), size)

    def up_copy(j):
        part = tile(j, tile_d)
        return pltpu.make_async_copy(up_hbm.at[part], up_buf.at[part], up_sem.at[j])

    for j in range(steps_d):
        if j == 0 or j > steps_f:
            up_copy(j).start()
    rows_buf[...] = rows_ref[...].T

    def first(j, carry):
        @pl.when(j + 1 < steps_d)
        def _():
            up_copy(j + 1).start()

        part = tile(j, tile_f)
        grad_hidden = jnp.dot(
            down_ref[part, :], rows_buf[...], preferred_element_type=jnp.float32
        )
        slope = slope_ref[0, part, :].astype(jnp.float32)
        grad_buf[part, :] = (grad_hidden * slope).astype(jnp.bfloat16)
        return carry

    lax.fori_loop(0, steps_f, first, 0)

    up_part = jnp.dot(sketch_ref[...], grad_buf[...], preferred_element_type=jnp.float32).T
    vectors = jnp.concatenate([down_part_ref[0], up_part], axis=1)
    keep_ref[:, width:] = vectors[:half]
    give_ref[:, width:] = vectors[half:].astype(jnp.bfloat16)

    def second(j, carry):
        up_copy(j).wait()
        part = tile(j, tile_d)
        term = jnp.dot(up_buf[part, :], grad_buf[...], preferred_element_type=jnp.float32).T
        keep_ref[:, part] = term[:half]
        give_ref[:, part] = term[half:].astype(jnp.bfloat16)
        return carry

    lax.fori_loop(0, steps_d, second, 0)


def expert(chunk, rows, slope, down_part, sketch_t, down_local, up_local, *events):
    count, width = rows.shape
    hidden_cols = down_local.shape[0]
    rank = sketch_t.shape[0]
    wide = width + 2 * rank
    tile_f, tile_d = tile_of(hidden_cols, 1792), tile_of(width, 1024)
    up_local = pltpu.with_memory_space_constraint(up_local, pltpu.HBM)
    return pl.pallas_call(
        functools.partial(expert_kernel, tile_f, tile_d),
        grid=(1,),
        in_specs=[
            RESIDENT,
            pl.BlockSpec((1, hidden_cols, count), lambda i: (chunk, 0, 0)),
            pl.BlockSpec((1, count, rank), lambda i: (chunk, 0, 0)),
        ]
        + [RESIDENT] * 2
        + [pl.BlockSpec(memory_space=pltpu.HBM)]
        + [ANYWHERE] * len(events),
        out_specs=[RESIDENT] * 2,
        out_shape=[
            jax.ShapeDtypeStruct((count // 2, wide), jnp.float32),
            jax.ShapeDtypeStruct((count // 2, wide), jnp.bfloat16),
        ],
        scratch_shapes=[
            pltpu.VMEM((width, count), jnp.bfloat16),
            pltpu.VMEM((hidden_cols, count), jnp.bfloat16),
            pltpu.VMEM((width, hidden_cols), jnp.bfloat16),
            pltpu.SemaphoreType.DMA((width // tile_d,)),
        ],
        compiler_params=pltpu.CompilerParams(vmem_limit_bytes=26 << 20),
        cost_estimate=pl.CostEstimate(
            flops=4 * count * hidden_cols * width,
            bytes_accessed=4 * hidden_cols * width,
            transcendentals=0,
        ),
        name="expert",
    )(rows, slope, down_part, sketch_t, down_local, up_local, *events)


def per_device(
    cotangent,
    routes,
    gate_values,
    up_weight,
    down_weight,
    pre_activation,
    input_sketch,
    model_sketch,
    hidden_sketch,
    lengths,
):
    pieces = lax.axis_size("dp")
    sections = lax.axis_size("section")
    per_expert = pieces // EXPERTS
    place = lax.axis_index("dp")
    core = lax.axis_index("tensor")
    cot = cotangent[0]
    tok_dev, width = cot.shape
    half = tok_dev // 2
    rows = half // CHUNKS
    rank = model_sketch.shape[2]
    blocks = routes.shape[1]
    block_len = tok_dev // blocks
    sketch_local = hidden_sketch[0, 0]
    pre_all = pre_activation[0, 0]
    hidden_cols = pre_all.shape[2]
    pre_all = pre_all.reshape(pieces, 2, CHUNKS, rows, hidden_cols)

    def below(block):
        return lax.ppermute(block, "section", [(s, (s - 1) % sections) for s in range(sections)])

    token_routes = jnp.broadcast_to(routes[0][:, None, :], (blocks, block_len, 2)).reshape(
        tok_dev, 2
    )
    half_routes = lax.dynamic_slice_in_dim(token_routes, core * half, half, 0)
    half_gates = lax.dynamic_slice_in_dim(gate_values[0], core * half, half, 0)
    slot_expert = (place ^ jnp.arange(pieces, dtype=jnp.int32)) // per_expert
    hits = half_routes[:, None, :] == slot_expert[None, :, None]
    weight = jnp.sum(jnp.where(hits, half_gates[:, None, :], 0.0), axis=2)

    sketch_t = sketch_local.T
    cot_mine = lax.dynamic_slice_in_dim(cot, core * half, half, 0)
    cot_theirs = lax.dynamic_slice_in_dim(cot, (1 - core) * half, half, 0)
    order = sorted(range(2, pieces), reverse=True)
    slope, down_part, down_here = slopes(pre_all, sketch_t, down_weight[0, 0], place, core)
    near_rows = xored(cot_mine, "dp", 1)
    fetched = {slot: xored(cot_mine[:rows], "dp", slot) for slot in order}
    own, sent, grad, passed, backs = (), (), (), (), ()
    below_mine, vectors = [], []
    for a in range(CHUNKS):
        part = slice(a * rows, (a + 1) * rows)
        blocks = [fetched[slot] for slot in order] + [near_rows] * (a == 0)
        blocks = jnp.concatenate(blocks, axis=0)
        if a > 0:
            blocks = held(blocks, own)
        traded = xored(blocks, "tensor", 1)
        mine = dict(fetched)
        theirs = {slot: traded[at * rows : (at + 1) * rows] for at, slot in enumerate(order)}
        if a == 0:
            near_theirs = traded[len(order) * rows :]
        mine[0], mine[1] = cot_mine[part], near_rows[part]
        theirs[0], theirs[1] = cot_theirs[part], near_theirs[part]
        rows_in = jnp.concatenate(
            [mine[k] for k in range(pieces)] + [theirs[k] for k in range(pieces)], axis=0
        )

        kept, give = expert(
            a, rows_in, slope, down_part, sketch_t, down_here, up_weight[0, 0], *sent
        )
        if a + 1 < CHUNKS:
            coming = held(cot_mine[(a + 1) * rows : (a + 2) * rows], near_rows)
            fetched = {slot: held(xored(coming, "dp", slot), kept) for slot in order}
            give = held(give, *fetched.values(), *backs)
        else:
            give = held(give, *backs)
        own, *sent = merged(kept, xored(give, "tensor", 1), rows)
        backs = [xored(out, "dp", slot + 1) for slot, out in enumerate(sent)]
        if grad:
            passed = (below(held(*grad, backs[0])),)
            below_mine.append(*passed)
        new, vec = finished(own, cot_mine[part], weight[part], backs, *passed)
        grad = (new,)
        vectors.append(vec)
    below_mine.append(below(*grad))

    mine = jnp.concatenate(below_mine, axis=0)
    theirs = jnp.concatenate([xored(f, "tensor", 1) for f in below_mine], axis=0)
    handed = jnp.concatenate(
        [jnp.where(core == 0, mine, theirs), jnp.where(core == 0, theirs, mine)], axis=0
    )

    vec_mine = jnp.concatenate(vectors, axis=0)
    vec_theirs = xored(vec_mine, "tensor", 1)
    sketch_sum = jnp.concatenate(
        [jnp.where(core == 0, vec_mine, vec_theirs), jnp.where(core == 0, vec_theirs, vec_mine)],
        axis=0,
    )
    out_vec = jnp.dot(cot, model_sketch[0], preferred_element_type=jnp.float32)
    counts = lengths[0, 0]
    upto = jnp.arange(counts.shape[0])
    ends = jnp.sum(jnp.where(upto[None, :] <= upto[:, None], counts[None, :], 0), axis=1)
    starts = ends - counts
    position = jnp.arange(tok_dev, dtype=jnp.int32)
    member = ((position[None, :] >= starts[:, None]) & (position[None, :] < ends[:, None])).astype(
        jnp.float32
    )
    down_feat = jnp.einsum(
        "et,ta,tb->eab", member, out_vec, sketch_sum[:, :rank], precision=lax.Precision.HIGHEST
    )
    up_feat = jnp.einsum(
        "et,ta,tb->eab",
        member,
        sketch_sum[:, rank:],
        input_sketch[0],
        precision=lax.Precision.HIGHEST,
    )
    features = jnp.concatenate([down_feat, up_feat], axis=2)
    return (handed[None], features[None])


def solution(mesh):
    in_specs = (
        P("section", ("groups", "dp"), None),
        P("section", ("groups", "dp"), None),
        P("section", ("groups", "dp"), None),
        P("section", "dp", None, "tensor"),
        P("section", "dp", "tensor", None),
        P("section", ("groups", "dp"), None, None, "tensor"),
        P("section", ("groups", "dp"), None),
        P("section", None, None),
        P("section", "dp", "tensor", None),
        P("section", ("groups", "dp"), None),
    )
    out_specs = (P("section", ("groups", "dp"), None), P("section", ("groups", "dp"), None, None))
    return jax.shard_map(
        per_device, mesh=mesh, in_specs=in_specs, out_specs=out_specs, check_vma=False
    )
```

```python
import functools

import jax
import jax.numpy as jnp
from jax import lax
from jax.experimental import pallas as pl
from jax.experimental.pallas import tpu as pltpu
from jax.sharding import PartitionSpec as P

EXPERTS = 4
CHUNKS = 2
NT = (((1,), (1,)), ((), ()))


def xored(block, axis, bits):
    n = lax.axis_size(axis)
    return lax.ppermute(block, axis, [(i, i ^ bits) for i in range(n)])


ANYWHERE = pl.BlockSpec(memory_space=pl.ANY)
RESIDENT = pl.BlockSpec(memory_space=pltpu.VMEM)


def halves_kernel(core_ref, cot_ref, mine_ref, theirs_ref, first_ref):
    half = mine_ref.shape[0]
    for h, out_ref in enumerate((mine_ref, theirs_ref)):
        start = pl.multiple_of((core_ref[0] ^ h) * half, half)
        out_ref[...] = cot_ref[pl.ds(start, half), :]
    start = pl.multiple_of(core_ref[0] * half, half)
    first_ref[...] = cot_ref[pl.ds(start, first_ref.shape[0]), :]


def halves(cot, core, rows):
    tok_dev, width = cot.shape
    cot = pltpu.with_memory_space_constraint(cot, pltpu.HBM)
    counts = (tok_dev // 2, tok_dev // 2, rows)
    return pl.pallas_call(
        halves_kernel,
        grid_spec=pltpu.PrefetchScalarGridSpec(
            num_scalar_prefetch=1,
            grid=(1,),
            in_specs=[pl.BlockSpec((tok_dev, width), lambda i, core: (0, 0))],
            out_specs=[RESIDENT] * 3,
        ),
        out_shape=[jax.ShapeDtypeStruct((count, width), cot.dtype) for count in counts],
        compiler_params=pltpu.CompilerParams(vmem_limit_bytes=4 << 20),
        name="halves",
    )(core.astype(jnp.int32).reshape(1), cot)


def held_kernel(block_ref, *refs):
    refs[-1][...] = block_ref[...]


def held(block, *events):
    return pl.pallas_call(
        held_kernel,
        in_specs=[RESIDENT] + [ANYWHERE] * len(events),
        out_specs=RESIDENT,
        out_shape=jax.ShapeDtypeStruct(block.shape, block.dtype),
        compiler_params=pltpu.CompilerParams(vmem_limit_bytes=1 << 20),
        name="held",
    )(block, *events)


def merge_kernel(keep_ref, came_ref, own_ref, *sent_refs):
    rows = own_ref.shape[0]
    own_ref[...] = keep_ref[:rows] + came_ref[:rows].astype(jnp.float32)
    for at, sent_ref in enumerate(sent_refs):
        part = slice((at + 1) * rows, (at + 2) * rows)
        total = keep_ref[part] + came_ref[part].astype(jnp.float32)
        sent_ref[...] = total.astype(jnp.bfloat16)


def merged(keep, came, rows):
    count, wide = keep.shape
    others = count // rows - 1
    return pl.pallas_call(
        merge_kernel,
        in_specs=[RESIDENT] * 2,
        out_specs=[RESIDENT] * (1 + others),
        out_shape=[jax.ShapeDtypeStruct((rows, wide), jnp.float32)]
        + [jax.ShapeDtypeStruct((rows, wide), jnp.bfloat16)] * others,
        compiler_params=pltpu.CompilerParams(vmem_limit_bytes=4 << 20),
        cost_estimate=pl.CostEstimate(
            flops=count * wide, bytes_accessed=8 * count * wide, transcendentals=0
        ),
        name="merge",
    )(keep, came)


def finish_kernel(slots, own_ref, cot_ref, weight_ref, *refs):
    grad_ref, vec_ref = refs[-2:]
    width = grad_ref.shape[1]
    total = weight_ref[:, :1] * own_ref[...]
    for slot in range(1, slots):
        back = refs[slots - 1 - slot][...].astype(jnp.float32)
        total += weight_ref[:, slot : slot + 1] * back
    grad_ref[...] = (cot_ref[...].astype(jnp.float32) + total[:, :width]).astype(jnp.bfloat16)
    vec_ref[...] = total[:, width:]


def finished(own, cot, weight, backs, *events):
    rows, wide = own.shape
    width = cot.shape[1]
    return pl.pallas_call(
        functools.partial(finish_kernel, 1 + len(backs)),
        in_specs=[RESIDENT] * (3 + len(backs)) + [ANYWHERE] * len(events),
        out_specs=[RESIDENT] * 2,
        out_shape=[
            jax.ShapeDtypeStruct((rows, width), jnp.bfloat16),
            jax.ShapeDtypeStruct((rows, wide - width), jnp.float32),
        ],
        compiler_params=pltpu.CompilerParams(vmem_limit_bytes=4 << 20),
        cost_estimate=pl.CostEstimate(
            flops=8 * rows * wide, bytes_accessed=12 * rows * wide, transcendentals=0
        ),
        name="finish",
    )(own, cot, weight, *backs, *events)


def tile_of(size, most):
    best = 128
    for tile in range(128, most + 1, 128):
        if size % tile == 0:
            best = tile
    return best


def slope_kernel(groups, index_ref, *refs):
    del index_ref
    pre_refs, sketch_ref, weight_hbm = refs[:groups], refs[groups], refs[groups + 1]
    slope_ref, down_ref, weight_ref, weight_sem = refs[-4:]
    load = pltpu.make_async_copy(weight_hbm, weight_ref, weight_sem)

    @pl.when((pl.program_id(0) == 0) & (pl.program_id(1) == 0))
    def _():
        load.start()

    pre = jnp.concatenate([r[0, 0, 0] for r in pre_refs], axis=0).astype(jnp.float32)
    sig = 0.5 + 0.5 * jnp.tanh(0.5 * pre)
    hidden = pre * sig
    slope = sig + hidden * (1.0 - sig)
    slope_ref[0] = slope.T.astype(slope_ref.dtype)
    term = lax.dot_general(
        hidden.astype(jnp.bfloat16), sketch_ref[...], NT, preferred_element_type=jnp.float32
    )

    @pl.when(pl.program_id(1) == 0)
    def _():
        down_ref[...] = jnp.zeros_like(down_ref)

    down_ref[0] += term

    @pl.when(
        (pl.program_id(0) == pl.num_programs(0) - 1) & (pl.program_id(1) == pl.num_programs(1) - 1)
    )
    def _():
        load.wait()


def slopes(pre, sketch_t, weight, place, core):
    n, _, chunks, rows, cols = pre.shape
    rank = sketch_t.shape[0]
    groups = 2 * n
    tile = tile_of(cols, 896)
    index = jnp.stack([place, core]).astype(jnp.int32)
    weight = pltpu.with_memory_space_constraint(weight, pltpu.HBM)

    def spec_of(h, slot):
        return pl.BlockSpec(
            (1, 1, 1, rows, tile), lambda a, j, ix: (ix[0] ^ slot, ix[1] ^ h, a, 0, j)
        )

    return pl.pallas_call(
        functools.partial(slope_kernel, groups),
        grid_spec=pltpu.PrefetchScalarGridSpec(
            num_scalar_prefetch=1,
            grid=(chunks, cols // tile),
            in_specs=[spec_of(h, slot) for h in range(2) for slot in range(n)]
            + [pl.BlockSpec((rank, tile), lambda a, j, ix: (0, j))]
            + [pl.BlockSpec(memory_space=pltpu.HBM)],
            out_specs=[
                pl.BlockSpec((1, tile, groups * rows), lambda a, j, ix: (a, j, 0)),
                pl.BlockSpec((1, groups * rows, rank), lambda a, j, ix: (a, 0, 0)),
                RESIDENT,
            ],
            scratch_shapes=[pltpu.SemaphoreType.DMA],
        ),
        out_shape=[
            jax.ShapeDtypeStruct((chunks, cols, groups * rows), jnp.bfloat16),
            jax.ShapeDtypeStruct((chunks, groups * rows, rank), jnp.float32),
            jax.ShapeDtypeStruct(weight.shape, weight.dtype),
        ],
        cost_estimate=pl.CostEstimate(
            flops=2 * chunks * groups * rows * cols * rank,
            bytes_accessed=4 * chunks * groups * rows * cols,
            transcendentals=chunks * groups * rows * cols,
        ),
        compiler_params=pltpu.CompilerParams(vmem_limit_bytes=7 << 20),
        name="slopes",
    )(index, *([pre] * groups), sketch_t, weight)


def expert_kernel(
    tile_f, tile_d, rows_ref, slope_ref, down_part_ref, sketch_ref, down_ref, up_hbm, *refs
):
    keep_ref, give_ref, rows_buf, grad_buf, up_buf, up_sem = refs[-6:]
    hidden_cols, width = down_ref.shape
    steps_f, steps_d = hidden_cols // tile_f, width // tile_d
    half = keep_ref.shape[0]

    def tile(j, size):
        return pl.ds(pl.multiple_of(j * size, size), size)

    def up_copy(j):
        part = tile(j, tile_d)
        return pltpu.make_async_copy(up_hbm.at[part], up_buf.at[part], up_sem.at[j])

    for j in range(steps_d):
        if j == 0 or j > steps_f:
            up_copy(j).start()
    rows_buf[...] = rows_ref[...].T

    def first(j, carry):
        @pl.when(j + 1 < steps_d)
        def _():
            up_copy(j + 1).start()

        part = tile(j, tile_f)
        grad_hidden = jnp.dot(
            down_ref[part, :], rows_buf[...], preferred_element_type=jnp.float32
        )
        slope = slope_ref[0, part, :].astype(jnp.float32)
        grad_buf[part, :] = (grad_hidden * slope).astype(jnp.bfloat16)
        return carry

    lax.fori_loop(0, steps_f, first, 0)

    up_part = jnp.dot(sketch_ref[...], grad_buf[...], preferred_element_type=jnp.float32).T
    vectors = jnp.concatenate([down_part_ref[0], up_part], axis=1)
    keep_ref[:, width:] = vectors[:half]
    give_ref[:, width:] = vectors[half:].astype(jnp.bfloat16)

    def second(j, carry):
        up_copy(j).wait()
        part = tile(j, tile_d)
        term = jnp.dot(up_buf[part, :], grad_buf[...], preferred_element_type=jnp.float32).T
        keep_ref[:, part] = term[:half]
        give_ref[:, part] = term[half:].astype(jnp.bfloat16)
        return carry

    lax.fori_loop(0, steps_d, second, 0)


def expert(chunk, rows, slope, down_part, sketch_t, down_local, up_local, *events):
    count, width = rows.shape
    hidden_cols = down_local.shape[0]
    rank = sketch_t.shape[0]
    wide = width + 2 * rank
    tile_f, tile_d = tile_of(hidden_cols, 1792), tile_of(width, 1024)
    up_local = pltpu.with_memory_space_constraint(up_local, pltpu.HBM)
    return pl.pallas_call(
        functools.partial(expert_kernel, tile_f, tile_d),
        grid=(1,),
        in_specs=[
            RESIDENT,
            pl.BlockSpec((1, hidden_cols, count), lambda i: (chunk, 0, 0)),
            pl.BlockSpec((1, count, rank), lambda i: (chunk, 0, 0)),
        ]
        + [RESIDENT] * 2
        + [pl.BlockSpec(memory_space=pltpu.HBM)]
        + [ANYWHERE] * len(events),
        out_specs=[RESIDENT] * 2,
        out_shape=[
            jax.ShapeDtypeStruct((count // 2, wide), jnp.float32),
            jax.ShapeDtypeStruct((count // 2, wide), jnp.bfloat16),
        ],
        scratch_shapes=[
            pltpu.VMEM((width, count), jnp.bfloat16),
            pltpu.VMEM((hidden_cols, count), jnp.bfloat16),
            pltpu.VMEM((width, hidden_cols), jnp.bfloat16),
            pltpu.SemaphoreType.DMA((width // tile_d,)),
        ],
        compiler_params=pltpu.CompilerParams(vmem_limit_bytes=26 << 20),
        cost_estimate=pl.CostEstimate(
            flops=4 * count * hidden_cols * width,
            bytes_accessed=4 * hidden_cols * width,
            transcendentals=0,
        ),
        name="expert",
    )(rows, slope, down_part, sketch_t, down_local, up_local, *events)


def per_device(
    cotangent,
    routes,
    gate_values,
    up_weight,
    down_weight,
    pre_activation,
    input_sketch,
    model_sketch,
    hidden_sketch,
    lengths,
):
    pieces = lax.axis_size("dp")
    sections = lax.axis_size("section")
    per_expert = pieces // EXPERTS
    place = lax.axis_index("dp")
    core = lax.axis_index("tensor")
    cot = cotangent[0]
    tok_dev, width = cot.shape
    half = tok_dev // 2
    rows = half // CHUNKS
    rank = model_sketch.shape[2]
    blocks = routes.shape[1]
    block_len = tok_dev // blocks
    sketch_local = hidden_sketch[0, 0]
    pre_all = pre_activation[0, 0]
    hidden_cols = pre_all.shape[2]
    pre_all = pre_all.reshape(pieces, 2, CHUNKS, rows, hidden_cols)

    def below(block):
        return lax.ppermute(block, "section", [(s, (s - 1) % sections) for s in range(sections)])

    token_routes = jnp.broadcast_to(routes[0][:, None, :], (blocks, block_len, 2)).reshape(
        tok_dev, 2
    )
    half_routes = lax.dynamic_slice_in_dim(token_routes, core * half, half, 0)
    half_gates = lax.dynamic_slice_in_dim(gate_values[0], core * half, half, 0)
    slot_expert = (place ^ jnp.arange(pieces, dtype=jnp.int32)) // per_expert
    hits = half_routes[:, None, :] == slot_expert[None, :, None]
    weight = jnp.sum(jnp.where(hits, half_gates[:, None, :], 0.0), axis=2)

    sketch_t = sketch_local.T
    cot_mine, cot_theirs, cot_first = halves(cot, core, rows)
    order = sorted(range(2, pieces), reverse=True)
    slope, down_part, down_here = slopes(pre_all, sketch_t, down_weight[0, 0], place, core)
    near_rows = xored(cot_mine, "dp", 1)
    fetched = {slot: xored(cot_first, "dp", slot) for slot in order}
    own, sent, grad, passed, backs = (), (), (), (), ()
    below_mine, vectors = [], []
    for a in range(CHUNKS):
        part = slice(a * rows, (a + 1) * rows)
        blocks = [fetched[slot] for slot in order] + [near_rows] * (a == 0)
        blocks = jnp.concatenate(blocks, axis=0)
        if a > 0:
            blocks = held(blocks, own)
        traded = xored(blocks, "tensor", 1)
        mine = dict(fetched)
        theirs = {slot: traded[at * rows : (at + 1) * rows] for at, slot in enumerate(order)}
        if a == 0:
            near_theirs = traded[len(order) * rows :]
        mine[0], mine[1] = cot_mine[part], near_rows[part]
        theirs[0], theirs[1] = cot_theirs[part], near_theirs[part]
        rows_in = jnp.concatenate(
            [mine[k] for k in range(pieces)] + [theirs[k] for k in range(pieces)], axis=0
        )

        kept, give = expert(
            a, rows_in, slope, down_part, sketch_t, down_here, up_weight[0, 0], *sent
        )
        if a + 1 < CHUNKS:
            coming = held(cot_mine[(a + 1) * rows : (a + 2) * rows], *fetched.values())
            fetched = {slot: held(xored(coming, "dp", slot), kept) for slot in order}
            give = held(give, *fetched.values(), *backs)
        else:
            give = held(give, *backs)
        own, *sent = merged(kept, xored(give, "tensor", 1), rows)
        backs = [xored(out, "dp", slot + 1) for slot, out in enumerate(sent)][::-1]
        if grad:
            passed = (below(held(*grad, own)),)
            below_mine.append(*passed)
        new, vec = finished(own, cot_mine[part], weight[part], backs, *passed)
        grad = (new,)
        vectors.append(vec)
    below_mine.append(below(*grad))

    mine = jnp.concatenate(below_mine, axis=0)
    theirs = [held(block, *grad) for block in below_mine[:-1]] + below_mine[-1:]
    theirs = jnp.concatenate([xored(block, "tensor", 1) for block in theirs], axis=0)
    handed = jnp.concatenate(
        [jnp.where(core == 0, mine, theirs), jnp.where(core == 0, theirs, mine)], axis=0
    )

    vec_mine = jnp.concatenate(vectors, axis=0)
    vec_theirs = xored(vec_mine, "tensor", 1)
    sketch_sum = jnp.concatenate(
        [jnp.where(core == 0, vec_mine, vec_theirs), jnp.where(core == 0, vec_theirs, vec_mine)],
        axis=0,
    )
    out_vec = jnp.dot(cot, model_sketch[0], preferred_element_type=jnp.float32)
    counts = lengths[0, 0]
    upto = jnp.arange(counts.shape[0])
    ends = jnp.sum(jnp.where(upto[None, :] <= upto[:, None], counts[None, :], 0), axis=1)
    starts = ends - counts
    position = jnp.arange(tok_dev, dtype=jnp.int32)
    member = ((position[None, :] >= starts[:, None]) & (position[None, :] < ends[:, None])).astype(
        jnp.float32
    )
    down_feat = jnp.einsum(
        "et,ta,tb->eab", member, out_vec, sketch_sum[:, :rank], precision=lax.Precision.HIGHEST
    )
    up_feat = jnp.einsum(
        "et,ta,tb->eab",
        member,
        sketch_sum[:, rank:],
        input_sketch[0],
        precision=lax.Precision.HIGHEST,
    )
    features = jnp.concatenate([down_feat, up_feat], axis=2)
    return (handed[None], features[None])


def solution(mesh):
    in_specs = (
        P("section", ("groups", "dp"), None),
        P("section", ("groups", "dp"), None),
        P("section", ("groups", "dp"), None),
        P("section", "dp", None, "tensor"),
        P("section", "dp", "tensor", None),
        P("section", ("groups", "dp"), None, None, "tensor"),
        P("section", ("groups", "dp"), None),
        P("section", None, None),
        P("section", "dp", "tensor", None),
        P("section", ("groups", "dp"), None),
    )
    out_specs = (P("section", ("groups", "dp"), None), P("section", ("groups", "dp"), None, None))
    return jax.shard_map(
        per_device, mesh=mesh, in_specs=in_specs, out_specs=out_specs, check_vma=False
    )
```

```python
import functools

import jax
import jax.numpy as jnp
from jax import lax
from jax.experimental import pallas as pl
from jax.experimental.pallas import tpu as pltpu
from jax.sharding import PartitionSpec as P

EXPERTS = 4
CHUNKS = 2
NT = (((1,), (1,)), ((), ()))


def xored(block, axis, bits):
    n = lax.axis_size(axis)
    return lax.ppermute(block, axis, [(i, i ^ bits) for i in range(n)])


ANYWHERE = pl.BlockSpec(memory_space=pl.ANY)
RESIDENT = pl.BlockSpec(memory_space=pltpu.VMEM)


def held_kernel(block_ref, *refs):
    refs[-1][...] = block_ref[...]


def held(block, *events):
    return pl.pallas_call(
        held_kernel,
        in_specs=[RESIDENT] + [ANYWHERE] * len(events),
        out_specs=RESIDENT,
        out_shape=jax.ShapeDtypeStruct(block.shape, block.dtype),
        compiler_params=pltpu.CompilerParams(vmem_limit_bytes=1 << 20),
        name="held",
    )(block, *events)


def merge_kernel(keep_ref, came_ref, own_ref, *sent_refs):
    rows = own_ref.shape[0]
    own_ref[...] = keep_ref[:rows] + came_ref[:rows].astype(jnp.float32)
    for at, sent_ref in enumerate(sent_refs):
        part = slice((at + 1) * rows, (at + 2) * rows)
        total = keep_ref[part] + came_ref[part].astype(jnp.float32)
        sent_ref[...] = total.astype(jnp.bfloat16)


def merged(keep, came, rows):
    count, wide = keep.shape
    others = count // rows - 1
    return pl.pallas_call(
        merge_kernel,
        in_specs=[RESIDENT] * 2,
        out_specs=[RESIDENT] * (1 + others),
        out_shape=[jax.ShapeDtypeStruct((rows, wide), jnp.float32)]
        + [jax.ShapeDtypeStruct((rows, wide), jnp.bfloat16)] * others,
        compiler_params=pltpu.CompilerParams(vmem_limit_bytes=4 << 20),
        cost_estimate=pl.CostEstimate(
            flops=count * wide, bytes_accessed=8 * count * wide, transcendentals=0
        ),
        name="merge",
    )(keep, came)


def finish_kernel(slots, own_ref, cot_ref, weight_ref, *refs):
    grad_ref, vec_ref = refs[-2:]
    width = grad_ref.shape[1]
    total = weight_ref[:, :1] * own_ref[...]
    for slot in range(1, slots):
        back = refs[slots - 1 - slot][...].astype(jnp.float32)
        total += weight_ref[:, slot : slot + 1] * back
    grad_ref[...] = (cot_ref[...].astype(jnp.float32) + total[:, :width]).astype(jnp.bfloat16)
    vec_ref[...] = total[:, width:]


def finished(own, cot, weight, backs, *events):
    rows, wide = own.shape
    width = cot.shape[1]
    return pl.pallas_call(
        functools.partial(finish_kernel, 1 + len(backs)),
        in_specs=[RESIDENT] * (3 + len(backs)) + [ANYWHERE] * len(events),
        out_specs=[RESIDENT] * 2,
        out_shape=[
            jax.ShapeDtypeStruct((rows, width), jnp.bfloat16),
            jax.ShapeDtypeStruct((rows, wide - width), jnp.float32),
        ],
        compiler_params=pltpu.CompilerParams(vmem_limit_bytes=4 << 20),
        cost_estimate=pl.CostEstimate(
            flops=8 * rows * wide, bytes_accessed=12 * rows * wide, transcendentals=0
        ),
        name="finish",
    )(own, cot, weight, *backs, *events)


def tile_of(size, most):
    best = 128
    for tile in range(128, most + 1, 128):
        if size % tile == 0:
            best = tile
    return best


def slope_kernel(groups, index_ref, *refs):
    del index_ref
    pre_refs, sketch_ref, weight_hbm = refs[:groups], refs[groups], refs[groups + 1]
    slope_ref, down_ref, weight_ref, weight_sem = refs[-4:]
    load = pltpu.make_async_copy(weight_hbm, weight_ref, weight_sem)

    @pl.when((pl.program_id(0) == 0) & (pl.program_id(1) == 0))
    def _():
        load.start()

    pre = jnp.concatenate([r[0, 0, 0] for r in pre_refs], axis=0).astype(jnp.float32)
    sig = 0.5 + 0.5 * jnp.tanh(0.5 * pre)
    hidden = pre * sig
    slope = sig + hidden * (1.0 - sig)
    slope_ref[0] = slope.T.astype(slope_ref.dtype)
    term = lax.dot_general(
        hidden.astype(jnp.bfloat16), sketch_ref[...], NT, preferred_element_type=jnp.float32
    )

    @pl.when(pl.program_id(1) == 0)
    def _():
        down_ref[...] = jnp.zeros_like(down_ref)

    down_ref[0] += term

    @pl.when(
        (pl.program_id(0) == pl.num_programs(0) - 1) & (pl.program_id(1) == pl.num_programs(1) - 1)
    )
    def _():
        load.wait()


def slopes(pre, sketch_t, weight, place, core):
    n, _, chunks, rows, cols = pre.shape
    rank = sketch_t.shape[0]
    groups = 2 * n
    tile = tile_of(cols, 896)
    index = jnp.stack([place, core]).astype(jnp.int32)
    weight = pltpu.with_memory_space_constraint(weight, pltpu.HBM)

    def spec_of(h, slot):
        return pl.BlockSpec(
            (1, 1, 1, rows, tile), lambda a, j, ix: (ix[0] ^ slot, ix[1] ^ h, a, 0, j)
        )

    return pl.pallas_call(
        functools.partial(slope_kernel, groups),
        grid_spec=pltpu.PrefetchScalarGridSpec(
            num_scalar_prefetch=1,
            grid=(chunks, cols // tile),
            in_specs=[spec_of(h, slot) for h in range(2) for slot in range(n)]
            + [pl.BlockSpec((rank, tile), lambda a, j, ix: (0, j))]
            + [pl.BlockSpec(memory_space=pltpu.HBM)],
            out_specs=[
                pl.BlockSpec((1, tile, groups * rows), lambda a, j, ix: (a, j, 0)),
                pl.BlockSpec((1, groups * rows, rank), lambda a, j, ix: (a, 0, 0)),
                RESIDENT,
            ],
            scratch_shapes=[pltpu.SemaphoreType.DMA],
        ),
        out_shape=[
            jax.ShapeDtypeStruct((chunks, cols, groups * rows), jnp.bfloat16),
            jax.ShapeDtypeStruct((chunks, groups * rows, rank), jnp.float32),
            jax.ShapeDtypeStruct(weight.shape, weight.dtype),
        ],
        cost_estimate=pl.CostEstimate(
            flops=2 * chunks * groups * rows * cols * rank,
            bytes_accessed=4 * chunks * groups * rows * cols,
            transcendentals=chunks * groups * rows * cols,
        ),
        compiler_params=pltpu.CompilerParams(vmem_limit_bytes=7 << 20),
        name="slopes",
    )(index, *([pre] * groups), sketch_t, weight)


def expert_kernel(
    tile_f, tile_d, rows_ref, slope_ref, down_part_ref, sketch_ref, down_ref, up_hbm, *refs
):
    keep_ref, give_ref, rows_buf, grad_buf, up_buf, up_sem = refs[-6:]
    hidden_cols, width = down_ref.shape
    steps_f, steps_d = hidden_cols // tile_f, width // tile_d
    half = keep_ref.shape[0]

    def tile(j, size):
        return pl.ds(pl.multiple_of(j * size, size), size)

    def up_copy(j):
        part = tile(j, tile_d)
        return pltpu.make_async_copy(up_hbm.at[part], up_buf.at[part], up_sem.at[j])

    for j in range(steps_d):
        if j == 0 or j > steps_f:
            up_copy(j).start()
    rows_buf[...] = rows_ref[...].T

    def first(j, carry):
        @pl.when(j + 1 < steps_d)
        def _():
            up_copy(j + 1).start()

        part = tile(j, tile_f)
        grad_hidden = jnp.dot(
            down_ref[part, :], rows_buf[...], preferred_element_type=jnp.float32
        )
        slope = slope_ref[0, part, :].astype(jnp.float32)
        grad_buf[part, :] = (grad_hidden * slope).astype(jnp.bfloat16)
        return carry

    lax.fori_loop(0, steps_f, first, 0)

    up_part = jnp.dot(sketch_ref[...], grad_buf[...], preferred_element_type=jnp.float32).T
    vectors = jnp.concatenate([down_part_ref[0], up_part], axis=1)
    keep_ref[:, width:] = vectors[:half]
    give_ref[:, width:] = vectors[half:].astype(jnp.bfloat16)

    def second(j, carry):
        up_copy(j).wait()
        part = tile(j, tile_d)
        term = jnp.dot(up_buf[part, :], grad_buf[...], preferred_element_type=jnp.float32).T
        keep_ref[:, part] = term[:half]
        give_ref[:, part] = term[half:].astype(jnp.bfloat16)
        return carry

    lax.fori_loop(0, steps_d, second, 0)


def expert(chunk, rows, slope, down_part, sketch_t, down_local, up_local, *events):
    count, width = rows.shape
    hidden_cols = down_local.shape[0]
    rank = sketch_t.shape[0]
    wide = width + 2 * rank
    tile_f, tile_d = tile_of(hidden_cols, 1792), tile_of(width, 1024)
    up_local = pltpu.with_memory_space_constraint(up_local, pltpu.HBM)
    return pl.pallas_call(
        functools.partial(expert_kernel, tile_f, tile_d),
        grid=(1,),
        in_specs=[
            RESIDENT,
            pl.BlockSpec((1, hidden_cols, count), lambda i: (chunk, 0, 0)),
            pl.BlockSpec((1, count, rank), lambda i: (chunk, 0, 0)),
        ]
        + [RESIDENT] * 2
        + [pl.BlockSpec(memory_space=pltpu.HBM)]
        + [ANYWHERE] * len(events),
        out_specs=[RESIDENT] * 2,
        out_shape=[
            jax.ShapeDtypeStruct((count // 2, wide), jnp.float32),
            jax.ShapeDtypeStruct((count // 2, wide), jnp.bfloat16),
        ],
        scratch_shapes=[
            pltpu.VMEM((width, count), jnp.bfloat16),
            pltpu.VMEM((hidden_cols, count), jnp.bfloat16),
            pltpu.VMEM((width, hidden_cols), jnp.bfloat16),
            pltpu.SemaphoreType.DMA((width // tile_d,)),
        ],
        compiler_params=pltpu.CompilerParams(vmem_limit_bytes=26 << 20),
        cost_estimate=pl.CostEstimate(
            flops=4 * count * hidden_cols * width,
            bytes_accessed=4 * hidden_cols * width,
            transcendentals=0,
        ),
        name="expert",
    )(rows, slope, down_part, sketch_t, down_local, up_local, *events)


def per_device(
    cotangent,
    routes,
    gate_values,
    up_weight,
    down_weight,
    pre_activation,
    input_sketch,
    model_sketch,
    hidden_sketch,
    lengths,
):
    pieces = lax.axis_size("dp")
    sections = lax.axis_size("section")
    per_expert = pieces // EXPERTS
    place = lax.axis_index("dp")
    core = lax.axis_index("tensor")
    cot = cotangent[0]
    tok_dev, width = cot.shape
    half = tok_dev // 2
    rows = half // CHUNKS
    rank = model_sketch.shape[2]
    blocks = routes.shape[1]
    block_len = tok_dev // blocks
    sketch_local = hidden_sketch[0, 0]
    pre_all = pre_activation[0, 0]
    hidden_cols = pre_all.shape[2]
    pre_all = pre_all.reshape(pieces, 2, CHUNKS, rows, hidden_cols)

    def below(block):
        return lax.ppermute(block, "section", [(s, (s - 1) % sections) for s in range(sections)])

    token_routes = jnp.broadcast_to(routes[0][:, None, :], (blocks, block_len, 2)).reshape(
        tok_dev, 2
    )
    half_routes = lax.dynamic_slice_in_dim(token_routes, core * half, half, 0)
    half_gates = lax.dynamic_slice_in_dim(gate_values[0], core * half, half, 0)
    slot_expert = (place ^ jnp.arange(pieces, dtype=jnp.int32)) // per_expert
    hits = half_routes[:, None, :] == slot_expert[None, :, None]
    weight = jnp.sum(jnp.where(hits, half_gates[:, None, :], 0.0), axis=2)

    sketch_t = sketch_local.T
    cot_mine = lax.dynamic_slice_in_dim(cot, core * half, half, 0)
    cot_theirs = lax.dynamic_slice_in_dim(cot, (1 - core) * half, half, 0)
    order = sorted(range(2, pieces), reverse=True)
    slope, down_part, down_here = slopes(pre_all, sketch_t, down_weight[0, 0], place, core)
    near_rows = xored(cot_mine, "dp", 1)
    fetched = {slot: xored(cot_mine[:rows], "dp", slot) for slot in order}
    own, sent, grad, passed, backs = (), (), (), (), ()
    below_mine, vectors = [], []
    for a in range(CHUNKS):
        part = slice(a * rows, (a + 1) * rows)
        blocks = [fetched[slot] for slot in order] + [near_rows] * (a == 0)
        blocks = jnp.concatenate(blocks, axis=0)
        if a > 0:
            blocks = held(blocks, own)
        traded = xored(blocks, "tensor", 1)
        mine = dict(fetched)
        theirs = {slot: traded[at * rows : (at + 1) * rows] for at, slot in enumerate(order)}
        if a == 0:
            near_theirs = traded[len(order) * rows :]
        mine[0], mine[1] = cot_mine[part], near_rows[part]
        theirs[0], theirs[1] = cot_theirs[part], near_theirs[part]
        rows_in = jnp.concatenate(
            [mine[k] for k in range(pieces)] + [theirs[k] for k in range(pieces)], axis=0
        )

        kept, give = expert(
            a, rows_in, slope, down_part, sketch_t, down_here, up_weight[0, 0], *sent
        )
        if a + 1 < CHUNKS:
            coming = held(cot_mine[(a + 1) * rows : (a + 2) * rows], near_rows)
            fetched = {slot: held(xored(coming, "dp", slot), kept) for slot in order}
            give = held(give, *fetched.values(), *backs)
        else:
            give = held(give, *backs)
        own, *sent = merged(kept, xored(give, "tensor", 1), rows)
        backs = [xored(out, "dp", slot + 1) for slot, out in enumerate(sent)][::-1]
        if grad:
            passed = (below(held(*grad, backs[0])),)
            below_mine.append(*passed)
        new, vec = finished(own, cot_mine[part], weight[part], backs, *passed)
        grad = (new,)
        vectors.append(vec)
    below_mine.append(below(*grad))

    mine = jnp.concatenate(below_mine, axis=0)
    theirs = jnp.concatenate([xored(f, "tensor", 1) for f in below_mine], axis=0)
    handed = jnp.concatenate(
        [jnp.where(core == 0, mine, theirs), jnp.where(core == 0, theirs, mine)], axis=0
    )

    vec_mine = jnp.concatenate(vectors, axis=0)
    vec_theirs = xored(vec_mine, "tensor", 1)
    sketch_sum = jnp.concatenate(
        [jnp.where(core == 0, vec_mine, vec_theirs), jnp.where(core == 0, vec_theirs, vec_mine)],
        axis=0,
    )
    out_vec = jnp.dot(cot, model_sketch[0], preferred_element_type=jnp.float32)
    counts = lengths[0, 0]
    upto = jnp.arange(counts.shape[0])
    ends = jnp.sum(jnp.where(upto[None, :] <= upto[:, None], counts[None, :], 0), axis=1)
    starts = ends - counts
    position = jnp.arange(tok_dev, dtype=jnp.int32)
    member = ((position[None, :] >= starts[:, None]) & (position[None, :] < ends[:, None])).astype(
        jnp.float32
    )
    down_feat = jnp.einsum(
        "et,ta,tb->eab", member, out_vec, sketch_sum[:, :rank], precision=lax.Precision.HIGHEST
    )
    up_feat = jnp.einsum(
        "et,ta,tb->eab",
        member,
        sketch_sum[:, rank:],
        input_sketch[0],
        precision=lax.Precision.HIGHEST,
    )
    features = jnp.concatenate([down_feat, up_feat], axis=2)
    return (handed[None], features[None])


def solution(mesh):
    in_specs = (
        P("section", ("groups", "dp"), None),
        P("section", ("groups", "dp"), None),
        P("section", ("groups", "dp"), None),
        P("section", "dp", None, "tensor"),
        P("section", "dp", "tensor", None),
        P("section", ("groups", "dp"), None, None, "tensor"),
        P("section", ("groups", "dp"), None),
        P("section", None, None),
        P("section", "dp", "tensor", None),
        P("section", ("groups", "dp"), None),
    )
    out_specs = (P("section", ("groups", "dp"), None), P("section", ("groups", "dp"), None, None))
    return jax.shard_map(
        per_device, mesh=mesh, in_specs=in_specs, out_specs=out_specs, check_vma=False
    )
```

```python
import functools

import jax
import jax.numpy as jnp
from jax import lax
from jax.experimental import pallas as pl
from jax.experimental.pallas import tpu as pltpu
from jax.sharding import PartitionSpec as P

EXPERTS = 4
CHUNKS = 2
NT = (((1,), (1,)), ((), ()))


def xored(block, axis, bits):
    n = lax.axis_size(axis)
    return lax.ppermute(block, axis, [(i, i ^ bits) for i in range(n)])


ANYWHERE = pl.BlockSpec(memory_space=pl.ANY)
RESIDENT = pl.BlockSpec(memory_space=pltpu.VMEM)


def held_kernel(block_ref, *refs):
    refs[-1][...] = block_ref[...]


def held(block, *events):
    return pl.pallas_call(
        held_kernel,
        in_specs=[RESIDENT] + [ANYWHERE] * len(events),
        out_specs=RESIDENT,
        out_shape=jax.ShapeDtypeStruct(block.shape, block.dtype),
        compiler_params=pltpu.CompilerParams(vmem_limit_bytes=1 << 20),
        name="held",
    )(block, *events)


def merge_kernel(keep_ref, came_ref, own_ref, *sent_refs):
    rows = own_ref.shape[0]
    own_ref[...] = keep_ref[:rows] + came_ref[:rows].astype(jnp.float32)
    for at, sent_ref in enumerate(sent_refs):
        part = slice((at + 1) * rows, (at + 2) * rows)
        total = keep_ref[part] + came_ref[part].astype(jnp.float32)
        sent_ref[...] = total.astype(jnp.bfloat16)


def merged(keep, came, rows):
    count, wide = keep.shape
    others = count // rows - 1
    return pl.pallas_call(
        merge_kernel,
        in_specs=[RESIDENT] * 2,
        out_specs=[RESIDENT] * (1 + others),
        out_shape=[jax.ShapeDtypeStruct((rows, wide), jnp.float32)]
        + [jax.ShapeDtypeStruct((rows, wide), jnp.bfloat16)] * others,
        compiler_params=pltpu.CompilerParams(vmem_limit_bytes=4 << 20),
        cost_estimate=pl.CostEstimate(
            flops=count * wide, bytes_accessed=8 * count * wide, transcendentals=0
        ),
        name="merge",
    )(keep, came)


def finish_kernel(slots, own_ref, cot_ref, weight_ref, *refs):
    grad_ref, vec_ref = refs[-2:]
    width = grad_ref.shape[1]
    total = weight_ref[:, :1] * own_ref[...]
    for slot in range(1, slots):
        back = refs[slots - 1 - slot][...].astype(jnp.float32)
        total += weight_ref[:, slot : slot + 1] * back
    grad_ref[...] = (cot_ref[...].astype(jnp.float32) + total[:, :width]).astype(jnp.bfloat16)
    vec_ref[...] = total[:, width:]


def finished(own, cot, weight, backs, *events):
    rows, wide = own.shape
    width = cot.shape[1]
    return pl.pallas_call(
        functools.partial(finish_kernel, 1 + len(backs)),
        in_specs=[RESIDENT] * (3 + len(backs)) + [ANYWHERE] * len(events),
        out_specs=[RESIDENT] * 2,
        out_shape=[
            jax.ShapeDtypeStruct((rows, width), jnp.bfloat16),
            jax.ShapeDtypeStruct((rows, wide - width), jnp.float32),
        ],
        compiler_params=pltpu.CompilerParams(vmem_limit_bytes=4 << 20),
        cost_estimate=pl.CostEstimate(
            flops=8 * rows * wide, bytes_accessed=12 * rows * wide, transcendentals=0
        ),
        name="finish",
    )(own, cot, weight, *backs, *events)


def tile_of(size, most):
    best = 128
    for tile in range(128, most + 1, 128):
        if size % tile == 0:
            best = tile
    return best


def slope_kernel(groups, index_ref, *refs):
    del index_ref
    pre_refs, sketch_ref, weight_hbm = refs[:groups], refs[groups], refs[groups + 1]
    slope_ref, down_ref, weight_ref, weight_sem = refs[-4:]
    load = pltpu.make_async_copy(weight_hbm, weight_ref, weight_sem)

    @pl.when((pl.program_id(0) == 0) & (pl.program_id(1) == 0))
    def _():
        load.start()

    pre = jnp.concatenate([r[0, 0, 0] for r in pre_refs], axis=0).astype(jnp.float32)
    sig = 0.5 + 0.5 * jnp.tanh(0.5 * pre)
    hidden = pre * sig
    slope = sig + hidden * (1.0 - sig)
    slope_ref[0] = slope.T.astype(slope_ref.dtype)
    term = lax.dot_general(
        hidden.astype(jnp.bfloat16), sketch_ref[...], NT, preferred_element_type=jnp.float32
    )

    @pl.when(pl.program_id(1) == 0)
    def _():
        down_ref[...] = jnp.zeros_like(down_ref)

    down_ref[0] += term

    @pl.when(
        (pl.program_id(0) == pl.num_programs(0) - 1) & (pl.program_id(1) == pl.num_programs(1) - 1)
    )
    def _():
        load.wait()


def slopes(pre, sketch_t, weight, place, core):
    n, _, chunks, rows, cols = pre.shape
    rank = sketch_t.shape[0]
    groups = 2 * n
    tile = tile_of(cols, 896)
    index = jnp.stack([place, core]).astype(jnp.int32)
    weight = pltpu.with_memory_space_constraint(weight, pltpu.HBM)

    def spec_of(h, slot):
        return pl.BlockSpec(
            (1, 1, 1, rows, tile), lambda a, j, ix: (ix[0] ^ slot, ix[1] ^ h, a, 0, j)
        )

    return pl.pallas_call(
        functools.partial(slope_kernel, groups),
        grid_spec=pltpu.PrefetchScalarGridSpec(
            num_scalar_prefetch=1,
            grid=(chunks, cols // tile),
            in_specs=[spec_of(h, slot) for h in range(2) for slot in range(n)]
            + [pl.BlockSpec((rank, tile), lambda a, j, ix: (0, j))]
            + [pl.BlockSpec(memory_space=pltpu.HBM)],
            out_specs=[
                pl.BlockSpec((1, tile, groups * rows), lambda a, j, ix: (a, j, 0)),
                pl.BlockSpec((1, groups * rows, rank), lambda a, j, ix: (a, 0, 0)),
                RESIDENT,
            ],
            scratch_shapes=[pltpu.SemaphoreType.DMA],
        ),
        out_shape=[
            jax.ShapeDtypeStruct((chunks, cols, groups * rows), jnp.bfloat16),
            jax.ShapeDtypeStruct((chunks, groups * rows, rank), jnp.float32),
            jax.ShapeDtypeStruct(weight.shape, weight.dtype),
        ],
        cost_estimate=pl.CostEstimate(
            flops=2 * chunks * groups * rows * cols * rank,
            bytes_accessed=4 * chunks * groups * rows * cols,
            transcendentals=chunks * groups * rows * cols,
        ),
        compiler_params=pltpu.CompilerParams(vmem_limit_bytes=7 << 20),
        name="slopes",
    )(index, *([pre] * groups), sketch_t, weight)


def expert_kernel(
    tile_f, tile_d, rows_ref, slope_ref, down_part_ref, sketch_ref, down_ref, up_hbm, *refs
):
    keep_ref, give_ref, rows_buf, grad_buf, up_buf, up_sem = refs[-6:]
    hidden_cols, width = down_ref.shape
    steps_f, steps_d = hidden_cols // tile_f, width // tile_d
    half = keep_ref.shape[0]

    def tile(j, size):
        return pl.ds(pl.multiple_of(j * size, size), size)

    def up_copy(j):
        part = tile(j, tile_d)
        return pltpu.make_async_copy(up_hbm.at[part], up_buf.at[part], up_sem.at[j])

    for j in range(steps_d):
        if j == 0 or j > steps_f:
            up_copy(j).start()
    rows_buf[...] = rows_ref[...].T

    def first(j, carry):
        @pl.when(j + 1 < steps_d)
        def _():
            up_copy(j + 1).start()

        part = tile(j, tile_f)
        grad_hidden = jnp.dot(
            down_ref[part, :], rows_buf[...], preferred_element_type=jnp.float32
        )
        slope = slope_ref[0, part, :].astype(jnp.float32)
        grad_buf[part, :] = (grad_hidden * slope).astype(jnp.bfloat16)
        return carry

    lax.fori_loop(0, steps_f, first, 0)

    up_part = jnp.dot(sketch_ref[...], grad_buf[...], preferred_element_type=jnp.float32).T
    vectors = jnp.concatenate([down_part_ref[0], up_part], axis=1)
    keep_ref[:, width:] = vectors[:half]
    give_ref[:, width:] = vectors[half:].astype(jnp.bfloat16)

    def second(j, carry):
        up_copy(j).wait()
        part = tile(j, tile_d)
        term = jnp.dot(up_buf[part, :], grad_buf[...], preferred_element_type=jnp.float32).T
        keep_ref[:, part] = term[:half]
        give_ref[:, part] = term[half:].astype(jnp.bfloat16)
        return carry

    lax.fori_loop(0, steps_d, second, 0)


def expert(chunk, rows, slope, down_part, sketch_t, down_local, up_local, *events):
    count, width = rows.shape
    hidden_cols = down_local.shape[0]
    rank = sketch_t.shape[0]
    wide = width + 2 * rank
    tile_f, tile_d = tile_of(hidden_cols, 1792), tile_of(width, 1024)
    up_local = pltpu.with_memory_space_constraint(up_local, pltpu.HBM)
    return pl.pallas_call(
        functools.partial(expert_kernel, tile_f, tile_d),
        grid=(1,),
        in_specs=[
            RESIDENT,
            pl.BlockSpec((1, hidden_cols, count), lambda i: (chunk, 0, 0)),
            pl.BlockSpec((1, count, rank), lambda i: (chunk, 0, 0)),
        ]
        + [RESIDENT] * 2
        + [pl.BlockSpec(memory_space=pltpu.HBM)]
        + [ANYWHERE] * len(events),
        out_specs=[RESIDENT] * 2,
        out_shape=[
            jax.ShapeDtypeStruct((count // 2, wide), jnp.float32),
            jax.ShapeDtypeStruct((count // 2, wide), jnp.bfloat16),
        ],
        scratch_shapes=[
            pltpu.VMEM((width, count), jnp.bfloat16),
            pltpu.VMEM((hidden_cols, count), jnp.bfloat16),
            pltpu.VMEM((width, hidden_cols), jnp.bfloat16),
            pltpu.SemaphoreType.DMA((width // tile_d,)),
        ],
        compiler_params=pltpu.CompilerParams(vmem_limit_bytes=26 << 20),
        cost_estimate=pl.CostEstimate(
            flops=4 * count * hidden_cols * width,
            bytes_accessed=4 * hidden_cols * width,
            transcendentals=0,
        ),
        name="expert",
    )(rows, slope, down_part, sketch_t, down_local, up_local, *events)


def per_device(
    cotangent,
    routes,
    gate_values,
    up_weight,
    down_weight,
    pre_activation,
    input_sketch,
    model_sketch,
    hidden_sketch,
    lengths,
):
    pieces = lax.axis_size("dp")
    sections = lax.axis_size("section")
    per_expert = pieces // EXPERTS
    place = lax.axis_index("dp")
    core = lax.axis_index("tensor")
    cot = cotangent[0]
    tok_dev, width = cot.shape
    half = tok_dev // 2
    rows = half // CHUNKS
    rank = model_sketch.shape[2]
    blocks = routes.shape[1]
    block_len = tok_dev // blocks
    sketch_local = hidden_sketch[0, 0]
    pre_all = pre_activation[0, 0]
    hidden_cols = pre_all.shape[2]
    pre_all = pre_all.reshape(pieces, 2, CHUNKS, rows, hidden_cols)

    def below(block):
        return lax.ppermute(block, "section", [(s, (s - 1) % sections) for s in range(sections)])

    token_routes = jnp.broadcast_to(routes[0][:, None, :], (blocks, block_len, 2)).reshape(
        tok_dev, 2
    )
    half_routes = lax.dynamic_slice_in_dim(token_routes, core * half, half, 0)
    half_gates = lax.dynamic_slice_in_dim(gate_values[0], core * half, half, 0)
    slot_expert = (place ^ jnp.arange(pieces, dtype=jnp.int32)) // per_expert
    hits = half_routes[:, None, :] == slot_expert[None, :, None]
    weight = jnp.sum(jnp.where(hits, half_gates[:, None, :], 0.0), axis=2)

    sketch_t = sketch_local.T
    cot_mine = lax.optimization_barrier(lax.dynamic_slice_in_dim(cot, core * half, half, 0))
    cot_theirs = lax.dynamic_slice_in_dim(cot, (1 - core) * half, half, 0)
    order = sorted(range(2, pieces), reverse=True)
    slope, down_part, down_here = slopes(pre_all, sketch_t, down_weight[0, 0], place, core)
    near_rows = xored(cot_mine, "dp", 1)
    fetched = {slot: xored(cot_mine[:rows], "dp", slot) for slot in order}
    own, sent, grad, passed, backs = (), (), (), (), ()
    below_mine, vectors = [], []
    for a in range(CHUNKS):
        part = slice(a * rows, (a + 1) * rows)
        blocks = [fetched[slot] for slot in order] + [near_rows] * (a == 0)
        blocks = jnp.concatenate(blocks, axis=0)
        if a > 0:
            blocks = held(blocks, own)
        traded = xored(blocks, "tensor", 1)
        mine = dict(fetched)
        theirs = {slot: traded[at * rows : (at + 1) * rows] for at, slot in enumerate(order)}
        if a == 0:
            near_theirs = traded[len(order) * rows :]
        mine[0], mine[1] = cot_mine[part], near_rows[part]
        theirs[0], theirs[1] = cot_theirs[part], near_theirs[part]
        rows_in = jnp.concatenate(
            [mine[k] for k in range(pieces)] + [theirs[k] for k in range(pieces)], axis=0
        )

        kept, give = expert(
            a, rows_in, slope, down_part, sketch_t, down_here, up_weight[0, 0], *sent
        )
        if a + 1 < CHUNKS:
            coming = held(cot_mine[(a + 1) * rows : (a + 2) * rows], near_rows)
            fetched = {slot: held(xored(coming, "dp", slot), kept) for slot in order}
            give = held(give, *fetched.values(), *backs)
        else:
            give = held(give, *backs)
        own, *sent = merged(kept, xored(give, "tensor", 1), rows)
        backs = [xored(out, "dp", slot + 1) for slot, out in enumerate(sent)][::-1]
        if grad:
            passed = (below(held(*grad, backs[0])),)
            below_mine.append(*passed)
        new, vec = finished(own, cot_mine[part], weight[part], backs, *passed)
        grad = (new,)
        vectors.append(vec)
    below_mine.append(below(*grad))

    mine = jnp.concatenate(below_mine, axis=0)
    theirs = jnp.concatenate([xored(f, "tensor", 1) for f in below_mine], axis=0)
    handed = jnp.concatenate(
        [jnp.where(core == 0, mine, theirs), jnp.where(core == 0, theirs, mine)], axis=0
    )

    vec_mine = jnp.concatenate(vectors, axis=0)
    vec_theirs = xored(vec_mine, "tensor", 1)
    sketch_sum = jnp.concatenate(
        [jnp.where(core == 0, vec_mine, vec_theirs), jnp.where(core == 0, vec_theirs, vec_mine)],
        axis=0,
    )
    out_vec = jnp.dot(cot, model_sketch[0], preferred_element_type=jnp.float32)
    counts = lengths[0, 0]
    upto = jnp.arange(counts.shape[0])
    ends = jnp.sum(jnp.where(upto[None, :] <= upto[:, None], counts[None, :], 0), axis=1)
    starts = ends - counts
    position = jnp.arange(tok_dev, dtype=jnp.int32)
    member = ((position[None, :] >= starts[:, None]) & (position[None, :] < ends[:, None])).astype(
        jnp.float32
    )
    down_feat = jnp.einsum(
        "et,ta,tb->eab", member, out_vec, sketch_sum[:, :rank], precision=lax.Precision.HIGHEST
    )
    up_feat = jnp.einsum(
        "et,ta,tb->eab",
        member,
        sketch_sum[:, rank:],
        input_sketch[0],
        precision=lax.Precision.HIGHEST,
    )
    features = jnp.concatenate([down_feat, up_feat], axis=2)
    return (handed[None], features[None])


def solution(mesh):
    in_specs = (
        P("section", ("groups", "dp"), None),
        P("section", ("groups", "dp"), None),
        P("section", ("groups", "dp"), None),
        P("section", "dp", None, "tensor"),
        P("section", "dp", "tensor", None),
        P("section", ("groups", "dp"), None, None, "tensor"),
        P("section", ("groups", "dp"), None),
        P("section", None, None),
        P("section", "dp", "tensor", None),
        P("section", ("groups", "dp"), None),
    )
    out_specs = (P("section", ("groups", "dp"), None), P("section", ("groups", "dp"), None, None))
    return jax.shard_map(
        per_device, mesh=mesh, in_specs=in_specs, out_specs=out_specs, check_vma=False
    )
```

```python
import functools

import jax
import jax.numpy as jnp
from jax import lax
from jax.experimental import pallas as pl
from jax.experimental.pallas import tpu as pltpu
from jax.sharding import PartitionSpec as P

EXPERTS = 4
CHUNKS = 2
NT = (((1,), (1,)), ((), ()))


def xored(block, axis, bits):
    n = lax.axis_size(axis)
    return lax.ppermute(block, axis, [(i, i ^ bits) for i in range(n)])


ANYWHERE = pl.BlockSpec(memory_space=pl.ANY)
RESIDENT = pl.BlockSpec(memory_space=pltpu.VMEM)


def held_kernel(block_ref, *refs):
    refs[-1][...] = block_ref[...]


def held(block, *events):
    return pl.pallas_call(
        held_kernel,
        in_specs=[RESIDENT] + [ANYWHERE] * len(events),
        out_specs=RESIDENT,
        out_shape=jax.ShapeDtypeStruct(block.shape, block.dtype),
        compiler_params=pltpu.CompilerParams(vmem_limit_bytes=1 << 20),
        name="held",
    )(block, *events)


def merge_kernel(others, keep_ref, came_ref, *refs):
    own_ref, *sent_refs = refs[-1 - others :]
    rows = own_ref.shape[0]
    own_ref[...] = keep_ref[:rows] + came_ref[:rows].astype(jnp.float32)
    for at, sent_ref in enumerate(sent_refs):
        part = slice((at + 1) * rows, (at + 2) * rows)
        total = keep_ref[part] + came_ref[part].astype(jnp.float32)
        sent_ref[...] = total.astype(jnp.bfloat16)


def merged(keep, came, rows, *events):
    count, wide = keep.shape
    others = count // rows - 1
    return pl.pallas_call(
        functools.partial(merge_kernel, others),
        in_specs=[RESIDENT] * 2 + [ANYWHERE] * len(events),
        out_specs=[RESIDENT] * (1 + others),
        out_shape=[jax.ShapeDtypeStruct((rows, wide), jnp.float32)]
        + [jax.ShapeDtypeStruct((rows, wide), jnp.bfloat16)] * others,
        compiler_params=pltpu.CompilerParams(vmem_limit_bytes=4 << 20),
        cost_estimate=pl.CostEstimate(
            flops=count * wide, bytes_accessed=8 * count * wide, transcendentals=0
        ),
        name="merge",
    )(keep, came, *events)


def finish_kernel(slots, own_ref, cot_ref, weight_ref, *refs):
    grad_ref, vec_ref = refs[-2:]
    width = grad_ref.shape[1]
    total = weight_ref[:, :1] * own_ref[...]
    for slot in range(1, slots):
        back = refs[slots - 1 - slot][...].astype(jnp.float32)
        total += weight_ref[:, slot : slot + 1] * back
    grad_ref[...] = (cot_ref[...].astype(jnp.float32) + total[:, :width]).astype(jnp.bfloat16)
    vec_ref[...] = total[:, width:]


def finished(own, cot, weight, backs, *events):
    rows, wide = own.shape
    width = cot.shape[1]
    return pl.pallas_call(
        functools.partial(finish_kernel, 1 + len(backs)),
        in_specs=[RESIDENT] * (3 + len(backs)) + [ANYWHERE] * len(events),
        out_specs=[RESIDENT] * 2,
        out_shape=[
            jax.ShapeDtypeStruct((rows, width), jnp.bfloat16),
            jax.ShapeDtypeStruct((rows, wide - width), jnp.float32),
        ],
        compiler_params=pltpu.CompilerParams(vmem_limit_bytes=4 << 20),
        cost_estimate=pl.CostEstimate(
            flops=8 * rows * wide, bytes_accessed=12 * rows * wide, transcendentals=0
        ),
        name="finish",
    )(own, cot, weight, *backs, *events)


def place_kernel(cuts, index_ref, *refs):
    out_ref, sems = refs[-2:]
    half = out_ref.shape[0] // 2
    rows = half // cuts
    copies = []
    for at, block_ref in enumerate(refs[: 2 * cuts]):
        h, cut = at // cuts, at % cuts
        start = pl.multiple_of((index_ref[1] ^ h) * half + cut * rows, rows)
        copies.append(
            pltpu.make_async_copy(block_ref, out_ref.at[pl.ds(start, rows)], sems.at[at])
        )
    for copy in copies:
        copy.start()
    for copy in copies:
        copy.wait()


def placed(index, mine, theirs):
    cuts, (rows, width) = len(mine), mine[0].shape
    return pl.pallas_call(
        functools.partial(place_kernel, cuts),
        in_specs=[pl.BlockSpec(memory_space=pltpu.SMEM)] + [RESIDENT] * (2 * cuts),
        out_specs=ANYWHERE,
        out_shape=jax.ShapeDtypeStruct((2 * cuts * rows, width), mine[0].dtype),
        scratch_shapes=[pltpu.SemaphoreType.DMA((2 * cuts,))],
        compiler_params=pltpu.CompilerParams(vmem_limit_bytes=1 << 20),
        name="place",
    )(index, *mine, *theirs)


def tile_of(size, most):
    best = 128
    for tile in range(128, most + 1, 128):
        if size % tile == 0:
            best = tile
    return best


def slope_kernel(groups, index_ref, *refs):
    del index_ref
    pre_refs, sketch_ref, weight_hbm = refs[:groups], refs[groups], refs[groups + 1]
    slope_ref, down_ref, weight_ref, weight_sem = refs[-4:]
    load = pltpu.make_async_copy(weight_hbm, weight_ref, weight_sem)

    @pl.when((pl.program_id(0) == 0) & (pl.program_id(1) == 0))
    def _():
        load.start()

    pre = jnp.concatenate([r[0, 0, 0] for r in pre_refs], axis=0).astype(jnp.float32)
    sig = 0.5 + 0.5 * jnp.tanh(0.5 * pre)
    hidden = pre * sig
    slope = sig + hidden * (1.0 - sig)
    slope_ref[0] = slope.T.astype(slope_ref.dtype)
    term = lax.dot_general(
        hidden.astype(jnp.bfloat16), sketch_ref[...], NT, preferred_element_type=jnp.float32
    )

    @pl.when(pl.program_id(1) == 0)
    def _():
        down_ref[...] = jnp.zeros_like(down_ref)

    down_ref[0] += term

    @pl.when(
        (pl.program_id(0) == pl.num_programs(0) - 1) & (pl.program_id(1) == pl.num_programs(1) - 1)
    )
    def _():
        load.wait()


def slopes(pre, sketch_t, weight, place, core):
    n, _, chunks, rows, cols = pre.shape
    rank = sketch_t.shape[0]
    groups = 2 * n
    tile = tile_of(cols, 896)
    index = jnp.stack([place, core]).astype(jnp.int32)
    weight = pltpu.with_memory_space_constraint(weight, pltpu.HBM)

    def spec_of(h, slot):
        return pl.BlockSpec(
            (1, 1, 1, rows, tile), lambda a, j, ix: (ix[0] ^ slot, ix[1] ^ h, a, 0, j)
        )

    return pl.pallas_call(
        functools.partial(slope_kernel, groups),
        grid_spec=pltpu.PrefetchScalarGridSpec(
            num_scalar_prefetch=1,
            grid=(chunks, cols // tile),
            in_specs=[spec_of(h, slot) for h in range(2) for slot in range(n)]
            + [pl.BlockSpec((rank, tile), lambda a, j, ix: (0, j))]
            + [pl.BlockSpec(memory_space=pltpu.HBM)],
            out_specs=[
                pl.BlockSpec((1, tile, groups * rows), lambda a, j, ix: (a, j, 0)),
                pl.BlockSpec((1, groups * rows, rank), lambda a, j, ix: (a, 0, 0)),
                RESIDENT,
            ],
            scratch_shapes=[pltpu.SemaphoreType.DMA],
        ),
        out_shape=[
            jax.ShapeDtypeStruct((chunks, cols, groups * rows), jnp.bfloat16),
            jax.ShapeDtypeStruct((chunks, groups * rows, rank), jnp.float32),
            jax.ShapeDtypeStruct(weight.shape, weight.dtype),
        ],
        cost_estimate=pl.CostEstimate(
            flops=2 * chunks * groups * rows * cols * rank,
            bytes_accessed=4 * chunks * groups * rows * cols,
            transcendentals=chunks * groups * rows * cols,
        ),
        compiler_params=pltpu.CompilerParams(vmem_limit_bytes=7 << 20),
        name="slopes",
    )(index, *([pre] * groups), sketch_t, weight)


def expert_kernel(
    tile_f, tile_d, rows_ref, slope_ref, down_part_ref, sketch_ref, down_ref, up_hbm, *refs
):
    keep_ref, give_ref, rows_buf, grad_buf, up_buf, up_sem = refs[-6:]
    hidden_cols, width = down_ref.shape
    steps_f, steps_d = hidden_cols // tile_f, width // tile_d
    half = keep_ref.shape[0]

    def tile(j, size):
        return pl.ds(pl.multiple_of(j * size, size), size)

    def up_copy(j):
        part = tile(j, tile_d)
        return pltpu.make_async_copy(up_hbm.at[part], up_buf.at[part], up_sem.at[j])

    for j in range(steps_d):
        if j == 0 or j > steps_f:
            up_copy(j).start()
    rows_buf[...] = rows_ref[...].T

    def first(j, carry):
        @pl.when(j + 1 < steps_d)
        def _():
            up_copy(j + 1).start()

        part = tile(j, tile_f)
        grad_hidden = jnp.dot(
            down_ref[part, :], rows_buf[...], preferred_element_type=jnp.float32
        )
        slope = slope_ref[0, part, :].astype(jnp.float32)
        grad_buf[part, :] = (grad_hidden * slope).astype(jnp.bfloat16)
        return carry

    lax.fori_loop(0, steps_f, first, 0)

    up_part = jnp.dot(sketch_ref[...], grad_buf[...], preferred_element_type=jnp.float32).T
    vectors = jnp.concatenate([down_part_ref[0], up_part], axis=1)
    keep_ref[:, width:] = vectors[:half]
    give_ref[:, width:] = vectors[half:].astype(jnp.bfloat16)

    def second(j, carry):
        up_copy(j).wait()
        part = tile(j, tile_d)
        term = jnp.dot(up_buf[part, :], grad_buf[...], preferred_element_type=jnp.float32).T
        keep_ref[:, part] = term[:half]
        give_ref[:, part] = term[half:].astype(jnp.bfloat16)
        return carry

    lax.fori_loop(0, steps_d, second, 0)


def expert(chunk, rows, slope, down_part, sketch_t, down_local, up_local, *events):
    count, width = rows.shape
    hidden_cols = down_local.shape[0]
    rank = sketch_t.shape[0]
    wide = width + 2 * rank
    tile_f, tile_d = tile_of(hidden_cols, 1792), tile_of(width, 1024)
    up_local = pltpu.with_memory_space_constraint(up_local, pltpu.HBM)
    return pl.pallas_call(
        functools.partial(expert_kernel, tile_f, tile_d),
        grid=(1,),
        in_specs=[
            RESIDENT,
            pl.BlockSpec((1, hidden_cols, count), lambda i: (chunk, 0, 0)),
            pl.BlockSpec((1, count, rank), lambda i: (chunk, 0, 0)),
        ]
        + [RESIDENT] * 2
        + [pl.BlockSpec(memory_space=pltpu.HBM)]
        + [ANYWHERE] * len(events),
        out_specs=[RESIDENT] * 2,
        out_shape=[
            jax.ShapeDtypeStruct((count // 2, wide), jnp.float32),
            jax.ShapeDtypeStruct((count // 2, wide), jnp.bfloat16),
        ],
        scratch_shapes=[
            pltpu.VMEM((width, count), jnp.bfloat16),
            pltpu.VMEM((hidden_cols, count), jnp.bfloat16),
            pltpu.VMEM((width, hidden_cols), jnp.bfloat16),
            pltpu.SemaphoreType.DMA((width // tile_d,)),
        ],
        compiler_params=pltpu.CompilerParams(vmem_limit_bytes=26 << 20),
        cost_estimate=pl.CostEstimate(
            flops=4 * count * hidden_cols * width,
            bytes_accessed=4 * hidden_cols * width,
            transcendentals=0,
        ),
        name="expert",
    )(rows, slope, down_part, sketch_t, down_local, up_local, *events)


def per_device(
    cotangent,
    routes,
    gate_values,
    up_weight,
    down_weight,
    pre_activation,
    input_sketch,
    model_sketch,
    hidden_sketch,
    lengths,
):
    pieces = lax.axis_size("dp")
    sections = lax.axis_size("section")
    per_expert = pieces // EXPERTS
    place = lax.axis_index("dp")
    core = lax.axis_index("tensor")
    cot = cotangent[0]
    tok_dev, width = cot.shape
    half = tok_dev // 2
    rows = half // CHUNKS
    rank = model_sketch.shape[2]
    blocks = routes.shape[1]
    block_len = tok_dev // blocks
    sketch_local = hidden_sketch[0, 0]
    pre_all = pre_activation[0, 0]
    hidden_cols = pre_all.shape[2]
    pre_all = pre_all.reshape(pieces, 2, CHUNKS, rows, hidden_cols)

    def below(block):
        return lax.ppermute(block, "section", [(s, (s - 1) % sections) for s in range(sections)])

    token_routes = jnp.broadcast_to(routes[0][:, None, :], (blocks, block_len, 2)).reshape(
        tok_dev, 2
    )
    half_routes = lax.dynamic_slice_in_dim(token_routes, core * half, half, 0)
    half_gates = lax.dynamic_slice_in_dim(gate_values[0], core * half, half, 0)
    slot_expert = (place ^ jnp.arange(pieces, dtype=jnp.int32)) // per_expert
    hits = half_routes[:, None, :] == slot_expert[None, :, None]
    weight = jnp.sum(jnp.where(hits, half_gates[:, None, :], 0.0), axis=2)

    sketch_t = sketch_local.T
    cot_mine = lax.dynamic_slice_in_dim(cot, core * half, half, 0)
    cot_theirs = lax.dynamic_slice_in_dim(cot, (1 - core) * half, half, 0)
    order = sorted(range(2, pieces), reverse=True)
    slope, down_part, down_here = slopes(pre_all, sketch_t, down_weight[0, 0], place, core)
    near_rows = xored(cot_mine, "dp", 1)
    fetched = {slot: xored(cot_mine[:rows], "dp", slot) for slot in order}
    own, sent, grad, passed, backs = (), (), (), (), ()
    below_mine, vectors = [], []
    for a in range(CHUNKS):
        part = slice(a * rows, (a + 1) * rows)
        blocks = [fetched[slot] for slot in order] + [near_rows] * (a == 0)
        blocks = jnp.concatenate(blocks, axis=0)
        if a > 0:
            blocks = held(blocks, own)
        traded = xored(blocks, "tensor", 1)
        mine = dict(fetched)
        theirs = {slot: traded[at * rows : (at + 1) * rows] for at, slot in enumerate(order)}
        if a == 0:
            near_theirs = traded[len(order) * rows :]
        mine[0], mine[1] = cot_mine[part], near_rows[part]
        theirs[0], theirs[1] = cot_theirs[part], near_theirs[part]
        rows_in = jnp.concatenate(
            [mine[k] for k in range(pieces)] + [theirs[k] for k in range(pieces)], axis=0
        )

        kept, give = expert(
            a, rows_in, slope, down_part, sketch_t, down_here, up_weight[0, 0], *sent
        )
        if a + 1 < CHUNKS:
            coming = held(cot_mine[(a + 1) * rows : (a + 2) * rows], near_rows)
            fetched = {slot: held(xored(coming, "dp", slot), kept) for slot in order}
            late = tuple(fetched.values())
        else:
            give, late = held(give, *backs), ()
        own, *sent = merged(kept, xored(give, "tensor", 1), rows, *late)
        backs = [xored(out, "dp", slot + 1) for slot, out in enumerate(sent)][::-1]
        if grad:
            passed = (below(held(*grad, backs[0])),)
            below_mine.append(*passed)
        new, vec = finished(own, cot_mine[part], weight[part], backs, *passed)
        grad = (new,)
        vectors.append(vec)
    below_mine.append(below(*grad))

    index = jnp.stack([place, core]).astype(jnp.int32)
    handed = placed(index, below_mine, [xored(block, "tensor", 1) for block in below_mine])

    vec_mine = jnp.concatenate(vectors, axis=0)
    vec_theirs = xored(vec_mine, "tensor", 1)
    sketch_sum = jnp.concatenate(
        [jnp.where(core == 0, vec_mine, vec_theirs), jnp.where(core == 0, vec_theirs, vec_mine)],
        axis=0,
    )
    out_vec = jnp.dot(cot, model_sketch[0], preferred_element_type=jnp.float32)
    counts = lengths[0, 0]
    upto = jnp.arange(counts.shape[0])
    ends = jnp.sum(jnp.where(upto[None, :] <= upto[:, None], counts[None, :], 0), axis=1)
    starts = ends - counts
    position = jnp.arange(tok_dev, dtype=jnp.int32)
    member = ((position[None, :] >= starts[:, None]) & (position[None, :] < ends[:, None])).astype(
        jnp.float32
    )
    down_feat = jnp.einsum(
        "et,ta,tb->eab", member, out_vec, sketch_sum[:, :rank], precision=lax.Precision.HIGHEST
    )
    up_feat = jnp.einsum(
        "et,ta,tb->eab",
        member,
        sketch_sum[:, rank:],
        input_sketch[0],
        precision=lax.Precision.HIGHEST,
    )
    features = jnp.concatenate([down_feat, up_feat], axis=2)
    return (handed[None], features[None])


def solution(mesh):
    in_specs = (
        P("section", ("groups", "dp"), None),
        P("section", ("groups", "dp"), None),
        P("section", ("groups", "dp"), None),
        P("section", "dp", None, "tensor"),
        P("section", "dp", "tensor", None),
        P("section", ("groups", "dp"), None, None, "tensor"),
        P("section", ("groups", "dp"), None),
        P("section", None, None),
        P("section", "dp", "tensor", None),
        P("section", ("groups", "dp"), None),
    )
    out_specs = (P("section", ("groups", "dp"), None), P("section", ("groups", "dp"), None, None))
    return jax.shard_map(
        per_device, mesh=mesh, in_specs=in_specs, out_specs=out_specs, check_vma=False
    )
```

```python
import functools

import jax
import jax.numpy as jnp
from jax import lax
from jax.experimental import pallas as pl
from jax.experimental.pallas import tpu as pltpu
from jax.sharding import PartitionSpec as P

EXPERTS = 4
CHUNKS = 2
NT = (((1,), (1,)), ((), ()))


def xored(block, axis, bits):
    n = lax.axis_size(axis)
    return lax.ppermute(block, axis, [(i, i ^ bits) for i in range(n)])


ANYWHERE = pl.BlockSpec(memory_space=pl.ANY)
RESIDENT = pl.BlockSpec(memory_space=pltpu.VMEM)


def held_kernel(block_ref, *refs):
    refs[-1][...] = block_ref[...]


def held(block, *events):
    return pl.pallas_call(
        held_kernel,
        in_specs=[RESIDENT] + [ANYWHERE] * len(events),
        out_specs=RESIDENT,
        out_shape=jax.ShapeDtypeStruct(block.shape, block.dtype),
        compiler_params=pltpu.CompilerParams(vmem_limit_bytes=1 << 20),
        name="held",
    )(block, *events)


def merge_kernel(others, keep_ref, came_ref, *refs):
    own_ref, *sent_refs = refs[-1 - others :]
    rows = own_ref.shape[0]
    own_ref[...] = keep_ref[:rows] + came_ref[:rows].astype(jnp.float32)
    for at, sent_ref in enumerate(sent_refs):
        part = slice((at + 1) * rows, (at + 2) * rows)
        total = keep_ref[part] + came_ref[part].astype(jnp.float32)
        sent_ref[...] = total.astype(jnp.bfloat16)


def merged(keep, came, rows, *events):
    count, wide = keep.shape
    others = count // rows - 1
    return pl.pallas_call(
        functools.partial(merge_kernel, others),
        in_specs=[RESIDENT] * 2 + [ANYWHERE] * len(events),
        out_specs=[RESIDENT] * (1 + others),
        out_shape=[jax.ShapeDtypeStruct((rows, wide), jnp.float32)]
        + [jax.ShapeDtypeStruct((rows, wide), jnp.bfloat16)] * others,
        compiler_params=pltpu.CompilerParams(vmem_limit_bytes=4 << 20),
        cost_estimate=pl.CostEstimate(
            flops=count * wide, bytes_accessed=8 * count * wide, transcendentals=0
        ),
        name="merge",
    )(keep, came, *events)


def finish_kernel(slots, own_ref, cot_ref, weight_ref, *refs):
    grad_ref, vec_ref = refs[-2:]
    width = grad_ref.shape[1]
    total = weight_ref[:, :1] * own_ref[...]
    for slot in range(1, slots):
        back = refs[slots - 1 - slot][...].astype(jnp.float32)
        total += weight_ref[:, slot : slot + 1] * back
    grad_ref[...] = (cot_ref[...].astype(jnp.float32) + total[:, :width]).astype(jnp.bfloat16)
    vec_ref[...] = total[:, width:]


def finished(own, cot, weight, backs, *events):
    rows, wide = own.shape
    width = cot.shape[1]
    return pl.pallas_call(
        functools.partial(finish_kernel, 1 + len(backs)),
        in_specs=[RESIDENT] * (3 + len(backs)) + [ANYWHERE] * len(events),
        out_specs=[RESIDENT] * 2,
        out_shape=[
            jax.ShapeDtypeStruct((rows, width), jnp.bfloat16),
            jax.ShapeDtypeStruct((rows, wide - width), jnp.float32),
        ],
        compiler_params=pltpu.CompilerParams(vmem_limit_bytes=4 << 20),
        cost_estimate=pl.CostEstimate(
            flops=8 * rows * wide, bytes_accessed=12 * rows * wide, transcendentals=0
        ),
        name="finish",
    )(own, cot, weight, *backs, *events)


def tile_of(size, most):
    best = 128
    for tile in range(128, most + 1, 128):
        if size % tile == 0:
            best = tile
    return best


def slope_kernel(groups, index_ref, *refs):
    del index_ref
    pre_refs, sketch_ref, weight_hbm = refs[:groups], refs[groups], refs[groups + 1]
    slope_ref, down_ref, weight_ref, weight_sem = refs[-4:]
    load = pltpu.make_async_copy(weight_hbm, weight_ref, weight_sem)

    @pl.when((pl.program_id(0) == 0) & (pl.program_id(1) == 0))
    def _():
        load.start()

    pre = jnp.concatenate([r[0, 0, 0] for r in pre_refs], axis=0).astype(jnp.float32)
    sig = 0.5 + 0.5 * jnp.tanh(0.5 * pre)
    hidden = pre * sig
    slope = sig + hidden * (1.0 - sig)
    slope_ref[0] = slope.T.astype(slope_ref.dtype)
    term = lax.dot_general(
        hidden.astype(jnp.bfloat16), sketch_ref[...], NT, preferred_element_type=jnp.float32
    )

    @pl.when(pl.program_id(1) == 0)
    def _():
        down_ref[...] = jnp.zeros_like(down_ref)

    down_ref[0] += term

    @pl.when(
        (pl.program_id(0) == pl.num_programs(0) - 1) & (pl.program_id(1) == pl.num_programs(1) - 1)
    )
    def _():
        load.wait()


def slopes(pre, sketch_t, weight, place, core):
    n, _, chunks, rows, cols = pre.shape
    rank = sketch_t.shape[0]
    groups = 2 * n
    tile = tile_of(cols, 896)
    index = jnp.stack([place, core]).astype(jnp.int32)
    weight = pltpu.with_memory_space_constraint(weight, pltpu.HBM)

    def spec_of(h, slot):
        return pl.BlockSpec(
            (1, 1, 1, rows, tile), lambda a, j, ix: (ix[0] ^ slot, ix[1] ^ h, a, 0, j)
        )

    return pl.pallas_call(
        functools.partial(slope_kernel, groups),
        grid_spec=pltpu.PrefetchScalarGridSpec(
            num_scalar_prefetch=1,
            grid=(chunks, cols // tile),
            in_specs=[spec_of(h, slot) for h in range(2) for slot in range(n)]
            + [pl.BlockSpec((rank, tile), lambda a, j, ix: (0, j))]
            + [pl.BlockSpec(memory_space=pltpu.HBM)],
            out_specs=[
                pl.BlockSpec((1, tile, groups * rows), lambda a, j, ix: (a, j, 0)),
                pl.BlockSpec((1, groups * rows, rank), lambda a, j, ix: (a, 0, 0)),
                RESIDENT,
            ],
            scratch_shapes=[pltpu.SemaphoreType.DMA],
        ),
        out_shape=[
            jax.ShapeDtypeStruct((chunks, cols, groups * rows), jnp.bfloat16),
            jax.ShapeDtypeStruct((chunks, groups * rows, rank), jnp.float32),
            jax.ShapeDtypeStruct(weight.shape, weight.dtype),
        ],
        cost_estimate=pl.CostEstimate(
            flops=2 * chunks * groups * rows * cols * rank,
            bytes_accessed=4 * chunks * groups * rows * cols,
            transcendentals=chunks * groups * rows * cols,
        ),
        compiler_params=pltpu.CompilerParams(vmem_limit_bytes=7 << 20),
        name="slopes",
    )(index, *([pre] * groups), sketch_t, weight)


def expert_kernel(
    tile_f, tile_d, rows_ref, slope_ref, down_part_ref, sketch_ref, down_ref, up_hbm, *refs
):
    keep_ref, give_ref, rows_buf, grad_buf, up_buf, up_sem = refs[-6:]
    hidden_cols, width = down_ref.shape
    steps_f, steps_d = hidden_cols // tile_f, width // tile_d
    half = keep_ref.shape[0]

    def tile(j, size):
        return pl.ds(pl.multiple_of(j * size, size), size)

    def up_copy(j):
        part = tile(j, tile_d)
        return pltpu.make_async_copy(up_hbm.at[part], up_buf.at[part], up_sem.at[j])

    for j in range(steps_d):
        if j == 0 or j > steps_f:
            up_copy(j).start()
    rows_buf[...] = rows_ref[...].T

    def first(j, carry):
        @pl.when(j + 1 < steps_d)
        def _():
            up_copy(j + 1).start()

        part = tile(j, tile_f)
        grad_hidden = jnp.dot(
            down_ref[part, :], rows_buf[...], preferred_element_type=jnp.float32
        )
        slope = slope_ref[0, part, :].astype(jnp.float32)
        grad_buf[part, :] = (grad_hidden * slope).astype(jnp.bfloat16)
        return carry

    lax.fori_loop(0, steps_f, first, 0)

    up_part = jnp.dot(sketch_ref[...], grad_buf[...], preferred_element_type=jnp.float32).T
    vectors = jnp.concatenate([down_part_ref[0], up_part], axis=1)
    keep_ref[:, width:] = vectors[:half]
    give_ref[:, width:] = vectors[half:].astype(jnp.bfloat16)

    def second(j, carry):
        up_copy(j).wait()
        part = tile(j, tile_d)
        term = jnp.dot(up_buf[part, :], grad_buf[...], preferred_element_type=jnp.float32).T
        keep_ref[:, part] = term[:half]
        give_ref[:, part] = term[half:].astype(jnp.bfloat16)
        return carry

    lax.fori_loop(0, steps_d, second, 0)


def expert(chunk, rows, slope, down_part, sketch_t, down_local, up_local, *events):
    count, width = rows.shape
    hidden_cols = down_local.shape[0]
    rank = sketch_t.shape[0]
    wide = width + 2 * rank
    tile_f, tile_d = tile_of(hidden_cols, 1792), tile_of(width, 1024)
    up_local = pltpu.with_memory_space_constraint(up_local, pltpu.HBM)
    return pl.pallas_call(
        functools.partial(expert_kernel, tile_f, tile_d),
        grid=(1,),
        in_specs=[
            RESIDENT,
            pl.BlockSpec((1, hidden_cols, count), lambda i: (chunk, 0, 0)),
            pl.BlockSpec((1, count, rank), lambda i: (chunk, 0, 0)),
        ]
        + [RESIDENT] * 2
        + [pl.BlockSpec(memory_space=pltpu.HBM)]
        + [ANYWHERE] * len(events),
        out_specs=[RESIDENT] * 2,
        out_shape=[
            jax.ShapeDtypeStruct((count // 2, wide), jnp.float32),
            jax.ShapeDtypeStruct((count // 2, wide), jnp.bfloat16),
        ],
        scratch_shapes=[
            pltpu.VMEM((width, count), jnp.bfloat16),
            pltpu.VMEM((hidden_cols, count), jnp.bfloat16),
            pltpu.VMEM((width, hidden_cols), jnp.bfloat16),
            pltpu.SemaphoreType.DMA((width // tile_d,)),
        ],
        compiler_params=pltpu.CompilerParams(vmem_limit_bytes=26 << 20),
        cost_estimate=pl.CostEstimate(
            flops=4 * count * hidden_cols * width,
            bytes_accessed=4 * hidden_cols * width,
            transcendentals=0,
        ),
        name="expert",
    )(rows, slope, down_part, sketch_t, down_local, up_local, *events)


def per_device(
    cotangent,
    routes,
    gate_values,
    up_weight,
    down_weight,
    pre_activation,
    input_sketch,
    model_sketch,
    hidden_sketch,
    lengths,
):
    pieces = lax.axis_size("dp")
    sections = lax.axis_size("section")
    per_expert = pieces // EXPERTS
    place = lax.axis_index("dp")
    core = lax.axis_index("tensor")
    cot = cotangent[0]
    tok_dev, width = cot.shape
    half = tok_dev // 2
    rows = half // CHUNKS
    rank = model_sketch.shape[2]
    blocks = routes.shape[1]
    block_len = tok_dev // blocks
    sketch_local = hidden_sketch[0, 0]
    pre_all = pre_activation[0, 0]
    hidden_cols = pre_all.shape[2]
    pre_all = pre_all.reshape(pieces, 2, CHUNKS, rows, hidden_cols)

    def below(block):
        return lax.ppermute(block, "section", [(s, (s - 1) % sections) for s in range(sections)])

    token_routes = jnp.broadcast_to(routes[0][:, None, :], (blocks, block_len, 2)).reshape(
        tok_dev, 2
    )
    half_routes = lax.dynamic_slice_in_dim(token_routes, core * half, half, 0)
    half_gates = lax.dynamic_slice_in_dim(gate_values[0], core * half, half, 0)
    slot_expert = (place ^ jnp.arange(pieces, dtype=jnp.int32)) // per_expert
    hits = half_routes[:, None, :] == slot_expert[None, :, None]
    weight = jnp.sum(jnp.where(hits, half_gates[:, None, :], 0.0), axis=2)

    sketch_t = sketch_local.T
    cot_mine = lax.dynamic_slice_in_dim(cot, core * half, half, 0)
    cot_theirs = lax.dynamic_slice_in_dim(cot, (1 - core) * half, half, 0)
    order = sorted(range(2, pieces), reverse=True)
    slope, down_part, down_here = slopes(pre_all, sketch_t, down_weight[0, 0], place, core)
    near_rows = xored(cot_mine, "dp", 1)
    fetched = {slot: xored(cot_mine[:rows], "dp", slot) for slot in order}
    own, sent, grad, passed, backs = (), (), (), (), ()
    below_mine, vectors = [], []
    for a in range(CHUNKS):
        part = slice(a * rows, (a + 1) * rows)
        blocks = [fetched[slot] for slot in order] + [near_rows] * (a == 0)
        blocks = jnp.concatenate(blocks, axis=0)
        if a > 0:
            blocks = held(blocks, own)
        traded = xored(blocks, "tensor", 1)
        mine = dict(fetched)
        theirs = {slot: traded[at * rows : (at + 1) * rows] for at, slot in enumerate(order)}
        if a == 0:
            near_theirs = traded[len(order) * rows :]
        mine[0], mine[1] = cot_mine[part], near_rows[part]
        theirs[0], theirs[1] = cot_theirs[part], near_theirs[part]
        rows_in = jnp.concatenate(
            [mine[k] for k in range(pieces)] + [theirs[k] for k in range(pieces)], axis=0
        )

        kept, give = expert(
            a, rows_in, slope, down_part, sketch_t, down_here, up_weight[0, 0], *sent
        )
        if a + 1 < CHUNKS:
            coming = held(cot_mine[(a + 1) * rows : (a + 2) * rows], near_rows)
            fetched = {slot: held(xored(coming, "dp", slot), kept) for slot in order}
            late = tuple(fetched.values())
        else:
            give, late = held(give, *backs), ()
        own, *sent = merged(kept, xored(give, "tensor", 1), rows, *late)
        backs = [xored(out, "dp", slot + 1) for slot, out in enumerate(sent)][::-1]
        if grad:
            passed = (below(held(*grad, backs[0])),)
            below_mine.append(*passed)
        new, vec = finished(own, cot_mine[part], weight[part], backs, *passed)
        grad = (new,)
        vectors.append(vec)
    below_mine.append(below(*grad))

    theirs = [xored(block, "tensor", 1) for block in below_mine]
    first = [jnp.where(core == 0, m, t) for m, t in zip(below_mine, theirs)]
    second = [jnp.where(core == 0, t, m) for m, t in zip(below_mine, theirs)]
    handed = jnp.concatenate(first + second, axis=0)

    vec_mine = jnp.concatenate(vectors, axis=0)
    vec_theirs = xored(vec_mine, "tensor", 1)
    sketch_sum = jnp.concatenate(
        [jnp.where(core == 0, vec_mine, vec_theirs), jnp.where(core == 0, vec_theirs, vec_mine)],
        axis=0,
    )
    out_vec = jnp.dot(cot, model_sketch[0], preferred_element_type=jnp.float32)
    counts = lengths[0, 0]
    upto = jnp.arange(counts.shape[0])
    ends = jnp.sum(jnp.where(upto[None, :] <= upto[:, None], counts[None, :], 0), axis=1)
    starts = ends - counts
    position = jnp.arange(tok_dev, dtype=jnp.int32)
    member = ((position[None, :] >= starts[:, None]) & (position[None, :] < ends[:, None])).astype(
        jnp.float32
    )
    down_feat = jnp.einsum(
        "et,ta,tb->eab", member, out_vec, sketch_sum[:, :rank], precision=lax.Precision.HIGHEST
    )
    up_feat = jnp.einsum(
        "et,ta,tb->eab",
        member,
        sketch_sum[:, rank:],
        input_sketch[0],
        precision=lax.Precision.HIGHEST,
    )
    features = jnp.concatenate([down_feat, up_feat], axis=2)
    return (handed[None], features[None])


def solution(mesh):
    in_specs = (
        P("section", ("groups", "dp"), None),
        P("section", ("groups", "dp"), None),
        P("section", ("groups", "dp"), None),
        P("section", "dp", None, "tensor"),
        P("section", "dp", "tensor", None),
        P("section", ("groups", "dp"), None, None, "tensor"),
        P("section", ("groups", "dp"), None),
        P("section", None, None),
        P("section", "dp", "tensor", None),
        P("section", ("groups", "dp"), None),
    )
    out_specs = (P("section", ("groups", "dp"), None), P("section", ("groups", "dp"), None, None))
    return jax.shard_map(
        per_device, mesh=mesh, in_specs=in_specs, out_specs=out_specs, check_vma=False
    )
```

```python
import functools

import jax
import jax.numpy as jnp
from jax import lax
from jax.experimental import pallas as pl
from jax.experimental.pallas import tpu as pltpu
from jax.sharding import PartitionSpec as P

EXPERTS = 4
CHUNKS = 2
LANES = 128
PARTS = 3
NT = (((1,), (1,)), ((), ()))


def xored(block, axis, bits):
    n = lax.axis_size(axis)
    return lax.ppermute(block, axis, [(i, i ^ bits) for i in range(n)])


ANYWHERE = pl.BlockSpec(memory_space=pl.ANY)
RESIDENT = pl.BlockSpec(memory_space=pltpu.VMEM)


def held_kernel(block_ref, *refs):
    refs[-1][...] = block_ref[...]


def held(block, *events):
    return pl.pallas_call(
        held_kernel,
        in_specs=[RESIDENT] + [ANYWHERE] * len(events),
        out_specs=RESIDENT,
        out_shape=jax.ShapeDtypeStruct(block.shape, block.dtype),
        compiler_params=pltpu.CompilerParams(vmem_limit_bytes=1 << 20),
        name="held",
    )(block, *events)


def merge_kernel(others, keep_ref, came_ref, *refs):
    own_ref, *sent_refs = refs[-1 - others :]
    rows = own_ref.shape[0]
    own_ref[...] = keep_ref[:rows] + came_ref[:rows].astype(jnp.float32)
    for at, sent_ref in enumerate(sent_refs):
        part = slice((at + 1) * rows, (at + 2) * rows)
        total = keep_ref[part] + came_ref[part].astype(jnp.float32)
        sent_ref[...] = total.astype(jnp.bfloat16)


def merged(keep, came, rows, *events):
    count, wide = keep.shape
    others = count // rows - 1
    return pl.pallas_call(
        functools.partial(merge_kernel, others),
        in_specs=[RESIDENT] * 2 + [ANYWHERE] * len(events),
        out_specs=[RESIDENT] * (1 + others),
        out_shape=[jax.ShapeDtypeStruct((rows, wide), jnp.float32)]
        + [jax.ShapeDtypeStruct((rows, wide), jnp.bfloat16)] * others,
        compiler_params=pltpu.CompilerParams(vmem_limit_bytes=4 << 20),
        cost_estimate=pl.CostEstimate(
            flops=count * wide, bytes_accessed=8 * count * wide, transcendentals=0
        ),
        name="merge",
    )(keep, came, *events)


def label_kernel(rows_ref, weight_ref, *refs):
    out_ref = refs[-1]
    rows, width = rows_ref.shape
    column = lax.broadcasted_iota(jnp.int32, (rows, LANES), 1)
    table = jnp.zeros((rows, LANES), jnp.float32)
    for slot in range(weight_ref.shape[1]):
        rest = weight_ref[:, slot : slot + 1]
        for j in range(PARTS):
            rounded = rest.astype(jnp.bfloat16).astype(jnp.float32)
            table = jnp.where(column == PARTS * slot + j, rounded, table)
            rest -= rounded
    out_ref[:, :width] = rows_ref[...]
    out_ref[:, width:] = table.astype(jnp.bfloat16)


def labelled(rows, weight, *events):
    count, width = rows.shape
    return pl.pallas_call(
        label_kernel,
        in_specs=[RESIDENT] * 2 + [ANYWHERE] * len(events),
        out_specs=RESIDENT,
        out_shape=jax.ShapeDtypeStruct((count, width + LANES), rows.dtype),
        compiler_params=pltpu.CompilerParams(vmem_limit_bytes=2 << 20),
        name="label",
    )(rows, weight, *events)


def sort_kernel(slots, keep_ref, came_ref, *refs):
    labels = refs[: slots - 2]
    own_ref, near_ref, odd_ref, *even_refs = refs[slots - 2 :]
    rows = own_ref.shape[0]
    first = labels[0].shape[1] - LANES

    def total(slot):
        part = slice(slot * rows, (slot + 1) * rows)
        return keep_ref[part] + came_ref[part].astype(jnp.float32)

    def weighted(slot):
        table = labels[slot - 2][:, first:].astype(jnp.float32)
        owner = lax.broadcasted_iota(jnp.int32, table.shape, 1) // PARTS
        weight = jnp.sum(jnp.where(owner == slot, table, 0.0), axis=1, keepdims=True)
        return weight * total(slot)

    own_ref[...] = total(0)
    near_ref[...] = total(1).astype(jnp.bfloat16)
    for at, even_ref in enumerate(even_refs):
        even_ref[...] = weighted(2 * at + 2)
        odd_ref[at * rows : (at + 1) * rows] = weighted(2 * at + 3).astype(jnp.bfloat16)


def sorted_sums(keep, came, labels):
    wide, slots = keep.shape[1], len(labels) + 2
    rows, pairs = keep.shape[0] // slots, len(labels) // 2
    own, *evens = [jax.ShapeDtypeStruct((rows, wide), jnp.float32)] * (1 + pairs)
    near = jax.ShapeDtypeStruct((rows, wide), jnp.bfloat16)
    odd = jax.ShapeDtypeStruct((pairs * rows, wide), jnp.bfloat16)
    return pl.pallas_call(
        functools.partial(sort_kernel, slots),
        in_specs=[RESIDENT] * (2 + len(labels)),
        out_specs=[RESIDENT] * (3 + pairs),
        out_shape=[own, near, odd, *evens],
        compiler_params=pltpu.CompilerParams(vmem_limit_bytes=4 << 20),
        name="sort",
    )(keep, came, *labels)


def join_kernel(pairs, came_ref, *refs):
    rows = refs[0].shape[0]
    for at in range(pairs):
        total = refs[at][...] + came_ref[at * rows : (at + 1) * rows].astype(jnp.float32)
        refs[pairs + at][...] = total.astype(jnp.bfloat16)


def joined(came, evens):
    pairs = len(evens)
    return pl.pallas_call(
        functools.partial(join_kernel, pairs),
        in_specs=[RESIDENT] * (1 + pairs),
        out_specs=[RESIDENT] * pairs,
        out_shape=[jax.ShapeDtypeStruct(evens[0].shape, jnp.bfloat16)] * pairs,
        compiler_params=pltpu.CompilerParams(vmem_limit_bytes=4 << 20),
        name="join",
    )(came, *evens)


def finish_kernel(slots, plain, own_ref, cot_ref, weight_ref, *refs):
    grad_ref, vec_ref = refs[-2:]
    width = grad_ref.shape[1]
    total = weight_ref[:, :1] * own_ref[...]
    for slot in range(1, slots):
        back = refs[plain + slots - 1 - slot][...].astype(jnp.float32)
        total += weight_ref[:, slot : slot + 1] * back
    for back_ref in refs[:plain]:
        total += back_ref[...].astype(jnp.float32)
    grad_ref[...] = (cot_ref[...].astype(jnp.float32) + total[:, :width]).astype(jnp.bfloat16)
    vec_ref[...] = total[:, width:]


def finished(own, cot, weight, backs, plain, *events):
    rows, wide = own.shape
    width = cot.shape[1]
    return pl.pallas_call(
        functools.partial(finish_kernel, 1 + len(backs), len(plain)),
        in_specs=[RESIDENT] * (3 + len(backs) + len(plain)) + [ANYWHERE] * len(events),
        out_specs=[RESIDENT] * 2,
        out_shape=[
            jax.ShapeDtypeStruct((rows, width), jnp.bfloat16),
            jax.ShapeDtypeStruct((rows, wide - width), jnp.float32),
        ],
        compiler_params=pltpu.CompilerParams(vmem_limit_bytes=4 << 20),
        cost_estimate=pl.CostEstimate(
            flops=8 * rows * wide, bytes_accessed=12 * rows * wide, transcendentals=0
        ),
        name="finish",
    )(own, cot, weight, *plain, *backs, *events)


def tile_of(size, most):
    best = 128
    for tile in range(128, most + 1, 128):
        if size % tile == 0:
            best = tile
    return best


def slope_kernel(groups, index_ref, *refs):
    del index_ref
    pre_refs, sketch_ref, weight_hbm = refs[:groups], refs[groups], refs[groups + 1]
    slope_ref, down_ref, weight_ref, weight_sem = refs[-4:]
    load = pltpu.make_async_copy(weight_hbm, weight_ref, weight_sem)

    @pl.when((pl.program_id(0) == 0) & (pl.program_id(1) == 0))
    def _():
        load.start()

    pre = jnp.concatenate([r[0, 0, 0] for r in pre_refs], axis=0).astype(jnp.float32)
    sig = 0.5 + 0.5 * jnp.tanh(0.5 * pre)
    hidden = pre * sig
    slope = sig + hidden * (1.0 - sig)
    slope_ref[0] = slope.T.astype(slope_ref.dtype)
    term = lax.dot_general(
        hidden.astype(jnp.bfloat16), sketch_ref[...], NT, preferred_element_type=jnp.float32
    )

    @pl.when(pl.program_id(1) == 0)
    def _():
        down_ref[...] = jnp.zeros_like(down_ref)

    down_ref[0] += term

    @pl.when(
        (pl.program_id(0) == pl.num_programs(0) - 1) & (pl.program_id(1) == pl.num_programs(1) - 1)
    )
    def _():
        load.wait()


def slopes(pre, sketch_t, weight, place, core):
    n, _, chunks, rows, cols = pre.shape
    rank = sketch_t.shape[0]
    groups = 2 * n
    tile = tile_of(cols, 896)
    index = jnp.stack([place, core]).astype(jnp.int32)
    weight = pltpu.with_memory_space_constraint(weight, pltpu.HBM)

    def spec_of(h, slot):
        return pl.BlockSpec(
            (1, 1, 1, rows, tile), lambda a, j, ix: (ix[0] ^ slot, ix[1] ^ h, a, 0, j)
        )

    return pl.pallas_call(
        functools.partial(slope_kernel, groups),
        grid_spec=pltpu.PrefetchScalarGridSpec(
            num_scalar_prefetch=1,
            grid=(chunks, cols // tile),
            in_specs=[spec_of(h, slot) for h in range(2) for slot in range(n)]
            + [pl.BlockSpec((rank, tile), lambda a, j, ix: (0, j))]
            + [pl.BlockSpec(memory_space=pltpu.HBM)],
            out_specs=[
                pl.BlockSpec((1, tile, groups * rows), lambda a, j, ix: (a, j, 0)),
                pl.BlockSpec((1, groups * rows, rank), lambda a, j, ix: (a, 0, 0)),
                RESIDENT,
            ],
            scratch_shapes=[pltpu.SemaphoreType.DMA],
        ),
        out_shape=[
            jax.ShapeDtypeStruct((chunks, cols, groups * rows), jnp.bfloat16),
            jax.ShapeDtypeStruct((chunks, groups * rows, rank), jnp.float32),
            jax.ShapeDtypeStruct(weight.shape, weight.dtype),
        ],
        cost_estimate=pl.CostEstimate(
            flops=2 * chunks * groups * rows * cols * rank,
            bytes_accessed=4 * chunks * groups * rows * cols,
            transcendentals=chunks * groups * rows * cols,
        ),
        compiler_params=pltpu.CompilerParams(vmem_limit_bytes=7 << 20),
        name="slopes",
    )(index, *([pre] * groups), sketch_t, weight)


def expert_kernel(
    tile_f, tile_d, rows_ref, slope_ref, down_part_ref, sketch_ref, down_ref, up_hbm, *refs
):
    keep_ref, give_ref, rows_buf, grad_buf, up_buf, up_sem = refs[-6:]
    hidden_cols, width = down_ref.shape
    steps_f, steps_d = hidden_cols // tile_f, width // tile_d
    half = keep_ref.shape[0]

    def tile(j, size):
        return pl.ds(pl.multiple_of(j * size, size), size)

    def up_copy(j):
        part = tile(j, tile_d)
        return pltpu.make_async_copy(up_hbm.at[part], up_buf.at[part], up_sem.at[j])

    for j in range(steps_d):
        if j == 0 or j > steps_f:
            up_copy(j).start()
    rows_buf[...] = rows_ref[...].T

    def first(j, carry):
        @pl.when(j + 1 < steps_d)
        def _():
            up_copy(j + 1).start()

        part = tile(j, tile_f)
        grad_hidden = jnp.dot(
            down_ref[part, :], rows_buf[...], preferred_element_type=jnp.float32
        )
        slope = slope_ref[0, part, :].astype(jnp.float32)
        grad_buf[part, :] = (grad_hidden * slope).astype(jnp.bfloat16)
        return carry

    lax.fori_loop(0, steps_f, first, 0)

    up_part = jnp.dot(sketch_ref[...], grad_buf[...], preferred_element_type=jnp.float32).T
    vectors = jnp.concatenate([down_part_ref[0], up_part], axis=1)
    keep_ref[:, width:] = vectors[:half]
    give_ref[:, width:] = vectors[half:].astype(jnp.bfloat16)

    def second(j, carry):
        up_copy(j).wait()
        part = tile(j, tile_d)
        term = jnp.dot(up_buf[part, :], grad_buf[...], preferred_element_type=jnp.float32).T
        keep_ref[:, part] = term[:half]
        give_ref[:, part] = term[half:].astype(jnp.bfloat16)
        return carry

    lax.fori_loop(0, steps_d, second, 0)


def expert(chunk, rows, slope, down_part, sketch_t, down_local, up_local, *events):
    count, width = rows.shape
    hidden_cols = down_local.shape[0]
    rank = sketch_t.shape[0]
    wide = width + 2 * rank
    tile_f, tile_d = tile_of(hidden_cols, 1792), tile_of(width, 1024)
    up_local = pltpu.with_memory_space_constraint(up_local, pltpu.HBM)
    return pl.pallas_call(
        functools.partial(expert_kernel, tile_f, tile_d),
        grid=(1,),
        in_specs=[
            RESIDENT,
            pl.BlockSpec((1, hidden_cols, count), lambda i: (chunk, 0, 0)),
            pl.BlockSpec((1, count, rank), lambda i: (chunk, 0, 0)),
        ]
        + [RESIDENT] * 2
        + [pl.BlockSpec(memory_space=pltpu.HBM)]
        + [ANYWHERE] * len(events),
        out_specs=[RESIDENT] * 2,
        out_shape=[
            jax.ShapeDtypeStruct((count // 2, wide), jnp.float32),
            jax.ShapeDtypeStruct((count // 2, wide), jnp.bfloat16),
        ],
        scratch_shapes=[
            pltpu.VMEM((width, count), jnp.bfloat16),
            pltpu.VMEM((hidden_cols, count), jnp.bfloat16),
            pltpu.VMEM((width, hidden_cols), jnp.bfloat16),
            pltpu.SemaphoreType.DMA((width // tile_d,)),
        ],
        compiler_params=pltpu.CompilerParams(vmem_limit_bytes=26 << 20),
        cost_estimate=pl.CostEstimate(
            flops=4 * count * hidden_cols * width,
            bytes_accessed=4 * hidden_cols * width,
            transcendentals=0,
        ),
        name="expert",
    )(rows, slope, down_part, sketch_t, down_local, up_local, *events)


def per_device(
    cotangent,
    routes,
    gate_values,
    up_weight,
    down_weight,
    pre_activation,
    input_sketch,
    model_sketch,
    hidden_sketch,
    lengths,
):
    pieces = lax.axis_size("dp")
    sections = lax.axis_size("section")
    per_expert = pieces // EXPERTS
    place = lax.axis_index("dp")
    core = lax.axis_index("tensor")
    cot = cotangent[0]
    tok_dev, width = cot.shape
    half = tok_dev // 2
    rows = half // CHUNKS
    rank = model_sketch.shape[2]
    blocks = routes.shape[1]
    block_len = tok_dev // blocks
    sketch_local = hidden_sketch[0, 0]
    pre_all = pre_activation[0, 0]
    hidden_cols = pre_all.shape[2]
    pre_all = pre_all.reshape(pieces, 2, CHUNKS, rows, hidden_cols)

    def below(block):
        return lax.ppermute(block, "section", [(s, (s - 1) % sections) for s in range(sections)])

    token_routes = jnp.broadcast_to(routes[0][:, None, :], (blocks, block_len, 2)).reshape(
        tok_dev, 2
    )
    half_routes = lax.dynamic_slice_in_dim(token_routes, core * half, half, 0)
    half_gates = lax.dynamic_slice_in_dim(gate_values[0], core * half, half, 0)
    slot_expert = (place ^ jnp.arange(pieces, dtype=jnp.int32)) // per_expert
    hits = half_routes[:, None, :] == slot_expert[None, :, None]
    weight = jnp.sum(jnp.where(hits, half_gates[:, None, :], 0.0), axis=2)

    sketch_t = sketch_local.T
    cot_mine = lax.dynamic_slice_in_dim(cot, core * half, half, 0)
    cot_theirs = lax.dynamic_slice_in_dim(cot, (1 - core) * half, half, 0)
    order = sorted(range(2, pieces), reverse=True)
    slope, down_part, down_here = slopes(pre_all, sketch_t, down_weight[0, 0], place, core)
    near_rows = xored(cot_mine, "dp", 1)
    fetched = {slot: xored(cot_mine[:rows], "dp", slot) for slot in order}
    own, sent, grad, passed, backs = (), (), (), (), ()
    below_mine, vectors = [], []
    for a in range(CHUNKS):
        part = slice(a * rows, (a + 1) * rows)
        rows_of = {slot: block[:, :width] for slot, block in fetched.items()}
        blocks = [rows_of[slot] for slot in order] + [near_rows] * (a == 0)
        blocks = jnp.concatenate(blocks, axis=0)
        if a > 0:
            blocks = held(blocks, own)
        traded = xored(blocks, "tensor", 1)
        mine = dict(rows_of)
        theirs = {slot: traded[at * rows : (at + 1) * rows] for at, slot in enumerate(order)}
        if a == 0:
            near_theirs = traded[len(order) * rows :]
        mine[0], mine[1] = cot_mine[part], near_rows[part]
        theirs[0], theirs[1] = cot_theirs[part], near_theirs[part]
        rows_in = jnp.concatenate(
            [mine[k] for k in range(pieces)] + [theirs[k] for k in range(pieces)], axis=0
        )

        kept, give = expert(
            a, rows_in, slope, down_part, sketch_t, down_here, up_weight[0, 0], *sent
        )
        if a + 1 < CHUNKS:
            part_next = slice((a + 1) * rows, (a + 2) * rows)
            coming = labelled(cot_mine[part_next], weight[part_next], near_rows)
            fetched = {slot: held(xored(coming, "dp", slot), kept) for slot in order}
            late = tuple(fetched.values())
        else:
            give, late = held(give, *backs), ()
        came = xored(give, "tensor", 1)
        if a == 0:
            own, *sent = merged(kept, came, rows, *late)
            backs = [xored(out, "dp", slot + 1) for slot, out in enumerate(sent)][::-1]
            new, vec = finished(own, cot_mine[part], weight[part], backs, [])
        else:
            own, near, odd, *evens = sorted_sums(kept, came, [fetched[k] for k in order[::-1]])
            sums = joined(xored(odd, "dp", 1), evens)
            plain = [xored(block, "dp", 2 * at + 2) for at, block in enumerate(sums)]
            near = xored(held(near, sums[0]), "dp", 1)
            below_mine.append(below(held(*grad, sums[0])))
            new, vec = finished(own, cot_mine[part], weight[part], [near], plain, *below_mine)
        grad = (new,)
        vectors.append(vec)
    below_mine.append(below(*grad))

    theirs = [xored(block, "tensor", 1) for block in below_mine]
    first = [jnp.where(core == 0, m, t) for m, t in zip(below_mine, theirs)]
    second = [jnp.where(core == 0, t, m) for m, t in zip(below_mine, theirs)]
    handed = jnp.concatenate(first + second, axis=0)

    vec_mine = jnp.concatenate(vectors, axis=0)
    vec_theirs = xored(vec_mine, "tensor", 1)
    sketch_sum = jnp.concatenate(
        [jnp.where(core == 0, vec_mine, vec_theirs), jnp.where(core == 0, vec_theirs, vec_mine)],
        axis=0,
    )
    out_vec = jnp.dot(cot, model_sketch[0], preferred_element_type=jnp.float32)
    counts = lengths[0, 0]
    upto = jnp.arange(counts.shape[0])
    ends = jnp.sum(jnp.where(upto[None, :] <= upto[:, None], counts[None, :], 0), axis=1)
    starts = ends - counts
    position = jnp.arange(tok_dev, dtype=jnp.int32)
    member = ((position[None, :] >= starts[:, None]) & (position[None, :] < ends[:, None])).astype(
        jnp.float32
    )
    down_feat = jnp.einsum(
        "et,ta,tb->eab", member, out_vec, sketch_sum[:, :rank], precision=lax.Precision.HIGHEST
    )
    up_feat = jnp.einsum(
        "et,ta,tb->eab",
        member,
        sketch_sum[:, rank:],
        input_sketch[0],
        precision=lax.Precision.HIGHEST,
    )
    features = jnp.concatenate([down_feat, up_feat], axis=2)
    return (handed[None], features[None])


def solution(mesh):
    in_specs = (
        P("section", ("groups", "dp"), None),
        P("section", ("groups", "dp"), None),
        P("section", ("groups", "dp"), None),
        P("section", "dp", None, "tensor"),
        P("section", "dp", "tensor", None),
        P("section", ("groups", "dp"), None, None, "tensor"),
        P("section", ("groups", "dp"), None),
        P("section", None, None),
        P("section", "dp", "tensor", None),
        P("section", ("groups", "dp"), None),
    )
    out_specs = (P("section", ("groups", "dp"), None), P("section", ("groups", "dp"), None, None))
    return jax.shard_map(
        per_device, mesh=mesh, in_specs=in_specs, out_specs=out_specs, check_vma=False
    )
```

```python
import functools

import jax
import jax.numpy as jnp
from jax import lax
from jax.experimental import pallas as pl
from jax.experimental.pallas import tpu as pltpu
from jax.sharding import PartitionSpec as P

EXPERTS = 4
CHUNKS = 2
NT = (((1,), (1,)), ((), ()))


def xored(block, axis, bits):
    n = lax.axis_size(axis)
    return lax.ppermute(block, axis, [(i, i ^ bits) for i in range(n)])


ANYWHERE = pl.BlockSpec(memory_space=pl.ANY)
RESIDENT = pl.BlockSpec(memory_space=pltpu.VMEM)


def held_kernel(block_ref, *refs):
    refs[-1][...] = block_ref[...]


def held(block, *events):
    return pl.pallas_call(
        held_kernel,
        in_specs=[RESIDENT] + [ANYWHERE] * len(events),
        out_specs=RESIDENT,
        out_shape=jax.ShapeDtypeStruct(block.shape, block.dtype),
        compiler_params=pltpu.CompilerParams(vmem_limit_bytes=1 << 20),
        name="held",
    )(block, *events)


def merge_kernel(others, keep_ref, came_ref, *refs):
    own_ref, *sent_refs = refs[-1 - others :]
    rows = own_ref.shape[0]
    own_ref[...] = keep_ref[:rows] + came_ref[:rows].astype(jnp.float32)
    for at, sent_ref in enumerate(sent_refs):
        part = slice((at + 1) * rows, (at + 2) * rows)
        total = keep_ref[part] + came_ref[part].astype(jnp.float32)
        sent_ref[...] = total.astype(jnp.bfloat16)


def merged(keep, came, rows, *events):
    count, wide = keep.shape
    others = count // rows - 1
    return pl.pallas_call(
        functools.partial(merge_kernel, others),
        in_specs=[RESIDENT] * 2 + [ANYWHERE] * len(events),
        out_specs=[RESIDENT] * (1 + others),
        out_shape=[jax.ShapeDtypeStruct((rows, wide), jnp.float32)]
        + [jax.ShapeDtypeStruct((rows, wide), jnp.bfloat16)] * others,
        compiler_params=pltpu.CompilerParams(vmem_limit_bytes=4 << 20),
        cost_estimate=pl.CostEstimate(
            flops=count * wide, bytes_accessed=8 * count * wide, transcendentals=0
        ),
        name="merge",
    )(keep, came, *events)


def finish_kernel(slots, own_ref, cot_ref, weight_ref, *refs):
    grad_ref, vec_ref = refs[-2:]
    width = grad_ref.shape[1]
    total = weight_ref[:, :1] * own_ref[...]
    for slot in range(1, slots):
        back = refs[slots - 1 - slot][...].astype(jnp.float32)
        total += weight_ref[:, slot : slot + 1] * back
    grad_ref[...] = (cot_ref[...].astype(jnp.float32) + total[:, :width]).astype(jnp.bfloat16)
    vec_ref[...] = total[:, width:]


def finished(own, cot, weight, backs, *events):
    rows, wide = own.shape
    width = cot.shape[1]
    return pl.pallas_call(
        functools.partial(finish_kernel, 1 + len(backs)),
        in_specs=[RESIDENT] * (3 + len(backs)) + [ANYWHERE] * len(events),
        out_specs=[RESIDENT] * 2,
        out_shape=[
            jax.ShapeDtypeStruct((rows, width), jnp.bfloat16),
            jax.ShapeDtypeStruct((rows, wide - width), jnp.float32),
        ],
        compiler_params=pltpu.CompilerParams(vmem_limit_bytes=4 << 20),
        cost_estimate=pl.CostEstimate(
            flops=8 * rows * wide, bytes_accessed=12 * rows * wide, transcendentals=0
        ),
        name="finish",
    )(own, cot, weight, *backs, *events)


def tile_of(size, most):
    best = 128
    for tile in range(128, most + 1, 128):
        if size % tile == 0:
            best = tile
    return best


def slope_kernel(groups, index_ref, *refs):
    del index_ref
    pre_refs, sketch_ref, weight_hbm = refs[:groups], refs[groups], refs[groups + 1]
    slope_ref, down_ref, weight_ref, weight_sem = refs[-4:]
    load = pltpu.make_async_copy(weight_hbm, weight_ref, weight_sem)

    @pl.when((pl.program_id(0) == 0) & (pl.program_id(1) == 0))
    def _():
        load.start()

    pre = jnp.concatenate([r[0, 0, 0] for r in pre_refs], axis=0).astype(jnp.float32)
    sig = 0.5 + 0.5 * jnp.tanh(0.5 * pre)
    hidden = pre * sig
    slope = sig + hidden * (1.0 - sig)
    slope_ref[0] = slope.T.astype(slope_ref.dtype)
    term = lax.dot_general(
        hidden.astype(jnp.bfloat16), sketch_ref[...], NT, preferred_element_type=jnp.float32
    )

    @pl.when(pl.program_id(1) == 0)
    def _():
        down_ref[...] = jnp.zeros_like(down_ref)

    down_ref[0] += term

    @pl.when(
        (pl.program_id(0) == pl.num_programs(0) - 1) & (pl.program_id(1) == pl.num_programs(1) - 1)
    )
    def _():
        load.wait()


def slopes(pre, sketch_t, weight, place, core):
    n, _, chunks, rows, cols = pre.shape
    rank = sketch_t.shape[0]
    groups = 2 * n
    tile = tile_of(cols, 896)
    index = jnp.stack([place, core]).astype(jnp.int32)
    weight = pltpu.with_memory_space_constraint(weight, pltpu.HBM)

    def spec_of(h, slot):
        return pl.BlockSpec(
            (1, 1, 1, rows, tile), lambda a, j, ix: (ix[0] ^ slot, ix[1] ^ h, a, 0, j)
        )

    return pl.pallas_call(
        functools.partial(slope_kernel, groups),
        grid_spec=pltpu.PrefetchScalarGridSpec(
            num_scalar_prefetch=1,
            grid=(chunks, cols // tile),
            in_specs=[spec_of(h, slot) for h in range(2) for slot in range(n)]
            + [pl.BlockSpec((rank, tile), lambda a, j, ix: (0, j))]
            + [pl.BlockSpec(memory_space=pltpu.HBM)],
            out_specs=[
                pl.BlockSpec((1, tile, groups * rows), lambda a, j, ix: (a, j, 0)),
                pl.BlockSpec((1, groups * rows, rank), lambda a, j, ix: (a, 0, 0)),
                RESIDENT,
            ],
            scratch_shapes=[pltpu.SemaphoreType.DMA],
        ),
        out_shape=[
            jax.ShapeDtypeStruct((chunks, cols, groups * rows), jnp.bfloat16),
            jax.ShapeDtypeStruct((chunks, groups * rows, rank), jnp.float32),
            jax.ShapeDtypeStruct(weight.shape, weight.dtype),
        ],
        cost_estimate=pl.CostEstimate(
            flops=2 * chunks * groups * rows * cols * rank,
            bytes_accessed=4 * chunks * groups * rows * cols,
            transcendentals=chunks * groups * rows * cols,
        ),
        compiler_params=pltpu.CompilerParams(vmem_limit_bytes=7 << 20),
        name="slopes",
    )(index, *([pre] * groups), sketch_t, weight)


def expert_kernel(
    chunk, tile_f, tile_d, rows_ref, slope_ref, down_part_ref, sketch_ref, down_ref, up_hbm, *refs
):
    keep_ref, give_ref, rows_buf, grad_buf, up_buf, up_sem = refs[-6:]
    hidden_cols, width = down_ref.shape
    steps_f, steps_d = hidden_cols // tile_f, width // tile_d
    half = keep_ref.shape[0]

    def tile(j, size):
        return pl.ds(pl.multiple_of(j * size, size), size)

    def up_copy(j):
        part = tile(j, tile_d)
        return pltpu.make_async_copy(up_hbm.at[part], up_buf.at[part], up_sem.at[j])

    for j in range(steps_d):
        if j == 0 or j > steps_f:
            up_copy(j).start()
    rows_buf[...] = rows_ref[...].T

    def first(j, carry):
        @pl.when(j + 1 < steps_d)
        def _():
            up_copy(j + 1).start()

        part = tile(j, tile_f)
        grad_hidden = jnp.dot(
            down_ref[part, :], rows_buf[...], preferred_element_type=jnp.float32
        )
        slope = slope_ref[chunk, part, :].astype(jnp.float32)
        grad_buf[part, :] = (grad_hidden * slope).astype(jnp.bfloat16)
        return carry

    lax.fori_loop(0, steps_f, first, 0)

    up_part = jnp.dot(sketch_ref[...], grad_buf[...], preferred_element_type=jnp.float32).T
    vectors = jnp.concatenate([down_part_ref[chunk], up_part], axis=1)
    keep_ref[:, width:] = vectors[:half]
    give_ref[:, width:] = vectors[half:].astype(jnp.bfloat16)

    def second(j, carry):
        up_copy(j).wait()
        part = tile(j, tile_d)
        term = jnp.dot(up_buf[part, :], grad_buf[...], preferred_element_type=jnp.float32).T
        keep_ref[:, part] = term[:half]
        give_ref[:, part] = term[half:].astype(jnp.bfloat16)
        return carry

    lax.fori_loop(0, steps_d, second, 0)


def expert(chunk, rows, slope, down_part, sketch_t, down_local, up_local, *events):
    count, width = rows.shape
    hidden_cols = down_local.shape[0]
    rank = sketch_t.shape[0]
    wide = width + 2 * rank
    tile_f, tile_d = tile_of(hidden_cols, 1792), tile_of(width, 1024)
    up_local = pltpu.with_memory_space_constraint(up_local, pltpu.HBM)
    return pl.pallas_call(
        functools.partial(expert_kernel, chunk, tile_f, tile_d),
        in_specs=[RESIDENT] * 5
        + [pl.BlockSpec(memory_space=pltpu.HBM)]
        + [ANYWHERE] * len(events),
        out_specs=[RESIDENT] * 2,
        out_shape=[
            jax.ShapeDtypeStruct((count // 2, wide), jnp.float32),
            jax.ShapeDtypeStruct((count // 2, wide), jnp.bfloat16),
        ],
        scratch_shapes=[
            pltpu.VMEM((width, count), jnp.bfloat16),
            pltpu.VMEM((hidden_cols, count), jnp.bfloat16),
            pltpu.VMEM((width, hidden_cols), jnp.bfloat16),
            pltpu.SemaphoreType.DMA((width // tile_d,)),
        ],
        compiler_params=pltpu.CompilerParams(vmem_limit_bytes=26 << 20),
        cost_estimate=pl.CostEstimate(
            flops=4 * count * hidden_cols * width,
            bytes_accessed=4 * hidden_cols * width,
            transcendentals=0,
        ),
        name="expert",
    )(rows, slope, down_part, sketch_t, down_local, up_local, *events)


def per_device(
    cotangent,
    routes,
    gate_values,
    up_weight,
    down_weight,
    pre_activation,
    input_sketch,
    model_sketch,
    hidden_sketch,
    lengths,
):
    pieces = lax.axis_size("dp")
    sections = lax.axis_size("section")
    per_expert = pieces // EXPERTS
    place = lax.axis_index("dp")
    core = lax.axis_index("tensor")
    cot = cotangent[0]
    tok_dev, width = cot.shape
    half = tok_dev // 2
    rows = half // CHUNKS
    rank = model_sketch.shape[2]
    blocks = routes.shape[1]
    block_len = tok_dev // blocks
    sketch_local = hidden_sketch[0, 0]
    pre_all = pre_activation[0, 0]
    hidden_cols = pre_all.shape[2]
    pre_all = pre_all.reshape(pieces, 2, CHUNKS, rows, hidden_cols)

    def below(block):
        return lax.ppermute(block, "section", [(s, (s - 1) % sections) for s in range(sections)])

    token_routes = jnp.broadcast_to(routes[0][:, None, :], (blocks, block_len, 2)).reshape(
        tok_dev, 2
    )
    half_routes = lax.dynamic_slice_in_dim(token_routes, core * half, half, 0)
    half_gates = lax.dynamic_slice_in_dim(gate_values[0], core * half, half, 0)
    slot_expert = (place ^ jnp.arange(pieces, dtype=jnp.int32)) // per_expert
    hits = half_routes[:, None, :] == slot_expert[None, :, None]
    weight = jnp.sum(jnp.where(hits, half_gates[:, None, :], 0.0), axis=2)

    sketch_t = sketch_local.T
    cot_mine = lax.dynamic_slice_in_dim(cot, core * half, half, 0)
    cot_theirs = lax.dynamic_slice_in_dim(cot, (1 - core) * half, half, 0)
    order = sorted(range(2, pieces), reverse=True)
    slope, down_part, down_here = slopes(pre_all, sketch_t, down_weight[0, 0], place, core)
    near_rows = xored(cot_mine, "dp", 1)
    fetched = {slot: xored(cot_mine[:rows], "dp", slot) for slot in order}
    own, sent, grad, passed, backs = (), (), (), (), ()
    below_mine, vectors = [], []
    for a in range(CHUNKS):
        part = slice(a * rows, (a + 1) * rows)
        blocks = [fetched[slot] for slot in order] + [near_rows] * (a == 0)
        blocks = jnp.concatenate(blocks, axis=0)
        if a > 0:
            blocks = held(blocks, own)
        traded = xored(blocks, "tensor", 1)
        mine = dict(fetched)
        theirs = {slot: traded[at * rows : (at + 1) * rows] for at, slot in enumerate(order)}
        if a == 0:
            near_theirs = traded[len(order) * rows :]
        mine[0], mine[1] = cot_mine[part], near_rows[part]
        theirs[0], theirs[1] = cot_theirs[part], near_theirs[part]
        rows_in = jnp.concatenate(
            [mine[k] for k in range(pieces)] + [theirs[k] for k in range(pieces)], axis=0
        )

        kept, give = expert(
            a, rows_in, slope, down_part, sketch_t, down_here, up_weight[0, 0], *sent
        )
        if a + 1 < CHUNKS:
            coming = held(cot_mine[(a + 1) * rows : (a + 2) * rows], near_rows)
            fetched = {slot: held(xored(coming, "dp", slot), kept) for slot in order}
            late = tuple(fetched.values())
        else:
            give, late = held(give, *backs), ()
        own, *sent = merged(kept, xored(give, "tensor", 1), rows, *late)
        backs = [xored(out, "dp", slot + 1) for slot, out in enumerate(sent)][::-1]
        if grad:
            passed = (below(held(*grad, backs[0])),)
            below_mine.append(*passed)
        new, vec = finished(own, cot_mine[part], weight[part], backs, *passed)
        grad = (new,)
        vectors.append(vec)
    below_mine.append(below(*grad))

    theirs = [xored(block, "tensor", 1) for block in below_mine]
    first = [jnp.where(core == 0, m, t) for m, t in zip(below_mine, theirs)]
    second = [jnp.where(core == 0, t, m) for m, t in zip(below_mine, theirs)]
    handed = jnp.concatenate(first + second, axis=0)

    vec_mine = jnp.concatenate(vectors, axis=0)
    vec_theirs = xored(vec_mine, "tensor", 1)
    sketch_sum = jnp.concatenate(
        [jnp.where(core == 0, vec_mine, vec_theirs), jnp.where(core == 0, vec_theirs, vec_mine)],
        axis=0,
    )
    out_vec = jnp.dot(cot, model_sketch[0], preferred_element_type=jnp.float32)
    counts = lengths[0, 0]
    upto = jnp.arange(counts.shape[0])
    ends = jnp.sum(jnp.where(upto[None, :] <= upto[:, None], counts[None, :], 0), axis=1)
    starts = ends - counts
    position = jnp.arange(tok_dev, dtype=jnp.int32)
    member = ((position[None, :] >= starts[:, None]) & (position[None, :] < ends[:, None])).astype(
        jnp.float32
    )
    down_feat = jnp.einsum(
        "et,ta,tb->eab", member, out_vec, sketch_sum[:, :rank], precision=lax.Precision.HIGHEST
    )
    up_feat = jnp.einsum(
        "et,ta,tb->eab",
        member,
        sketch_sum[:, rank:],
        input_sketch[0],
        precision=lax.Precision.HIGHEST,
    )
    features = jnp.concatenate([down_feat, up_feat], axis=2)
    return (handed[None], features[None])


def solution(mesh):
    in_specs = (
        P("section", ("groups", "dp"), None),
        P("section", ("groups", "dp"), None),
        P("section", ("groups", "dp"), None),
        P("section", "dp", None, "tensor"),
        P("section", "dp", "tensor", None),
        P("section", ("groups", "dp"), None, None, "tensor"),
        P("section", ("groups", "dp"), None),
        P("section", None, None),
        P("section", "dp", "tensor", None),
        P("section", ("groups", "dp"), None),
    )
    out_specs = (P("section", ("groups", "dp"), None), P("section", ("groups", "dp"), None, None))
    return jax.shard_map(
        per_device, mesh=mesh, in_specs=in_specs, out_specs=out_specs, check_vma=False
    )
```

```python
import functools

import jax
import jax.numpy as jnp
from jax import lax
from jax.experimental import pallas as pl
from jax.experimental.pallas import tpu as pltpu
from jax.sharding import PartitionSpec as P

EXPERTS = 4
CHUNKS = 2
NT = (((1,), (1,)), ((), ()))


def xored(block, axis, bits):
    n = lax.axis_size(axis)
    return lax.ppermute(block, axis, [(i, i ^ bits) for i in range(n)])


ANYWHERE = pl.BlockSpec(memory_space=pl.ANY)
RESIDENT = pl.BlockSpec(memory_space=pltpu.VMEM)


def held_kernel(block_ref, *refs):
    refs[-1][...] = block_ref[...]


def held(block, *events):
    return pl.pallas_call(
        held_kernel,
        in_specs=[RESIDENT] + [ANYWHERE] * len(events),
        out_specs=RESIDENT,
        out_shape=jax.ShapeDtypeStruct(block.shape, block.dtype),
        compiler_params=pltpu.CompilerParams(vmem_limit_bytes=1 << 20),
        name="held",
    )(block, *events)


def merge_kernel(others, keep_ref, came_ref, *refs):
    own_ref, *sent_refs = refs[-1 - others :]
    rows = own_ref.shape[0]
    own_ref[...] = keep_ref[:rows] + came_ref[:rows].astype(jnp.float32)
    for at, sent_ref in enumerate(sent_refs):
        part = slice((at + 1) * rows, (at + 2) * rows)
        total = keep_ref[part] + came_ref[part].astype(jnp.float32)
        sent_ref[...] = total.astype(jnp.bfloat16)


def merged(keep, came, rows, *events):
    count, wide = keep.shape
    others = count // rows - 1
    return pl.pallas_call(
        functools.partial(merge_kernel, others),
        in_specs=[RESIDENT] * 2 + [ANYWHERE] * len(events),
        out_specs=[RESIDENT] * (1 + others),
        out_shape=[jax.ShapeDtypeStruct((rows, wide), jnp.float32)]
        + [jax.ShapeDtypeStruct((rows, wide), jnp.bfloat16)] * others,
        compiler_params=pltpu.CompilerParams(vmem_limit_bytes=4 << 20),
        cost_estimate=pl.CostEstimate(
            flops=count * wide, bytes_accessed=8 * count * wide, transcendentals=0
        ),
        name="merge",
    )(keep, came, *events)


def finish_kernel(slots, own_ref, cot_ref, weight_ref, *refs):
    grad_ref, vec_ref = refs[-2:]
    width = grad_ref.shape[1]
    total = weight_ref[:, :1] * own_ref[...]
    for slot in range(1, slots):
        back = refs[slots - 1 - slot][...].astype(jnp.float32)
        total += weight_ref[:, slot : slot + 1] * back
    grad_ref[...] = (cot_ref[...].astype(jnp.float32) + total[:, :width]).astype(jnp.bfloat16)
    vec_ref[...] = total[:, width:]


def finished(own, cot, weight, backs, *events):
    rows, wide = own.shape
    width = cot.shape[1]
    return pl.pallas_call(
        functools.partial(finish_kernel, 1 + len(backs)),
        in_specs=[RESIDENT] * (3 + len(backs)) + [ANYWHERE] * len(events),
        out_specs=[RESIDENT] * 2,
        out_shape=[
            jax.ShapeDtypeStruct((rows, width), jnp.bfloat16),
            jax.ShapeDtypeStruct((rows, wide - width), jnp.float32),
        ],
        compiler_params=pltpu.CompilerParams(vmem_limit_bytes=4 << 20),
        cost_estimate=pl.CostEstimate(
            flops=8 * rows * wide, bytes_accessed=12 * rows * wide, transcendentals=0
        ),
        name="finish",
    )(own, cot, weight, *backs, *events)


def tile_of(size, most):
    best = 128
    for tile in range(128, most + 1, 128):
        if size % tile == 0:
            best = tile
    return best


def slope_kernel(groups, index_ref, *refs):
    del index_ref
    pre_refs, sketch_ref, weight_hbm = refs[:groups], refs[groups], refs[groups + 1]
    slope_ref, down_ref, weight_ref, weight_sem = refs[-4:]
    load = pltpu.make_async_copy(weight_hbm, weight_ref, weight_sem)

    @pl.when((pl.program_id(0) == 0) & (pl.program_id(1) == 0))
    def _():
        load.start()

    pre = jnp.concatenate([r[0, 0, 0] for r in pre_refs], axis=0).astype(jnp.float32)
    sig = 0.5 + 0.5 * jnp.tanh(0.5 * pre)
    hidden = pre * sig
    slope = sig + hidden * (1.0 - sig)
    slope_ref[0] = slope.T.astype(slope_ref.dtype)
    term = lax.dot_general(
        hidden.astype(jnp.bfloat16), sketch_ref[...], NT, preferred_element_type=jnp.float32
    )

    @pl.when(pl.program_id(1) == 0)
    def _():
        down_ref[...] = jnp.zeros_like(down_ref)

    down_ref[0] += term

    @pl.when(
        (pl.program_id(0) == pl.num_programs(0) - 1) & (pl.program_id(1) == pl.num_programs(1) - 1)
    )
    def _():
        load.wait()


def slopes(pre, sketch_t, weight, place, core):
    n, _, chunks, rows, cols = pre.shape
    rank = sketch_t.shape[0]
    groups = 2 * n
    tile = tile_of(cols, 896)
    index = jnp.stack([place, core]).astype(jnp.int32)
    weight = pltpu.with_memory_space_constraint(weight, pltpu.HBM)

    def spec_of(h, slot):
        return pl.BlockSpec(
            (1, 1, 1, rows, tile), lambda a, j, ix: (ix[0] ^ slot, ix[1] ^ h, a, 0, j)
        )

    return pl.pallas_call(
        functools.partial(slope_kernel, groups),
        grid_spec=pltpu.PrefetchScalarGridSpec(
            num_scalar_prefetch=1,
            grid=(chunks, cols // tile),
            in_specs=[spec_of(h, slot) for h in range(2) for slot in range(n)]
            + [pl.BlockSpec((rank, tile), lambda a, j, ix: (0, j))]
            + [pl.BlockSpec(memory_space=pltpu.HBM)],
            out_specs=[
                pl.BlockSpec((1, tile, groups * rows), lambda a, j, ix: (a, j, 0)),
                pl.BlockSpec((1, groups * rows, rank), lambda a, j, ix: (a, 0, 0)),
                RESIDENT,
            ],
            scratch_shapes=[pltpu.SemaphoreType.DMA],
        ),
        out_shape=[
            jax.ShapeDtypeStruct((chunks, cols, groups * rows), jnp.bfloat16),
            jax.ShapeDtypeStruct((chunks, groups * rows, rank), jnp.float32),
            jax.ShapeDtypeStruct(weight.shape, weight.dtype),
        ],
        cost_estimate=pl.CostEstimate(
            flops=2 * chunks * groups * rows * cols * rank,
            bytes_accessed=4 * chunks * groups * rows * cols,
            transcendentals=chunks * groups * rows * cols,
        ),
        compiler_params=pltpu.CompilerParams(vmem_limit_bytes=7 << 20),
        name="slopes",
    )(index, *([pre] * groups), sketch_t, weight)


def expert_kernel(
    chunk, tile_f, tile_d, rows_ref, slope_ref, down_part_ref, sketch_ref, down_ref, up_hbm, *refs
):
    keep_ref, give_ref, rows_buf, grad_buf, up_buf, up_sem = refs[-6:]
    hidden_cols, width = down_ref.shape
    steps_f, steps_d = hidden_cols // tile_f, width // tile_d
    half = keep_ref.shape[0]

    def tile(j, size):
        return pl.ds(pl.multiple_of(j * size, size), size)

    def up_copy(j):
        part = tile(j, tile_d)
        return pltpu.make_async_copy(up_hbm.at[part], up_buf.at[part], up_sem.at[j])

    for j in range(steps_d):
        if j == 0 or j > steps_f:
            up_copy(j).start()
    rows_buf[...] = rows_ref[...].T

    def first(j, carry):
        @pl.when(j + 1 < steps_d)
        def _():
            up_copy(j + 1).start()

        part = tile(j, tile_f)
        grad_hidden = jnp.dot(
            down_ref[part, :], rows_buf[...], preferred_element_type=jnp.float32
        )
        slope = slope_ref[chunk, part, :].astype(jnp.float32)
        grad_buf[part, :] = (grad_hidden * slope).astype(jnp.bfloat16)
        return carry

    lax.fori_loop(0, steps_f, first, 0)

    up_part = jnp.dot(sketch_ref[...], grad_buf[...], preferred_element_type=jnp.float32).T
    vectors = jnp.concatenate([down_part_ref[chunk], up_part], axis=1)
    keep_ref[:, width:] = vectors[:half]
    give_ref[:, width:] = vectors[half:].astype(jnp.bfloat16)

    def second(j, carry):
        up_copy(j).wait()
        part = tile(j, tile_d)
        term = jnp.dot(up_buf[part, :], grad_buf[...], preferred_element_type=jnp.float32).T
        keep_ref[:, part] = term[:half]
        give_ref[:, part] = term[half:].astype(jnp.bfloat16)
        return carry

    lax.fori_loop(0, steps_d, second, 0)


def expert(chunk, rows, slope, down_part, sketch_t, down_local, up_local, *events):
    count, width = rows.shape
    hidden_cols = down_local.shape[0]
    rank = sketch_t.shape[0]
    wide = width + 2 * rank
    tile_f, tile_d = tile_of(hidden_cols, 1792), tile_of(width, 1024)
    up_local = pltpu.with_memory_space_constraint(up_local, pltpu.HBM)
    return pl.pallas_call(
        functools.partial(expert_kernel, chunk, tile_f, tile_d),
        in_specs=[RESIDENT] * 5
        + [pl.BlockSpec(memory_space=pltpu.HBM)]
        + [ANYWHERE] * len(events),
        out_specs=[RESIDENT] * 2,
        out_shape=[
            jax.ShapeDtypeStruct((count // 2, wide), jnp.float32),
            jax.ShapeDtypeStruct((count // 2, wide), jnp.bfloat16),
        ],
        scratch_shapes=[
            pltpu.VMEM((width, count), jnp.bfloat16),
            pltpu.VMEM((hidden_cols, count), jnp.bfloat16),
            pltpu.VMEM((width, hidden_cols), jnp.bfloat16),
            pltpu.SemaphoreType.DMA((width // tile_d,)),
        ],
        compiler_params=pltpu.CompilerParams(vmem_limit_bytes=26 << 20),
        cost_estimate=pl.CostEstimate(
            flops=4 * count * hidden_cols * width,
            bytes_accessed=4 * hidden_cols * width,
            transcendentals=0,
        ),
        name="expert",
    )(rows, slope, down_part, sketch_t, down_local, up_local, *events)


def per_device(
    cotangent,
    routes,
    gate_values,
    up_weight,
    down_weight,
    pre_activation,
    input_sketch,
    model_sketch,
    hidden_sketch,
    lengths,
):
    pieces = lax.axis_size("dp")
    sections = lax.axis_size("section")
    per_expert = pieces // EXPERTS
    place = lax.axis_index("dp")
    core = lax.axis_index("tensor")
    cot = cotangent[0]
    tok_dev, width = cot.shape
    half = tok_dev // 2
    rows = half // CHUNKS
    rank = model_sketch.shape[2]
    blocks = routes.shape[1]
    block_len = tok_dev // blocks
    sketch_local = hidden_sketch[0, 0]
    pre_all = pre_activation[0, 0]
    hidden_cols = pre_all.shape[2]
    pre_all = pre_all.reshape(pieces, 2, CHUNKS, rows, hidden_cols)

    def below(block):
        return lax.ppermute(block, "section", [(s, (s - 1) % sections) for s in range(sections)])

    token_routes = jnp.broadcast_to(routes[0][:, None, :], (blocks, block_len, 2)).reshape(
        tok_dev, 2
    )
    half_routes = lax.dynamic_slice_in_dim(token_routes, core * half, half, 0)
    half_gates = lax.dynamic_slice_in_dim(gate_values[0], core * half, half, 0)
    slot_expert = (place ^ jnp.arange(pieces, dtype=jnp.int32)) // per_expert
    hits = half_routes[:, None, :] == slot_expert[None, :, None]
    weight = jnp.sum(jnp.where(hits, half_gates[:, None, :], 0.0), axis=2)

    sketch_t = sketch_local.T
    cot_mine = lax.dynamic_slice_in_dim(cot, core * half, half, 0)
    cot_theirs = lax.dynamic_slice_in_dim(cot, (1 - core) * half, half, 0)
    order = sorted(range(2, pieces), reverse=True)
    slope, down_part, down_here = slopes(pre_all, sketch_t, down_weight[0, 0], place, core)
    near_rows = xored(cot_mine, "dp", 1)
    fetched = {slot: xored(cot_mine[:rows], "dp", slot) for slot in order}
    own, sent, grad, passed, backs = (), (), (), (), ()
    below_mine, vectors = [], []
    for a in range(CHUNKS):
        part = slice(a * rows, (a + 1) * rows)
        blocks = [fetched[slot] for slot in order] + [near_rows] * (a == 0)
        blocks = jnp.concatenate(blocks, axis=0)
        if a > 0:
            blocks = held(blocks, own)
        traded = xored(blocks, "tensor", 1)
        mine = dict(fetched)
        theirs = {slot: traded[at * rows : (at + 1) * rows] for at, slot in enumerate(order)}
        if a == 0:
            near_theirs = traded[len(order) * rows :]
        mine[0], mine[1] = cot_mine[part], near_rows[part]
        theirs[0], theirs[1] = cot_theirs[part], near_theirs[part]
        rows_in = jnp.concatenate(
            [mine[k] for k in range(pieces)] + [theirs[k] for k in range(pieces)], axis=0
        )

        kept, give = expert(
            a, rows_in, slope, down_part, sketch_t, down_here, up_weight[0, 0], *sent
        )
        if a + 1 < CHUNKS:
            coming = held(cot_mine[(a + 1) * rows : (a + 2) * rows], near_rows)
            fetched = {slot: held(xored(coming, "dp", slot), kept) for slot in order}
            late = tuple(fetched.values())
        else:
            give, late = held(give, *backs), grad
        own, *sent = merged(kept, xored(give, "tensor", 1), rows, *late)
        backs = [xored(out, "dp", slot + 1) for slot, out in enumerate(sent)][::-1]
        if grad:
            passed = (below(held(*grad, backs[0])),)
            below_mine.append(*passed)
        new, vec = finished(own, cot_mine[part], weight[part], backs, *passed)
        grad = (new,)
        vectors.append(vec)
    below_mine.append(below(*grad))

    theirs = [xored(block, "tensor", 1) for block in below_mine]
    first = [jnp.where(core == 0, m, t) for m, t in zip(below_mine, theirs)]
    second = [jnp.where(core == 0, t, m) for m, t in zip(below_mine, theirs)]
    handed = jnp.concatenate(first + second, axis=0)

    vec_mine = jnp.concatenate(vectors, axis=0)
    vec_theirs = xored(vec_mine, "tensor", 1)
    sketch_sum = jnp.concatenate(
        [jnp.where(core == 0, vec_mine, vec_theirs), jnp.where(core == 0, vec_theirs, vec_mine)],
        axis=0,
    )
    out_vec = jnp.dot(cot, model_sketch[0], preferred_element_type=jnp.float32)
    counts = lengths[0, 0]
    upto = jnp.arange(counts.shape[0])
    ends = jnp.sum(jnp.where(upto[None, :] <= upto[:, None], counts[None, :], 0), axis=1)
    starts = ends - counts
    position = jnp.arange(tok_dev, dtype=jnp.int32)
    member = ((position[None, :] >= starts[:, None]) & (position[None, :] < ends[:, None])).astype(
        jnp.float32
    )
    down_feat = jnp.einsum(
        "et,ta,tb->eab", member, out_vec, sketch_sum[:, :rank], precision=lax.Precision.HIGHEST
    )
    up_feat = jnp.einsum(
        "et,ta,tb->eab",
        member,
        sketch_sum[:, rank:],
        input_sketch[0],
        precision=lax.Precision.HIGHEST,
    )
    features = jnp.concatenate([down_feat, up_feat], axis=2)
    return (handed[None], features[None])


def solution(mesh):
    in_specs = (
        P("section", ("groups", "dp"), None),
        P("section", ("groups", "dp"), None),
        P("section", ("groups", "dp"), None),
        P("section", "dp", None, "tensor"),
        P("section", "dp", "tensor", None),
        P("section", ("groups", "dp"), None, None, "tensor"),
        P("section", ("groups", "dp"), None),
        P("section", None, None),
        P("section", "dp", "tensor", None),
        P("section", ("groups", "dp"), None),
    )
    out_specs = (P("section", ("groups", "dp"), None), P("section", ("groups", "dp"), None, None))
    return jax.shard_map(
        per_device, mesh=mesh, in_specs=in_specs, out_specs=out_specs, check_vma=False
    )
```

```python
import functools

import jax
import jax.numpy as jnp
from jax import lax
from jax.experimental import pallas as pl
from jax.experimental.pallas import tpu as pltpu
from jax.sharding import PartitionSpec as P

EXPERTS = 4
CHUNKS = 2
NT = (((1,), (1,)), ((), ()))


def xored(block, axis, bits):
    n = lax.axis_size(axis)
    return lax.ppermute(block, axis, [(i, i ^ bits) for i in range(n)])


ANYWHERE = pl.BlockSpec(memory_space=pl.ANY)
RESIDENT = pl.BlockSpec(memory_space=pltpu.VMEM)


def held_kernel(block_ref, *refs):
    refs[-1][...] = block_ref[...]


def held(block, *events):
    return pl.pallas_call(
        held_kernel,
        in_specs=[RESIDENT] + [ANYWHERE] * len(events),
        out_specs=RESIDENT,
        out_shape=jax.ShapeDtypeStruct(block.shape, block.dtype),
        compiler_params=pltpu.CompilerParams(vmem_limit_bytes=1 << 20),
        name="held",
    )(block, *events)


def merge_kernel(others, keep_ref, came_ref, *refs):
    own_ref, *sent_refs = refs[-1 - others :]
    rows = own_ref.shape[0]
    own_ref[...] = keep_ref[:rows] + came_ref[:rows].astype(jnp.float32)
    for at, sent_ref in enumerate(sent_refs):
        part = slice((at + 1) * rows, (at + 2) * rows)
        total = keep_ref[part] + came_ref[part].astype(jnp.float32)
        sent_ref[...] = total.astype(jnp.bfloat16)


def merged(keep, came, rows, *events):
    count, wide = keep.shape
    others = count // rows - 1
    return pl.pallas_call(
        functools.partial(merge_kernel, others),
        in_specs=[RESIDENT] * 2 + [ANYWHERE] * len(events),
        out_specs=[RESIDENT] * (1 + others),
        out_shape=[jax.ShapeDtypeStruct((rows, wide), jnp.float32)]
        + [jax.ShapeDtypeStruct((rows, wide), jnp.bfloat16)] * others,
        compiler_params=pltpu.CompilerParams(vmem_limit_bytes=4 << 20),
        cost_estimate=pl.CostEstimate(
            flops=count * wide, bytes_accessed=8 * count * wide, transcendentals=0
        ),
        name="merge",
    )(keep, came, *events)


def finish_kernel(slots, own_ref, cot_ref, weight_ref, *refs):
    grad_ref, vec_ref = refs[-2:]
    width = grad_ref.shape[1]
    total = weight_ref[:, :1] * own_ref[...]
    for slot in range(1, slots):
        back = refs[slots - 1 - slot][...].astype(jnp.float32)
        total += weight_ref[:, slot : slot + 1] * back
    grad_ref[...] = (cot_ref[...].astype(jnp.float32) + total[:, :width]).astype(jnp.bfloat16)
    vec_ref[...] = total[:, width:]


def finished(own, cot, weight, backs, *events):
    rows, wide = own.shape
    width = cot.shape[1]
    return pl.pallas_call(
        functools.partial(finish_kernel, 1 + len(backs)),
        in_specs=[RESIDENT] * (3 + len(backs)) + [ANYWHERE] * len(events),
        out_specs=[RESIDENT] * 2,
        out_shape=[
            jax.ShapeDtypeStruct((rows, width), jnp.bfloat16),
            jax.ShapeDtypeStruct((rows, wide - width), jnp.float32),
        ],
        compiler_params=pltpu.CompilerParams(vmem_limit_bytes=4 << 20),
        cost_estimate=pl.CostEstimate(
            flops=8 * rows * wide, bytes_accessed=12 * rows * wide, transcendentals=0
        ),
        name="finish",
    )(own, cot, weight, *backs, *events)


def tile_of(size, most):
    best = 128
    for tile in range(128, most + 1, 128):
        if size % tile == 0:
            best = tile
    return best


def slope_kernel(groups, index_ref, *refs):
    del index_ref
    pre_refs, sketch_ref, weight_hbm = refs[:groups], refs[groups], refs[groups + 1]
    slope_ref, down_ref, weight_ref, weight_sem = refs[-4:]
    load = pltpu.make_async_copy(weight_hbm, weight_ref, weight_sem)

    @pl.when((pl.program_id(0) == 0) & (pl.program_id(1) == 0))
    def _():
        load.start()

    pre = jnp.concatenate([r[0, 0, 0] for r in pre_refs], axis=0).astype(jnp.float32)
    sig = 0.5 + 0.5 * jnp.tanh(0.5 * pre)
    hidden = pre * sig
    slope = sig + hidden * (1.0 - sig)
    slope_ref[0] = slope.T.astype(slope_ref.dtype)
    term = lax.dot_general(
        hidden.astype(jnp.bfloat16), sketch_ref[...], NT, preferred_element_type=jnp.float32
    )

    @pl.when(pl.program_id(1) == 0)
    def _():
        down_ref[...] = jnp.zeros_like(down_ref)

    down_ref[0] += term

    @pl.when(
        (pl.program_id(0) == pl.num_programs(0) - 1) & (pl.program_id(1) == pl.num_programs(1) - 1)
    )
    def _():
        load.wait()


def slopes(pre, sketch_t, weight, place, core):
    n, _, chunks, rows, cols = pre.shape
    rank = sketch_t.shape[0]
    groups = 2 * n
    tile = tile_of(cols, 896)
    index = jnp.stack([place, core]).astype(jnp.int32)
    weight = pltpu.with_memory_space_constraint(weight, pltpu.HBM)

    def spec_of(h, slot):
        return pl.BlockSpec(
            (1, 1, 1, rows, tile), lambda a, j, ix: (ix[0] ^ slot, ix[1] ^ h, a, 0, j)
        )

    return pl.pallas_call(
        functools.partial(slope_kernel, groups),
        grid_spec=pltpu.PrefetchScalarGridSpec(
            num_scalar_prefetch=1,
            grid=(chunks, cols // tile),
            in_specs=[spec_of(h, slot) for h in range(2) for slot in range(n)]
            + [pl.BlockSpec((rank, tile), lambda a, j, ix: (0, j))]
            + [pl.BlockSpec(memory_space=pltpu.HBM)],
            out_specs=[
                pl.BlockSpec((1, tile, groups * rows), lambda a, j, ix: (a, j, 0)),
                pl.BlockSpec((1, groups * rows, rank), lambda a, j, ix: (a, 0, 0)),
                RESIDENT,
            ],
            scratch_shapes=[pltpu.SemaphoreType.DMA],
        ),
        out_shape=[
            jax.ShapeDtypeStruct((chunks, cols, groups * rows), jnp.bfloat16),
            jax.ShapeDtypeStruct((chunks, groups * rows, rank), jnp.float32),
            jax.ShapeDtypeStruct(weight.shape, weight.dtype),
        ],
        cost_estimate=pl.CostEstimate(
            flops=2 * chunks * groups * rows * cols * rank,
            bytes_accessed=4 * chunks * groups * rows * cols,
            transcendentals=chunks * groups * rows * cols,
        ),
        compiler_params=pltpu.CompilerParams(vmem_limit_bytes=7 << 20),
        name="slopes",
    )(index, *([pre] * groups), sketch_t, weight)


def expert_kernel(
    chunk, tile_f, tile_d, rows_ref, slope_ref, down_part_ref, sketch_ref, down_ref, up_hbm, *refs
):
    keep_ref, give_ref, rows_buf, grad_buf, up_buf, up_sem = refs[-6:]
    hidden_cols, width = down_ref.shape
    steps_f, steps_d = hidden_cols // tile_f, width // tile_d
    half = keep_ref.shape[0]

    def tile(j, size):
        return pl.ds(pl.multiple_of(j * size, size), size)

    def up_copy(j):
        part = tile(j, tile_d)
        return pltpu.make_async_copy(up_hbm.at[part], up_buf.at[part], up_sem.at[j])

    for j in range(steps_d):
        if j == 0 or j > steps_f:
            up_copy(j).start()
    rows_buf[...] = rows_ref[...].T

    def first(j, carry):
        @pl.when(j + 1 < steps_d)
        def _():
            up_copy(j + 1).start()

        part = tile(j, tile_f)
        grad_hidden = jnp.dot(
            down_ref[part, :], rows_buf[...], preferred_element_type=jnp.float32
        )
        slope = slope_ref[chunk, part, :].astype(jnp.float32)
        grad_buf[part, :] = (grad_hidden * slope).astype(jnp.bfloat16)
        return carry

    lax.fori_loop(0, steps_f, first, 0)

    up_part = jnp.dot(sketch_ref[...], grad_buf[...], preferred_element_type=jnp.float32).T
    vectors = jnp.concatenate([down_part_ref[chunk], up_part], axis=1)
    keep_ref[:, width:] = vectors[:half]
    give_ref[:, width:] = vectors[half:].astype(jnp.bfloat16)

    def second(j, carry):
        up_copy(j).wait()
        part = tile(j, tile_d)
        term = jnp.dot(up_buf[part, :], grad_buf[...], preferred_element_type=jnp.float32).T
        keep_ref[:, part] = term[:half]
        give_ref[:, part] = term[half:].astype(jnp.bfloat16)
        return carry

    lax.fori_loop(0, steps_d, second, 0)


def expert(chunk, rows, slope, down_part, sketch_t, down_local, up_local, *events):
    count, width = rows.shape
    hidden_cols = down_local.shape[0]
    rank = sketch_t.shape[0]
    wide = width + 2 * rank
    tile_f, tile_d = tile_of(hidden_cols, 1792), tile_of(width, 1024)
    up_local = pltpu.with_memory_space_constraint(up_local, pltpu.HBM)
    return pl.pallas_call(
        functools.partial(expert_kernel, chunk, tile_f, tile_d),
        in_specs=[RESIDENT] * 5
        + [pl.BlockSpec(memory_space=pltpu.HBM)]
        + [ANYWHERE] * len(events),
        out_specs=[RESIDENT] * 2,
        out_shape=[
            jax.ShapeDtypeStruct((count // 2, wide), jnp.float32),
            jax.ShapeDtypeStruct((count // 2, wide), jnp.bfloat16),
        ],
        scratch_shapes=[
            pltpu.VMEM((width, count), jnp.bfloat16),
            pltpu.VMEM((hidden_cols, count), jnp.bfloat16),
            pltpu.VMEM((width, hidden_cols), jnp.bfloat16),
            pltpu.SemaphoreType.DMA((width // tile_d,)),
        ],
        compiler_params=pltpu.CompilerParams(vmem_limit_bytes=26 << 20),
        cost_estimate=pl.CostEstimate(
            flops=4 * count * hidden_cols * width,
            bytes_accessed=4 * hidden_cols * width,
            transcendentals=0,
        ),
        name="expert",
    )(rows, slope, down_part, sketch_t, down_local, up_local, *events)


def per_device(
    cotangent,
    routes,
    gate_values,
    up_weight,
    down_weight,
    pre_activation,
    input_sketch,
    model_sketch,
    hidden_sketch,
    lengths,
):
    pieces = lax.axis_size("dp")
    sections = lax.axis_size("section")
    per_expert = pieces // EXPERTS
    place = lax.axis_index("dp")
    core = lax.axis_index("tensor")
    cot = cotangent[0]
    tok_dev, width = cot.shape
    half = tok_dev // 2
    rows = half // CHUNKS
    rank = model_sketch.shape[2]
    blocks = routes.shape[1]
    block_len = tok_dev // blocks
    sketch_local = hidden_sketch[0, 0]
    pre_all = pre_activation[0, 0]
    hidden_cols = pre_all.shape[2]
    pre_all = pre_all.reshape(pieces, 2, CHUNKS, rows, hidden_cols)

    def below(block):
        return lax.ppermute(block, "section", [(s, (s - 1) % sections) for s in range(sections)])

    token_routes = jnp.broadcast_to(routes[0][:, None, :], (blocks, block_len, 2)).reshape(
        tok_dev, 2
    )
    half_routes = lax.dynamic_slice_in_dim(token_routes, core * half, half, 0)
    half_gates = lax.dynamic_slice_in_dim(gate_values[0], core * half, half, 0)
    slot_expert = (place ^ jnp.arange(pieces, dtype=jnp.int32)) // per_expert
    hits = half_routes[:, None, :] == slot_expert[None, :, None]
    weight = jnp.sum(jnp.where(hits, half_gates[:, None, :], 0.0), axis=2)

    sketch_t = sketch_local.T
    cot_mine = lax.dynamic_slice_in_dim(cot, core * half, half, 0)
    cot_theirs = lax.dynamic_slice_in_dim(cot, (1 - core) * half, half, 0)
    order = sorted(range(2, pieces), reverse=True)
    slope, down_part, down_here = slopes(pre_all, sketch_t, down_weight[0, 0], place, core)
    near_rows = xored(cot_mine, "dp", 1)
    fetched = {slot: xored(cot_mine[:rows], "dp", slot) for slot in order}
    out_vec = jnp.dot(cot, model_sketch[0], preferred_element_type=jnp.float32)
    own, sent, grad, passed, backs = (), (out_vec,), (), (), ()
    below_mine, vectors = [], []
    for a in range(CHUNKS):
        part = slice(a * rows, (a + 1) * rows)
        blocks = [fetched[slot] for slot in order] + [near_rows] * (a == 0)
        blocks = jnp.concatenate(blocks, axis=0)
        if a > 0:
            blocks = held(blocks, own)
        traded = xored(blocks, "tensor", 1)
        mine = dict(fetched)
        theirs = {slot: traded[at * rows : (at + 1) * rows] for at, slot in enumerate(order)}
        if a == 0:
            near_theirs = traded[len(order) * rows :]
        mine[0], mine[1] = cot_mine[part], near_rows[part]
        theirs[0], theirs[1] = cot_theirs[part], near_theirs[part]
        rows_in = jnp.concatenate(
            [mine[k] for k in range(pieces)] + [theirs[k] for k in range(pieces)], axis=0
        )

        kept, give = expert(
            a, rows_in, slope, down_part, sketch_t, down_here, up_weight[0, 0], *sent
        )
        if a + 1 < CHUNKS:
            coming = held(cot_mine[(a + 1) * rows : (a + 2) * rows], near_rows)
            fetched = {slot: held(xored(coming, "dp", slot), kept) for slot in order}
            late = tuple(fetched.values())
        else:
            give, late = held(give, *backs), grad
        own, *sent = merged(kept, xored(give, "tensor", 1), rows, *late)
        backs = [xored(out, "dp", slot + 1) for slot, out in enumerate(sent)][::-1]
        if grad:
            passed = (below(held(*grad, backs[0])),)
            below_mine.append(*passed)
        new, vec = finished(own, cot_mine[part], weight[part], backs, *passed)
        grad = (new,)
        vectors.append(vec)
    below_mine.append(below(*grad))

    theirs = [xored(block, "tensor", 1) for block in below_mine]
    first = [jnp.where(core == 0, m, t) for m, t in zip(below_mine, theirs)]
    second = [jnp.where(core == 0, t, m) for m, t in zip(below_mine, theirs)]
    handed = jnp.concatenate(first + second, axis=0)

    vec_mine = jnp.concatenate(vectors, axis=0)
    vec_theirs = xored(vec_mine, "tensor", 1)
    sketch_sum = jnp.concatenate(
        [jnp.where(core == 0, vec_mine, vec_theirs), jnp.where(core == 0, vec_theirs, vec_mine)],
        axis=0,
    )
    counts = lengths[0, 0]
    upto = jnp.arange(counts.shape[0])
    ends = jnp.sum(jnp.where(upto[None, :] <= upto[:, None], counts[None, :], 0), axis=1)
    starts = ends - counts
    position = jnp.arange(tok_dev, dtype=jnp.int32)
    member = ((position[None, :] >= starts[:, None]) & (position[None, :] < ends[:, None])).astype(
        jnp.float32
    )
    down_feat = jnp.einsum(
        "et,ta,tb->eab", member, out_vec, sketch_sum[:, :rank], precision=lax.Precision.HIGHEST
    )
    up_feat = jnp.einsum(
        "et,ta,tb->eab",
        member,
        sketch_sum[:, rank:],
        input_sketch[0],
        precision=lax.Precision.HIGHEST,
    )
    features = jnp.concatenate([down_feat, up_feat], axis=2)
    return (handed[None], features[None])


def solution(mesh):
    in_specs = (
        P("section", ("groups", "dp"), None),
        P("section", ("groups", "dp"), None),
        P("section", ("groups", "dp"), None),
        P("section", "dp", None, "tensor"),
        P("section", "dp", "tensor", None),
        P("section", ("groups", "dp"), None, None, "tensor"),
        P("section", ("groups", "dp"), None),
        P("section", None, None),
        P("section", "dp", "tensor", None),
        P("section", ("groups", "dp"), None),
    )
    out_specs = (P("section", ("groups", "dp"), None), P("section", ("groups", "dp"), None, None))
    return jax.shard_map(
        per_device, mesh=mesh, in_specs=in_specs, out_specs=out_specs, check_vma=False
    )
```

```python
import functools

import jax
import jax.numpy as jnp
from jax import lax
from jax.experimental import pallas as pl
from jax.experimental.pallas import tpu as pltpu
from jax.sharding import PartitionSpec as P

EXPERTS = 4
CHUNKS = 2
NT = (((1,), (1,)), ((), ()))


def xored(block, axis, bits):
    n = lax.axis_size(axis)
    return lax.ppermute(block, axis, [(i, i ^ bits) for i in range(n)])


ANYWHERE = pl.BlockSpec(memory_space=pl.ANY)
RESIDENT = pl.BlockSpec(memory_space=pltpu.VMEM)


def held_kernel(block_ref, *refs):
    refs[-1][...] = block_ref[...]


def held(block, *events):
    return pl.pallas_call(
        held_kernel,
        in_specs=[RESIDENT] + [ANYWHERE] * len(events),
        out_specs=RESIDENT,
        out_shape=jax.ShapeDtypeStruct(block.shape, block.dtype),
        compiler_params=pltpu.CompilerParams(vmem_limit_bytes=1 << 20),
        name="held",
    )(block, *events)


def merge_kernel(others, keep_ref, came_ref, *refs):
    own_ref, *sent_refs = refs[-1 - others :]
    rows = own_ref.shape[0]
    own_ref[...] = keep_ref[:rows] + came_ref[:rows].astype(jnp.float32)
    for at, sent_ref in enumerate(sent_refs):
        part = slice((at + 1) * rows, (at + 2) * rows)
        total = keep_ref[part] + came_ref[part].astype(jnp.float32)
        sent_ref[...] = total.astype(jnp.bfloat16)


def merged(keep, came, rows, *events):
    count, wide = keep.shape
    others = count // rows - 1
    return pl.pallas_call(
        functools.partial(merge_kernel, others),
        in_specs=[RESIDENT] * 2 + [ANYWHERE] * len(events),
        out_specs=[RESIDENT] * (1 + others),
        out_shape=[jax.ShapeDtypeStruct((rows, wide), jnp.float32)]
        + [jax.ShapeDtypeStruct((rows, wide), jnp.bfloat16)] * others,
        compiler_params=pltpu.CompilerParams(vmem_limit_bytes=4 << 20),
        cost_estimate=pl.CostEstimate(
            flops=count * wide, bytes_accessed=8 * count * wide, transcendentals=0
        ),
        name="merge",
    )(keep, came, *events)


def finish_kernel(slots, own_ref, cot_ref, weight_ref, *refs):
    grad_ref, vec_ref = refs[-2:]
    width = grad_ref.shape[1]
    total = weight_ref[:, :1] * own_ref[...]
    for slot in range(1, slots):
        back = refs[slots - 1 - slot][...].astype(jnp.float32)
        total += weight_ref[:, slot : slot + 1] * back
    grad_ref[...] = (cot_ref[...].astype(jnp.float32) + total[:, :width]).astype(jnp.bfloat16)
    vec_ref[...] = total[:, width:]


def finished(own, cot, weight, backs, *events):
    rows, wide = own.shape
    width = cot.shape[1]
    return pl.pallas_call(
        functools.partial(finish_kernel, 1 + len(backs)),
        in_specs=[RESIDENT] * (3 + len(backs)) + [ANYWHERE] * len(events),
        out_specs=[RESIDENT] * 2,
        out_shape=[
            jax.ShapeDtypeStruct((rows, width), jnp.bfloat16),
            jax.ShapeDtypeStruct((rows, wide - width), jnp.float32),
        ],
        compiler_params=pltpu.CompilerParams(vmem_limit_bytes=4 << 20),
        cost_estimate=pl.CostEstimate(
            flops=8 * rows * wide, bytes_accessed=12 * rows * wide, transcendentals=0
        ),
        name="finish",
    )(own, cot, weight, *backs, *events)


def tile_of(size, most):
    best = 128
    for tile in range(128, most + 1, 128):
        if size % tile == 0:
            best = tile
    return best


def slope_kernel(groups, index_ref, *refs):
    del index_ref
    pre_refs, sketch_ref, weight_hbm = refs[:groups], refs[groups], refs[groups + 1]
    slope_ref, down_ref, weight_ref, weight_sem = refs[-4:]
    load = pltpu.make_async_copy(weight_hbm, weight_ref, weight_sem)

    @pl.when((pl.program_id(0) == 0) & (pl.program_id(1) == 0))
    def _():
        load.start()

    pre = jnp.concatenate([r[0, 0, 0] for r in pre_refs], axis=0).astype(jnp.float32)
    sig = 0.5 + 0.5 * jnp.tanh(0.5 * pre)
    hidden = pre * sig
    slope = sig + hidden * (1.0 - sig)
    slope_ref[0] = slope.T.astype(slope_ref.dtype)
    term = lax.dot_general(
        hidden.astype(jnp.bfloat16), sketch_ref[...], NT, preferred_element_type=jnp.float32
    )

    @pl.when(pl.program_id(1) == 0)
    def _():
        down_ref[...] = jnp.zeros_like(down_ref)

    down_ref[0] += term

    @pl.when(
        (pl.program_id(0) == pl.num_programs(0) - 1) & (pl.program_id(1) == pl.num_programs(1) - 1)
    )
    def _():
        load.wait()


def slopes(pre, sketch_t, weight, place, core):
    n, _, chunks, rows, cols = pre.shape
    rank = sketch_t.shape[0]
    groups = 2 * n
    tile = tile_of(cols, 896)
    index = jnp.stack([place, core]).astype(jnp.int32)
    weight = pltpu.with_memory_space_constraint(weight, pltpu.HBM)

    def spec_of(h, slot):
        return pl.BlockSpec(
            (1, 1, 1, rows, tile), lambda a, j, ix: (ix[0] ^ slot, ix[1] ^ h, a, 0, j)
        )

    return pl.pallas_call(
        functools.partial(slope_kernel, groups),
        grid_spec=pltpu.PrefetchScalarGridSpec(
            num_scalar_prefetch=1,
            grid=(chunks, cols // tile),
            in_specs=[spec_of(h, slot) for h in range(2) for slot in range(n)]
            + [pl.BlockSpec((rank, tile), lambda a, j, ix: (0, j))]
            + [pl.BlockSpec(memory_space=pltpu.HBM)],
            out_specs=[
                pl.BlockSpec((1, tile, groups * rows), lambda a, j, ix: (a, j, 0)),
                pl.BlockSpec((1, groups * rows, rank), lambda a, j, ix: (a, 0, 0)),
                RESIDENT,
            ],
            scratch_shapes=[pltpu.SemaphoreType.DMA],
        ),
        out_shape=[
            jax.ShapeDtypeStruct((chunks, cols, groups * rows), jnp.bfloat16),
            jax.ShapeDtypeStruct((chunks, groups * rows, rank), jnp.float32),
            jax.ShapeDtypeStruct(weight.shape, weight.dtype),
        ],
        cost_estimate=pl.CostEstimate(
            flops=2 * chunks * groups * rows * cols * rank,
            bytes_accessed=4 * chunks * groups * rows * cols,
            transcendentals=chunks * groups * rows * cols,
        ),
        compiler_params=pltpu.CompilerParams(vmem_limit_bytes=7 << 20),
        name="slopes",
    )(index, *([pre] * groups), sketch_t, weight)


def expert_kernel(
    chunk, tile_f, tile_d, rows_ref, slope_ref, down_part_ref, sketch_ref, down_ref, up_hbm, *refs
):
    keep_ref, give_ref, rows_buf, grad_buf, up_buf, up_sem = refs[-6:]
    hidden_cols, width = down_ref.shape
    steps_f, steps_d = hidden_cols // tile_f, width // tile_d
    half = keep_ref.shape[0]

    def tile(j, size):
        return pl.ds(pl.multiple_of(j * size, size), size)

    def up_copy(j):
        part = tile(j, tile_d)
        return pltpu.make_async_copy(up_hbm.at[part], up_buf.at[part], up_sem.at[j])

    for j in range(steps_d):
        if j == 0 or j > steps_f:
            up_copy(j).start()
    rows_buf[...] = rows_ref[...].T

    def first(j, carry):
        @pl.when(j + 1 < steps_d)
        def _():
            up_copy(j + 1).start()

        part = tile(j, tile_f)
        grad_hidden = jnp.dot(
            down_ref[part, :], rows_buf[...], preferred_element_type=jnp.float32
        )
        slope = slope_ref[chunk, part, :].astype(jnp.float32)
        grad_buf[part, :] = (grad_hidden * slope).astype(jnp.bfloat16)
        return carry

    lax.fori_loop(0, steps_f, first, 0)

    up_part = jnp.dot(sketch_ref[...], grad_buf[...], preferred_element_type=jnp.float32).T
    vectors = jnp.concatenate([down_part_ref[chunk], up_part], axis=1)
    keep_ref[:, width:] = vectors[:half]
    give_ref[:, width:] = vectors[half:].astype(jnp.bfloat16)

    def second(j, carry):
        up_copy(j).wait()
        part = tile(j, tile_d)
        term = jnp.dot(up_buf[part, :], grad_buf[...], preferred_element_type=jnp.float32).T
        keep_ref[:, part] = term[:half]
        give_ref[:, part] = term[half:].astype(jnp.bfloat16)
        return carry

    lax.fori_loop(0, steps_d, second, 0)


def expert(chunk, rows, slope, down_part, sketch_t, down_local, up_local, *events):
    count, width = rows.shape
    hidden_cols = down_local.shape[0]
    rank = sketch_t.shape[0]
    wide = width + 2 * rank
    tile_f, tile_d = tile_of(hidden_cols, 1792), tile_of(width, 1024)
    up_local = pltpu.with_memory_space_constraint(up_local, pltpu.HBM)
    return pl.pallas_call(
        functools.partial(expert_kernel, chunk, tile_f, tile_d),
        in_specs=[RESIDENT] * 5
        + [pl.BlockSpec(memory_space=pltpu.HBM)]
        + [ANYWHERE] * len(events),
        out_specs=[RESIDENT] * 2,
        out_shape=[
            jax.ShapeDtypeStruct((count // 2, wide), jnp.float32),
            jax.ShapeDtypeStruct((count // 2, wide), jnp.bfloat16),
        ],
        scratch_shapes=[
            pltpu.VMEM((width, count), jnp.bfloat16),
            pltpu.VMEM((hidden_cols, count), jnp.bfloat16),
            pltpu.VMEM((width, hidden_cols), jnp.bfloat16),
            pltpu.SemaphoreType.DMA((width // tile_d,)),
        ],
        compiler_params=pltpu.CompilerParams(vmem_limit_bytes=26 << 20),
        cost_estimate=pl.CostEstimate(
            flops=4 * count * hidden_cols * width,
            bytes_accessed=4 * hidden_cols * width,
            transcendentals=0,
        ),
        name="expert",
    )(rows, slope, down_part, sketch_t, down_local, up_local, *events)


def per_device(
    cotangent,
    routes,
    gate_values,
    up_weight,
    down_weight,
    pre_activation,
    input_sketch,
    model_sketch,
    hidden_sketch,
    lengths,
):
    pieces = lax.axis_size("dp")
    sections = lax.axis_size("section")
    per_expert = pieces // EXPERTS
    place = lax.axis_index("dp")
    core = lax.axis_index("tensor")
    cot = cotangent[0]
    tok_dev, width = cot.shape
    half = tok_dev // 2
    rows = half // CHUNKS
    rank = model_sketch.shape[2]
    blocks = routes.shape[1]
    block_len = tok_dev // blocks
    sketch_local = hidden_sketch[0, 0]
    pre_all = pre_activation[0, 0]
    hidden_cols = pre_all.shape[2]
    pre_all = pre_all.reshape(pieces, 2, CHUNKS, rows, hidden_cols)

    def below(block):
        return lax.ppermute(block, "section", [(s, (s - 1) % sections) for s in range(sections)])

    token_routes = jnp.broadcast_to(routes[0][:, None, :], (blocks, block_len, 2)).reshape(
        tok_dev, 2
    )
    half_routes = lax.dynamic_slice_in_dim(token_routes, core * half, half, 0)
    half_gates = lax.dynamic_slice_in_dim(gate_values[0], core * half, half, 0)
    slot_expert = (place ^ jnp.arange(pieces, dtype=jnp.int32)) // per_expert
    hits = half_routes[:, None, :] == slot_expert[None, :, None]
    weight = jnp.sum(jnp.where(hits, half_gates[:, None, :], 0.0), axis=2)

    sketch_t = sketch_local.T
    cot_mine = lax.dynamic_slice_in_dim(cot, core * half, half, 0)
    cot_theirs = lax.dynamic_slice_in_dim(cot, (1 - core) * half, half, 0)
    order = sorted(range(2, pieces), reverse=True)
    slope, down_part, down_here = slopes(pre_all, sketch_t, down_weight[0, 0], place, core)
    near_rows = xored(cot_mine, "dp", 1)
    fetched = {slot: xored(cot_mine[:rows], "dp", slot) for slot in order}
    out_vec = jnp.dot(cot, model_sketch[0], preferred_element_type=jnp.float32)
    own, sent, grad, passed, backs = (), (), (), (), ()
    below_mine, vectors = [], []
    for a in range(CHUNKS):
        part = slice(a * rows, (a + 1) * rows)
        blocks = [fetched[slot] for slot in order] + [near_rows] * (a == 0)
        blocks = jnp.concatenate(blocks, axis=0)
        if a > 0:
            blocks = held(blocks, own)
        traded = xored(blocks, "tensor", 1)
        mine = dict(fetched)
        theirs = {slot: traded[at * rows : (at + 1) * rows] for at, slot in enumerate(order)}
        if a == 0:
            near_theirs = traded[len(order) * rows :]
        mine[0], mine[1] = cot_mine[part], near_rows[part]
        theirs[0], theirs[1] = cot_theirs[part], near_theirs[part]
        rows_in = jnp.concatenate(
            [mine[k] for k in range(pieces)] + [theirs[k] for k in range(pieces)], axis=0
        )

        kept, give = expert(
            a, rows_in, slope, down_part, sketch_t, down_here, up_weight[0, 0], *sent
        )
        if a + 1 < CHUNKS:
            coming = held(cot_mine[(a + 1) * rows : (a + 2) * rows], near_rows)
            fetched = {slot: held(xored(coming, "dp", slot), kept) for slot in order}
            late = tuple(fetched.values())
        else:
            give, late = held(give, *backs), (*grad, out_vec)
        own, *sent = merged(kept, xored(give, "tensor", 1), rows, *late)
        backs = [xored(out, "dp", slot + 1) for slot, out in enumerate(sent)][::-1]
        if grad:
            passed = (below(held(*grad, backs[0])),)
            below_mine.append(*passed)
        new, vec = finished(own, cot_mine[part], weight[part], backs, *passed)
        grad = (new,)
        vectors.append(vec)
    below_mine.append(below(*grad))

    theirs = [xored(block, "tensor", 1) for block in below_mine]
    first = [jnp.where(core == 0, m, t) for m, t in zip(below_mine, theirs)]
    second = [jnp.where(core == 0, t, m) for m, t in zip(below_mine, theirs)]
    handed = jnp.concatenate(first + second, axis=0)

    vec_mine = jnp.concatenate(vectors, axis=0)
    vec_theirs = xored(vec_mine, "tensor", 1)
    sketch_sum = jnp.concatenate(
        [jnp.where(core == 0, vec_mine, vec_theirs), jnp.where(core == 0, vec_theirs, vec_mine)],
        axis=0,
    )
    counts = lengths[0, 0]
    upto = jnp.arange(counts.shape[0])
    ends = jnp.sum(jnp.where(upto[None, :] <= upto[:, None], counts[None, :], 0), axis=1)
    starts = ends - counts
    position = jnp.arange(tok_dev, dtype=jnp.int32)
    member = ((position[None, :] >= starts[:, None]) & (position[None, :] < ends[:, None])).astype(
        jnp.float32
    )
    down_feat = jnp.einsum(
        "et,ta,tb->eab", member, out_vec, sketch_sum[:, :rank], precision=lax.Precision.HIGHEST
    )
    up_feat = jnp.einsum(
        "et,ta,tb->eab",
        member,
        sketch_sum[:, rank:],
        input_sketch[0],
        precision=lax.Precision.HIGHEST,
    )
    features = jnp.concatenate([down_feat, up_feat], axis=2)
    return (handed[None], features[None])


def solution(mesh):
    in_specs = (
        P("section", ("groups", "dp"), None),
        P("section", ("groups", "dp"), None),
        P("section", ("groups", "dp"), None),
        P("section", "dp", None, "tensor"),
        P("section", "dp", "tensor", None),
        P("section", ("groups", "dp"), None, None, "tensor"),
        P("section", ("groups", "dp"), None),
        P("section", None, None),
        P("section", "dp", "tensor", None),
        P("section", ("groups", "dp"), None),
    )
    out_specs = (P("section", ("groups", "dp"), None), P("section", ("groups", "dp"), None, None))
    return jax.shard_map(
        per_device, mesh=mesh, in_specs=in_specs, out_specs=out_specs, check_vma=False
    )
```
